32 devices in a mesh: seq: 4 (over x, core), batch: 2 (over y), tensor: 4 (over z).
Axes of the slice: x: 2, y: 2, z: 4, core: 2. Of those that a mesh axis runs over, the one named last changes fastest.
Arguments:
- tokens: bfloat16 [8, 1024, 2048], P('batch', 'seq'), may hold values from -6 to 6
- cotangent: bfloat16 [8, 1024, 2048], P('batch', 'seq'), may hold values from -6 to 6
- lengths: int32 [8], P('batch'), may hold values from 512 to 1024, as said below
- block_slot: int32 [4], replicated, may hold values from 0 to 3, each once
- gain_attn: float32 [2048], replicated, may hold values from 0.5 to 1.5
- shift_attn: float32 [2048], replicated, may hold values from -1.75 to 1.75
- gain_mlp: float32 [2048], replicated, may hold values from 0.5 to 1.5
- shift_mlp: float32 [2048], replicated, may hold values from -1.75 to 1.75
- w_qkv: bfloat16 [2048, 8, 768], P(('seq', 'batch'), 'tensor'), may hold values from -0.125 to 0.125
- b_qkv: float32 [8, 768], P('tensor'), may hold values from -1.75 to 1.75
- w_out: bfloat16 [2048, 2048], P('tensor', ('seq', 'batch')), may hold values from -2 to 2
- b_out: float32 [2048], replicated, may hold values from -1.75 to 1.75
- w_up: bfloat16 [2048, 8192], P(('seq', 'batch'), 'tensor'), may hold values from -0.125 to 0.125
- b_up: float32 [8192], P('tensor'), may hold values from -1.75 to 1.75
- w_down: bfloat16 [8192, 2048], P('tensor', ('seq', 'batch')), may hold values from -0.0625 to 0.0625
- b_down: float32 [2048], replicated, may hold values from -1.75 to 1.75
Outputs:
- mixed: bfloat16 [8, 1024, 2048], P('batch', 'seq')
- tokens_grad: float32 [8, 1024, 2048], P('batch', 'seq')
- gain_attn_grad: float32 [2048], replicated
- shift_attn_grad: float32 [2048], replicated
- gain_mlp_grad: float32 [2048], replicated
- shift_mlp_grad: float32 [2048], replicated
- w_qkv_grad: float32 [2048, 8, 768], P(('seq', 'batch'), 'tensor')
- b_qkv_grad: float32 [8, 768], P('tensor')
- w_out_grad: float32 [2048, 2048], P('tensor', ('seq', 'batch'))
- b_out_grad: float32 [2048], replicated
- w_up_grad: float32 [2048, 8192], P(('seq', 'batch'), 'tensor')
- b_up_grad: float32 [8192], P('tensor')
- w_down_grad: float32 [8192, 2048], P('tensor', ('seq', 'batch'))
- b_down_grad: float32 [2048], replicated
The draws below stay inside these ranges and needn't reach their ends.
Inputs may be any that keep to these rules, and one draw needn't show every extreme that they name: `lengths`: in every aligned block of 1 sequence one has length 1024. `block_slot`: every block index appears exactly once.
All inputs are finite; a program needn't handle non-finite values.
Results may differ from the reference program's by a relative error of at most 0.019.
Values may be sent and summed in bfloat16 or wider, within the bound.
No kernel may reach another device: no remote copies, remote signals or barrier semaphores. Data moves between devices by JAX's collectives and lax.ppermute only.
A program may use at most 192 MiB of HBM per device.

```python
import jax
import jax.numpy as jnp
from jax import lax

D = 2048
HEADS = 8
HEAD_DIM = 256
ROT = 64
FF = 8192
SEQS_DEV = 1
SEQ_LEN = 1024
SEQS = 8
N_SEQ = 4


def draw_lengths(key, part):
    key = jax.random.fold_in(key, 11)
    base_key, pick_key = jax.random.split(key)
    drawn = jax.random.randint(base_key, (SEQS,), SEQ_LEN // 2, SEQ_LEN + 1)
    picked = jax.random.randint(pick_key, (SEQS // SEQS_DEV,), 0, SEQS_DEV)
    position = jnp.arange(SEQS) % SEQS_DEV
    longest = position == jnp.repeat(picked, SEQS_DEV)
    return jnp.where(longest, SEQ_LEN, drawn).astype(jnp.int32)


def levels(rng, extent, cuts, least, top_value):
    def one(dim, blocks):
        steps = jax.random.uniform(jax.random.fold_in(jax.random.fold_in(rng, 6), dim), (blocks,), jnp.float32, least / len(cuts), top_value / len(cuts))
        return jnp.repeat(jnp.exp(steps), extent[dim] // blocks).reshape((-1,) + (1,) * (len(extent) - dim - 1))

    factor_of = one(*cuts[0])
    for cut in cuts[1:]:
        factor_of = factor_of * one(*cut)
    return factor_of


def centred(key, extent, scale, bound, cuts=(), kind=jnp.bfloat16):
    entries = scale * jax.random.normal(key, extent, jnp.float32)
    if cuts:
        entries = entries * levels(key, extent, cuts, -0.22, 0.18)
    return jnp.clip(entries, -bound, bound).astype(kind)


def setup_inputs(seed: int = 0) -> dict:
    key_of = jax.random.split(jax.random.key(seed), 17)
    tokens = centred(key_of[0], (SEQS, SEQ_LEN, D), 1.0, 6.0, ((0, 2), (1, 4)))
    cotangent = centred(key_of[1], (SEQS, SEQ_LEN, D), 1.0, 6.0, ((0, 2), (1, 4)))
    lengths = draw_lengths(jax.random.fold_in(key_of[16], 71), 0)
    block_slot = jax.random.permutation(key_of[3], N_SEQ).astype(jnp.int32)
    gain_attn = jnp.clip(1.0 + 0.1 * jax.random.normal(key_of[4], (D,), jnp.float32), 0.5, 1.5)
    shift_attn = centred(key_of[5], (D,), 0.3, 1.75, (), jnp.float32)
    gain_mlp = jnp.clip(1.0 + 0.1 * jax.random.normal(key_of[6], (D,), jnp.float32), 0.5, 1.5)
    shift_mlp = centred(key_of[7], (D,), 0.3, 1.75, (), jnp.float32)
    w_qkv = centred(key_of[8], (D, HEADS, 3 * HEAD_DIM), D ** -0.5, 0.125, ((0, 8), (1, 4)))
    b_qkv = centred(key_of[9], (HEADS, 3 * HEAD_DIM), 0.3, 1.75, ((0, 4),), jnp.float32)
    w_out = centred(key_of[10], (HEADS * HEAD_DIM, D), (max(1, HEADS * HEAD_DIM // 256)) ** -0.5, 2.0, ((0, 4), (1, 8)))
    b_out = centred(key_of[11], (D,), 0.3, 1.75, (), jnp.float32)
    w_up = centred(key_of[12], (D, FF), D ** -0.5, 0.125, ((0, 8), (1, 4)))
    b_up = centred(key_of[13], (FF,), 0.3, 1.75, ((0, 4),), jnp.float32)
    w_down = centred(key_of[14], (FF, D), FF ** -0.5, 0.0625, ((0, 4), (1, 8)))
    b_down = centred(key_of[15], (D,), 0.3, 1.75, (), jnp.float32)
    return dict(tokens=tokens, cotangent=cotangent, lengths=lengths, block_slot=block_slot, gain_attn=gain_attn, shift_attn=shift_attn, gain_mlp=gain_mlp, shift_mlp=shift_mlp, w_qkv=w_qkv, b_qkv=b_qkv, w_out=w_out, b_out=b_out, w_up=w_up, b_up=b_up, w_down=w_down, b_down=b_down)


EPS = 1e-05
FLOOR = -1e+30

@jax.custom_vjp
def low(v):
    return lax.optimization_barrier(v.astype(jnp.bfloat16)).astype(jnp.float32)

@jax.custom_vjp
def low_back(v):
    return v

def low_keep(v):
    return (low(v), None)

def low_pass(kept, grad):
    return (grad,)

def back_keep(v):
    return (v, None)

def back_low(kept, grad):
    return (low(grad),)
low.defvjp(low_keep, low_pass)
low_back.defvjp(back_keep, back_low)

def normalize(token_rows, gain_attn, shift_attn, gain_mlp, shift_mlp):
    centered = token_rows - lax.optimization_barrier(jnp.mean(token_rows, -1, keepdims=True))
    scaled = centered * lax.rsqrt(lax.optimization_barrier(jnp.mean(jnp.square(centered), -1, keepdims=True)) + EPS)
    return (scaled * gain_attn + shift_attn, scaled * gain_mlp + shift_mlp)

def rotate(field_in, places):
    half_rot = ROT // 2
    frequency = 10000.0 ** (jnp.arange(half_rot, dtype=jnp.float32) * (-2.0 / ROT))
    angles = places.astype(jnp.float32)[:, None] * frequency[None, :]
    cosine = jnp.cos(angles)[:, None, :]
    sine_part = jnp.sin(angles)[:, None, :]
    front_part = field_in[..., :half_rot]
    back_part = field_in[..., half_rot:ROT]
    return jnp.concatenate([front_part * cosine - back_part * sine_part, back_part * cosine + front_part * sine_part, field_in[..., ROT:]], -1)

def forward(seq_rows, params, places, length):
    gain_attn, shift_attn, gain_mlp, shift_mlp, w_qkv, b_qkv, w_out, b_out, w_up, b_up, w_down, b_down = params
    highest = lax.Precision.HIGHEST
    normed_attn, normed_mlp = normalize(seq_rows, gain_attn, shift_attn, gain_mlp, shift_mlp)
    input_attn = low(normed_attn)
    input_mlp = low(normed_mlp)
    project = low_back(jnp.einsum('ld,dhe->lhe', input_attn, w_qkv, precision=highest)) + b_qkv
    queries = low(rotate(project[..., :HEAD_DIM], places))
    keys_rot = low(rotate(project[..., HEAD_DIM:2 * HEAD_DIM], places))
    values = low(project[..., 2 * HEAD_DIM:])
    allowed = (places[None, :] <= places[:, None]) & (places[None, :] < length)
    score_scale = HEAD_DIM ** (-0.5)

    def one_head(triple):
        query_head, key_head, value_head = triple
        scores = low_back(jnp.dot(query_head, key_head.T, precision=highest) * score_scale)
        scores = jnp.where(allowed, scores, FLOOR)
        shifted = jnp.exp(scores - lax.optimization_barrier(jnp.max(scores, -1, keepdims=True)))
        prob_low = low(shifted / lax.optimization_barrier(jnp.sum(shifted, -1, keepdims=True)))
        return low_back(low(jnp.dot(prob_low, value_head, precision=highest)))
    heads_out = lax.map(jax.checkpoint(one_head), (jnp.swapaxes(queries, 0, 1), jnp.swapaxes(keys_rot, 0, 1), jnp.swapaxes(values, 0, 1)))
    attended = jnp.swapaxes(heads_out, 0, 1).reshape(SEQ_LEN, HEADS * HEAD_DIM)
    hidden_pre = low_back(jnp.dot(input_mlp, w_up, precision=highest)) + b_up
    activated = low(jax.nn.gelu(hidden_pre, approximate=False))
    branch = jnp.dot(attended, w_out, precision=highest) + jnp.dot(activated, w_down, precision=highest)
    return seq_rows + low_back(branch) + b_out + b_down

def reference(tokens, cotangent, lengths, block_slot, gain_attn, shift_attn, gain_mlp, shift_mlp, w_qkv, b_qkv, w_out, b_out, w_up, b_up, w_down, b_down):
    block_rows = SEQ_LEN // N_SEQ
    slot_index = jnp.arange(SEQ_LEN, dtype=jnp.int32)
    places = (block_slot[slot_index // block_rows] * block_rows + slot_index % block_rows).astype(jnp.int32)
    params = tuple((member.astype(jnp.float32) for member in (gain_attn, shift_attn, gain_mlp, shift_mlp, w_qkv, b_qkv, w_out, b_out, w_up, b_up, w_down, b_down)))

    def one_sequence(totals, entry):
        seq_tokens, seq_cotangent, length = entry
        output, pullback = jax.vjp(lambda seq_rows, weights: forward(seq_rows, weights, places, length), seq_tokens.astype(jnp.float32), params)
        valid_rows = (places < length).astype(jnp.float32)[:, None]
        input_grad, param_grads = pullback(seq_cotangent.astype(jnp.float32) * valid_rows)
        totals = jax.tree.map(jnp.add, totals, param_grads)
        return (totals, (output.astype(jnp.bfloat16), input_grad))
    zero_grads = jax.tree.map(jnp.zeros_like, params)
    totals, (mixed, tokens_grad) = lax.scan(one_sequence, zero_grads, (tokens, cotangent, lengths))
    gain_attn_grad, shift_attn_grad, gain_mlp_grad, shift_mlp_grad, w_qkv_grad, b_qkv_grad, w_out_grad, b_out_grad, w_up_grad, b_up_grad, w_down_grad, b_down_grad = totals
    return (mixed, tokens_grad, gain_attn_grad, shift_attn_grad, gain_mlp_grad, shift_mlp_grad, w_qkv_grad, b_qkv_grad, w_out_grad, b_out_grad, w_up_grad, b_up_grad, w_down_grad, b_down_grad)
```

```python
import jax
import jax.numpy as jnp
from jax import lax
from jax.sharding import PartitionSpec as P

D = 2048
HEAD_DIM = 256
ROT = 64
EPS = 1e-05
FLOOR = -1e30
BF = jnp.bfloat16
F32 = jnp.float32


def dot(a, b, dims):
    return lax.dot_general(a, b, (dims, ((), ())), preferred_element_type=F32)


def rotation(places):
    half_rot = ROT // 2
    frequency = 10000.0 ** (jnp.arange(half_rot, dtype=F32) * (-2.0 / ROT))
    angles = places.astype(F32)[:, None] * frequency[None, :]
    return jnp.cos(angles)[:, None, :], jnp.sin(angles)[:, None, :]


def rotate(field, cosine, sine):
    half_rot = ROT // 2
    front = field[..., :half_rot]
    back = field[..., half_rot:ROT]
    return jnp.concatenate(
        [front * cosine - back * sine, back * cosine + front * sine, field[..., ROT:]], -1
    )


def gelu_pair(z):
    phi_cdf = 0.5 * (1.0 + lax.erf(z * 0.7071067811865476))
    density = 0.3989422804014327 * jnp.exp(-0.5 * z * z)
    return z * phi_cdf, phi_cdf + z * density


def per_device(
    tokens,
    cotangent,
    lengths,
    block_slot,
    gain_attn,
    shift_attn,
    gain_mlp,
    shift_mlp,
    w_qkv,
    b_qkv,
    w_out,
    b_out,
    w_up,
    b_up,
    w_down,
    b_down,
):
    seqs, block_rows, _ = tokens.shape
    rows = seqs * block_rows
    shard = w_qkv.shape[0]
    heads = w_qkv.shape[1]
    width_qkv = heads * 3 * HEAD_DIM
    width_att = heads * HEAD_DIM
    units = w_up.shape[1]
    fsdp = ("seq", "batch")
    scale = HEAD_DIM ** (-0.5)
    seq_count = lax.axis_size("seq")
    device_ids = jnp.arange(seq_count, dtype=jnp.int32)
    own_slot = jnp.sum(jnp.where(device_ids == lax.axis_index("seq"), block_slot, 0))
    offsets = jnp.arange(block_rows, dtype=jnp.int32)
    query_places = own_slot * block_rows + offsets
    key_places = (block_slot[:, None] * block_rows + offsets[None, :]).reshape(-1)

    attn_shard = jnp.concatenate([w_qkv.reshape(shard, width_qkv), w_out.T], 1)
    mlp_shard = jnp.concatenate([w_up, w_down.T], 1)
    attn_full = lax.all_gather(attn_shard, fsdp, axis=0, tiled=True)
    mlp_full = lax.all_gather(mlp_shard, fsdp, axis=0, tiled=True)
    full_qkv = attn_full[:, :width_qkv]
    full_out_t = attn_full[:, width_qkv:]
    full_up = mlp_full[:, :units]
    full_down_t = mlp_full[:, units:]

    token_rows = tokens.astype(F32).reshape(rows, D)
    centered = token_rows - jnp.mean(token_rows, -1, keepdims=True)
    inverse = lax.rsqrt(jnp.mean(jnp.square(centered), -1, keepdims=True) + EPS)
    xhat = centered * inverse
    input_attn = (xhat * gain_attn + shift_attn).astype(BF)
    input_mlp = (xhat * gain_mlp + shift_mlp).astype(BF)

    valid = (query_places[None, :] < lengths[:, None]).astype(F32)
    grad_rows = (cotangent.astype(F32) * valid[..., None]).reshape(rows, D)
    grad_low = grad_rows.astype(BF)

    project = dot(input_attn, full_qkv, ((1,), (0,))).reshape(
        seqs, block_rows, heads, 3 * HEAD_DIM
    ) + b_qkv
    cosine, sine = rotation(query_places)
    queries = rotate(project[..., :HEAD_DIM], cosine, sine).astype(BF)
    keys = rotate(project[..., HEAD_DIM : 2 * HEAD_DIM], cosine, sine).astype(BF)
    values = project[..., 2 * HEAD_DIM :].astype(BF)
    pair = jnp.concatenate([keys, values], -1)
    gathered = lax.all_gather(pair, "seq", axis=0, tiled=False)
    gathered = jnp.transpose(gathered, (1, 3, 0, 2, 4)).reshape(
        seqs, heads, seq_count * block_rows, 2 * HEAD_DIM
    )
    all_keys = gathered[..., :HEAD_DIM]
    all_values = gathered[..., HEAD_DIM:]

    hidden_pre = dot(input_mlp, full_up, ((1,), (0,))) + b_up
    gelu, slope = gelu_pair(hidden_pre)
    activated = gelu.astype(BF)
    grad_hidden = dot(grad_low, full_down_t, ((1,), (0,))) * slope
    hidden_low = grad_hidden.astype(BF)
    bias_up_sum = jnp.sum(grad_hidden, 0)

    grad_att = dot(grad_low, full_out_t, ((1,), (0,))).reshape(
        seqs, block_rows, heads, HEAD_DIM
    ).astype(BF)

    causal = key_places[None, None, :] <= query_places[None, :, None]
    inside = key_places[None, None, :] < lengths[:, None, None]
    mask = (causal & inside)[:, None]
    scores = jnp.einsum("schd,shtd->shct", queries, all_keys, preferred_element_type=F32) * scale
    scores = jnp.where(mask, scores, FLOOR)
    top = jnp.max(scores, -1, keepdims=True)
    weights = jnp.where(mask, jnp.exp(scores - top), 0.0)
    probs = weights / jnp.sum(weights, -1, keepdims=True)
    prob_low = probs.astype(BF)
    attended = jnp.einsum("shct,shtd->schd", prob_low, all_values, preferred_element_type=F32)
    attended = attended.astype(BF).reshape(rows, width_att)

    partial = dot(attended, full_out_t, ((1,), (1,))) + dot(activated, full_down_t, ((1,), (1,)))
    branch = lax.psum(partial.astype(BF), "tensor").astype(F32)

    grad_mlp_weights = jnp.concatenate(
        [dot(input_mlp, hidden_low, ((0,), (0,))), dot(grad_low, activated, ((0,), (0,)))], 1
    ).astype(BF)
    mlp_reduced = lax.psum_scatter(
        grad_mlp_weights, fsdp, scatter_dimension=0, tiled=True
    ).astype(F32)

    grad_probs = jnp.einsum("schd,shtd->shct", grad_att, all_values, preferred_element_type=F32)
    delta = jnp.sum(probs * grad_probs, -1, keepdims=True)
    grad_scores = (probs * (grad_probs - delta)).astype(BF)
    grad_query = jnp.einsum("shct,shtd->schd", grad_scores, all_keys, preferred_element_type=F32) * scale
    key_term = jnp.einsum("shct,schd->tshd", grad_scores, queries, preferred_element_type=F32) * scale
    value_term = jnp.einsum("shct,schd->tshd", prob_low, grad_att, preferred_element_type=F32)
    terms = jnp.concatenate([key_term, value_term], -1).astype(BF)
    own_terms = lax.psum_scatter(terms, "seq", scatter_dimension=0, tiled=True).astype(F32)
    own_terms = jnp.swapaxes(own_terms, 0, 1)
    grad_key = own_terms[..., :HEAD_DIM]
    grad_value = own_terms[..., HEAD_DIM:]
    grad_project = jnp.concatenate(
        [rotate(grad_query, cosine, -sine), rotate(grad_key, cosine, -sine), grad_value], -1
    ).reshape(rows, width_qkv)
    bias_qkv_sum = jnp.sum(grad_project, 0)
    project_low = grad_project.astype(BF)

    grad_norm_attn = dot(project_low, full_qkv, ((1,), (1,)))
    grad_norm_mlp = dot(hidden_low, full_up, ((1,), (1,)))
    norm_sums = jnp.stack(
        [
            jnp.sum(grad_norm_attn * xhat, 0),
            jnp.sum(grad_norm_attn, 0),
            jnp.sum(grad_norm_mlp * xhat, 0),
            jnp.sum(grad_norm_mlp, 0),
        ]
    )
    grad_xhat = grad_norm_attn * gain_attn + grad_norm_mlp * gain_mlp
    input_part = inverse * (
        grad_xhat
        - jnp.mean(grad_xhat, -1, keepdims=True)
        - xhat * jnp.mean(grad_xhat * xhat, -1, keepdims=True)
    )
    input_part, branch = lax.optimization_barrier((input_part.astype(BF), branch))
    input_sum = lax.psum(input_part, "tensor").astype(F32)
    mixed = (token_rows + branch + b_out + b_down).astype(BF).reshape(tokens.shape)
    tokens_grad = (grad_rows + input_sum).reshape(tokens.shape)

    grad_attn_weights = jnp.concatenate(
        [dot(input_attn, project_low, ((0,), (0,))), dot(grad_low, attended, ((0,), (0,)))], 1
    ).astype(BF)
    attn_reduced = lax.psum_scatter(
        grad_attn_weights, fsdp, scatter_dimension=0, tiled=True
    ).astype(F32)

    norm_sums = lax.psum(norm_sums, "tensor").reshape(-1)
    small = lax.psum(
        jnp.concatenate([norm_sums, bias_qkv_sum, jnp.sum(grad_rows, 0), bias_up_sum]), fsdp
    )
    norm_sums = small[: 4 * D].reshape(4, D)
    small = small[4 * D :]
    bias_qkv_sum = small[:width_qkv].reshape(b_qkv.shape)
    bias_out_sum = small[width_qkv : width_qkv + D]
    bias_up_sum = small[width_qkv + D :]
    return (
        mixed,
        tokens_grad,
        norm_sums[0],
        norm_sums[1],
        norm_sums[2],
        norm_sums[3],
        attn_reduced[:, :width_qkv].reshape(w_qkv.shape),
        bias_qkv_sum,
        attn_reduced[:, width_qkv:].T,
        bias_out_sum,
        mlp_reduced[:, :units],
        bias_up_sum,
        mlp_reduced[:, units:].T,
        bias_out_sum,
    )


def solution(mesh):
    in_specs = (
        P("batch", "seq", None),
        P("batch", "seq", None),
        P("batch"),
        P(),
        P(),
        P(),
        P(),
        P(),
        P(("seq", "batch"), "tensor", None),
        P("tensor", None),
        P("tensor", ("seq", "batch")),
        P(),
        P(("seq", "batch"), "tensor"),
        P("tensor"),
        P("tensor", ("seq", "batch")),
        P(),
    )
    out_specs = (
        P("batch", "seq", None),
        P("batch", "seq", None),
        P(),
        P(),
        P(),
        P(),
        P(("seq", "batch"), "tensor", None),
        P("tensor", None),
        P("tensor", ("seq", "batch")),
        P(),
        P(("seq", "batch"), "tensor"),
        P("tensor"),
        P("tensor", ("seq", "batch")),
        P(),
    )
    return jax.shard_map(
        per_device, mesh=mesh, in_specs=in_specs, out_specs=out_specs, check_vma=False
    )
```

```python
import jax
import jax.numpy as jnp
from jax import lax
from jax.experimental import pallas as pl
from jax.experimental.pallas import tpu as pltpu
from jax.sharding import PartitionSpec as P

D = 2048
HEAD_DIM = 256
ROT = 64
EPS = 1e-05
FLOOR = -1e30
BF = jnp.bfloat16
F32 = jnp.float32


def dot(a, b, dims):
    return lax.dot_general(a, b, (dims, ((), ())), preferred_element_type=F32)


def rotation(places):
    half_rot = ROT // 2
    frequency = 10000.0 ** (jnp.arange(half_rot, dtype=F32) * (-2.0 / ROT))
    angles = places.astype(F32)[:, None] * frequency[None, :]
    return jnp.cos(angles)[:, None, :], jnp.sin(angles)[:, None, :]


def rotate(field, cosine, sine):
    half_rot = ROT // 2
    front = field[..., :half_rot]
    back = field[..., half_rot:ROT]
    return jnp.concatenate(
        [front * cosine - back * sine, back * cosine + front * sine, field[..., ROT:]], -1
    )


def gelu_pair(z):
    phi_cdf = 0.5 * (1.0 + lax.erf(z * 0.7071067811865476))
    density = 0.3989422804014327 * jnp.exp(-0.5 * z * z)
    return z * phi_cdf, phi_cdf + z * density


def per_device_any(
    tokens,
    cotangent,
    lengths,
    block_slot,
    gain_attn,
    shift_attn,
    gain_mlp,
    shift_mlp,
    w_qkv,
    b_qkv,
    w_out,
    b_out,
    w_up,
    b_up,
    w_down,
    b_down,
):
    seqs, block_rows, _ = tokens.shape
    rows = seqs * block_rows
    shard = w_qkv.shape[0]
    heads = w_qkv.shape[1]
    width_qkv = heads * 3 * HEAD_DIM
    width_att = heads * HEAD_DIM
    units = w_up.shape[1]
    fsdp = ("seq", "batch")
    scale = HEAD_DIM ** (-0.5)
    seq_count = lax.axis_size("seq")
    device_ids = jnp.arange(seq_count, dtype=jnp.int32)
    own_slot = jnp.sum(jnp.where(device_ids == lax.axis_index("seq"), block_slot, 0))
    offsets = jnp.arange(block_rows, dtype=jnp.int32)
    query_places = own_slot * block_rows + offsets
    key_places = (block_slot[:, None] * block_rows + offsets[None, :]).reshape(-1)

    attn_shard = jnp.concatenate([w_qkv.reshape(shard, width_qkv), w_out.T], 1)
    mlp_shard = jnp.concatenate([w_up, w_down.T], 1)
    attn_full = lax.all_gather(attn_shard, fsdp, axis=0, tiled=True)
    mlp_full = lax.all_gather(mlp_shard, fsdp, axis=0, tiled=True)
    full_qkv = attn_full[:, :width_qkv]
    full_out_t = attn_full[:, width_qkv:]
    full_up = mlp_full[:, :units]
    full_down_t = mlp_full[:, units:]

    token_rows = tokens.astype(F32).reshape(rows, D)
    centered = token_rows - jnp.mean(token_rows, -1, keepdims=True)
    inverse = lax.rsqrt(jnp.mean(jnp.square(centered), -1, keepdims=True) + EPS)
    xhat = centered * inverse
    input_attn = (xhat * gain_attn + shift_attn).astype(BF)
    input_mlp = (xhat * gain_mlp + shift_mlp).astype(BF)

    valid = (query_places[None, :] < lengths[:, None]).astype(F32)
    grad_rows = (cotangent.astype(F32) * valid[..., None]).reshape(rows, D)
    grad_low = grad_rows.astype(BF)

    project = dot(input_attn, full_qkv, ((1,), (0,))).reshape(
        seqs, block_rows, heads, 3 * HEAD_DIM
    ) + b_qkv
    cosine, sine = rotation(query_places)
    queries = rotate(project[..., :HEAD_DIM], cosine, sine).astype(BF)
    keys = rotate(project[..., HEAD_DIM : 2 * HEAD_DIM], cosine, sine).astype(BF)
    values = project[..., 2 * HEAD_DIM :].astype(BF)
    pair = jnp.concatenate([keys, values], -1)
    gathered = lax.all_gather(pair, "seq", axis=0, tiled=False)
    gathered = jnp.transpose(gathered, (1, 3, 0, 2, 4)).reshape(
        seqs, heads, seq_count * block_rows, 2 * HEAD_DIM
    )
    all_keys = gathered[..., :HEAD_DIM]
    all_values = gathered[..., HEAD_DIM:]

    hidden_pre = dot(input_mlp, full_up, ((1,), (0,))) + b_up
    gelu, slope = gelu_pair(hidden_pre)
    activated = gelu.astype(BF)
    grad_hidden = dot(grad_low, full_down_t, ((1,), (0,))) * slope
    hidden_low = grad_hidden.astype(BF)
    bias_up_sum = jnp.sum(grad_hidden, 0)

    grad_att = dot(grad_low, full_out_t, ((1,), (0,))).reshape(
        seqs, block_rows, heads, HEAD_DIM
    ).astype(BF)

    causal = key_places[None, None, :] <= query_places[None, :, None]
    inside = key_places[None, None, :] < lengths[:, None, None]
    mask = (causal & inside)[:, None]
    scores = jnp.einsum("schd,shtd->shct", queries, all_keys, preferred_element_type=F32) * scale
    scores = jnp.where(mask, scores, FLOOR)
    top = jnp.max(scores, -1, keepdims=True)
    weights = jnp.where(mask, jnp.exp(scores - top), 0.0)
    probs = weights / jnp.sum(weights, -1, keepdims=True)
    prob_low = probs.astype(BF)
    attended = jnp.einsum("shct,shtd->schd", prob_low, all_values, preferred_element_type=F32)
    attended = attended.astype(BF).reshape(rows, width_att)

    partial = dot(attended, full_out_t, ((1,), (1,))) + dot(activated, full_down_t, ((1,), (1,)))
    branch = lax.psum(partial.astype(BF), "tensor").astype(F32)

    grad_mlp_weights = jnp.concatenate(
        [dot(input_mlp, hidden_low, ((0,), (0,))), dot(grad_low, activated, ((0,), (0,)))], 1
    ).astype(BF)
    mlp_reduced = lax.psum_scatter(
        grad_mlp_weights, fsdp, scatter_dimension=0, tiled=True
    ).astype(F32)

    grad_probs = jnp.einsum("schd,shtd->shct", grad_att, all_values, preferred_element_type=F32)
    delta = jnp.sum(probs * grad_probs, -1, keepdims=True)
    grad_scores = (probs * (grad_probs - delta)).astype(BF)
    grad_query = jnp.einsum("shct,shtd->schd", grad_scores, all_keys, preferred_element_type=F32) * scale
    key_term = jnp.einsum("shct,schd->tshd", grad_scores, queries, preferred_element_type=F32) * scale
    value_term = jnp.einsum("shct,schd->tshd", prob_low, grad_att, preferred_element_type=F32)
    terms = jnp.concatenate([key_term, value_term], -1).astype(BF)
    own_terms = lax.psum_scatter(terms, "seq", scatter_dimension=0, tiled=True).astype(F32)
    own_terms = jnp.swapaxes(own_terms, 0, 1)
    grad_key = own_terms[..., :HEAD_DIM]
    grad_value = own_terms[..., HEAD_DIM:]
    grad_project = jnp.concatenate(
        [rotate(grad_query, cosine, -sine), rotate(grad_key, cosine, -sine), grad_value], -1
    ).reshape(rows, width_qkv)
    bias_qkv_sum = jnp.sum(grad_project, 0)
    project_low = grad_project.astype(BF)

    grad_norm_attn = dot(project_low, full_qkv, ((1,), (1,)))
    grad_norm_mlp = dot(hidden_low, full_up, ((1,), (1,)))
    norm_sums = jnp.stack(
        [
            jnp.sum(grad_norm_attn * xhat, 0),
            jnp.sum(grad_norm_attn, 0),
            jnp.sum(grad_norm_mlp * xhat, 0),
            jnp.sum(grad_norm_mlp, 0),
        ]
    )
    grad_xhat = grad_norm_attn * gain_attn + grad_norm_mlp * gain_mlp
    input_part = inverse * (
        grad_xhat
        - jnp.mean(grad_xhat, -1, keepdims=True)
        - xhat * jnp.mean(grad_xhat * xhat, -1, keepdims=True)
    )
    input_part, branch = lax.optimization_barrier((input_part.astype(BF), branch))
    input_sum = lax.psum(input_part, "tensor").astype(F32)
    mixed = (token_rows + branch + b_out + b_down).astype(BF).reshape(tokens.shape)
    tokens_grad = (grad_rows + input_sum).reshape(tokens.shape)

    grad_attn_weights = jnp.concatenate(
        [dot(input_attn, project_low, ((0,), (0,))), dot(grad_low, attended, ((0,), (0,)))], 1
    ).astype(BF)
    attn_reduced = lax.psum_scatter(
        grad_attn_weights, fsdp, scatter_dimension=0, tiled=True
    ).astype(F32)

    norm_sums = lax.psum(norm_sums, "tensor").reshape(-1)
    small = lax.psum(
        jnp.concatenate([norm_sums, bias_qkv_sum, jnp.sum(grad_rows, 0), bias_up_sum]), fsdp
    )
    norm_sums = small[: 4 * D].reshape(4, D)
    small = small[4 * D :]
    bias_qkv_sum = small[:width_qkv].reshape(b_qkv.shape)
    bias_out_sum = small[width_qkv : width_qkv + D]
    bias_up_sum = small[width_qkv + D :]
    return (
        mixed,
        tokens_grad,
        norm_sums[0],
        norm_sums[1],
        norm_sums[2],
        norm_sums[3],
        attn_reduced[:, :width_qkv].reshape(w_qkv.shape),
        bias_qkv_sum,
        attn_reduced[:, width_qkv:].T,
        bias_out_sum,
        mlp_reduced[:, :units],
        bias_up_sum,
        mlp_reduced[:, units:].T,
        bias_out_sum,
    )


def exchange(array, axis, flip):
    size = lax.axis_size(axis)
    return lax.ppermute(array, axis, [(i, i ^ flip) for i in range(size)])


def after(array, *others):
    return lax.optimization_barrier((array, *others))[0]


def gather_blocks(shard):
    by_x = exchange(shard, "seq", 2)
    by_y = exchange(shard, "batch", 1)
    half = shard.shape[0] // 2
    far = jnp.concatenate(
        [exchange(by_x[:half], "batch", 1), exchange(by_y[half:], "seq", 2)], 0
    )
    mine = [shard, by_y, by_x, far]
    other = [exchange(block, "seq", 1) for block in mine]
    return [mine[0], mine[1], other[0], other[1], mine[2], mine[3], other[2], other[3]], far


def call(body, grid, ins, outs, scratch=(), flops=0, moved=0):
    return pl.pallas_call(
        body,
        grid=grid,
        in_specs=[spec for spec, _ in ins],
        out_specs=[spec for spec, _ in outs],
        out_shape=[shape for _, shape in outs],
        scratch_shapes=list(scratch),
        compiler_params=pltpu.CompilerParams(vmem_limit_bytes=60 * 1024 * 1024),
        cost_estimate=pl.CostEstimate(flops=flops, bytes_accessed=moved, transcendentals=0),
    )(*[array for _, array in ins])


def smem():
    return pl.BlockSpec(memory_space=pltpu.SMEM)


def whole(array):
    dims = len(array.shape)
    return pl.BlockSpec(array.shape, lambda *_: (0,) * dims)


def block(shape, index):
    return pl.BlockSpec(shape, index)


def struct(shape, dtype):
    return jax.ShapeDtypeStruct(shape, dtype)


def columns(ref, info, place):
    start = pl.multiple_of((info[0] ^ place) * 256, 256)
    return ref[:, pl.ds(start, 256)]


def norm_body(info, tok, cot, gain_a, shift_a, gain_m, shift_m, in_a, in_m, grad, grad_sum):
    step = pl.program_id(0)
    t = tok[...].astype(F32)
    centered = t - jnp.mean(t, -1, keepdims=True)
    xhat = centered * lax.rsqrt(jnp.mean(centered * centered, -1, keepdims=True) + EPS)
    in_a[...] = (xhat * gain_a[...] + shift_a[...]).astype(BF)
    in_m[...] = (xhat * gain_m[...] + shift_m[...]).astype(BF)
    place = info[1] * 256 + lax.broadcasted_iota(jnp.int32, t.shape, 0)
    g = jnp.where(place < info[5 + step], cot[...].astype(F32), 0.0)
    grad[...] = g.astype(BF)

    @pl.when(step == 0)
    def _():
        grad_sum[...] = jnp.zeros_like(grad_sum)

    grad_sum[...] += jnp.sum(g, 0, keepdims=True)


def matched(x, blocks, info):
    left = jnp.concatenate([columns(x, info, r) for r in range(8)], 1)
    right = jnp.concatenate([b[...] for b in blocks], 0)
    return jnp.dot(left, right, preferred_element_type=F32)


def turn(z, cos, front, back):
    first = z[:, :128]
    first = (
        first * cos
        + pltpu.roll(first, 96, 1) * front
        + pltpu.roll(first, 32, 1) * back
    )
    return jnp.concatenate([first, z[:, 128:]], 1)


def qkv_body(info, x, bias, cos, front, back, *refs):
    blocks, (q, kv_a, kv_b) = refs[:8], refs[8:]
    step = pl.program_id(0)
    z = matched(x, blocks, info) + bias[...]

    def turned():
        c, f, b = (jnp.concatenate([t[...]] * 4, 0) for t in (cos, front, back))
        return turn(z, c, f, b).astype(BF)

    @pl.when(step < 2)
    def _():
        q[...] = turned()

    @pl.when((step >= 2) & (step < 4))
    def _():
        k = turned()
        kv_a[...] = k[:512]
        kv_b[...] = k[512:]

    @pl.when(step >= 4)
    def _():
        v = z.astype(BF)
        kv_a[...] = v[:512]
        kv_b[...] = v[512:]


def grad_att_body(info, g, *refs):
    refs[8][...] = matched(g, refs[:8], info).astype(BF)


ERFC = (
    0.17087277,
    -0.82215223,
    1.48851587,
    -1.13520398,
    0.27886807,
    -0.18628806,
    0.09678418,
    0.37409196,
    1.00002368,
    -1.26551223,
)


def gelu_terms(z):
    size = jnp.abs(z)
    t = 1.0 / (1.0 + size * 0.35355339059327373)
    p = jnp.full_like(t, ERFC[0])
    for c in ERFC[1:]:
        p = p * t + c
    square = -0.5 * z * z
    tail = 0.5 * t * jnp.exp(square + p)
    return jnp.where(z < 0, tail, 1.0 - tail), 0.3989422804014327 * jnp.exp(square)


def up_body(info, x, bias, *refs):
    blocks, (act, slope) = refs[:8], refs[8:]
    z = matched(x, blocks, info) + bias[...]
    phi, density = gelu_terms(z)
    act[...] = (z * phi).astype(BF)
    slope[...] = (phi + z * density).astype(BF)


def hidden_body(info, g, slope, *refs):
    blocks, (low, total) = refs[:8], refs[8:]
    grad = matched(g, blocks, info) * slope[...].astype(F32)
    low[...] = grad.astype(BF)
    total[...] = jnp.sum(grad, 0, keepdims=True)


def nt(a, b):
    return lax.dot_general(a, b, (((1,), (1,)), ((), ())), preferred_element_type=F32)


def tn(a, b):
    return lax.dot_general(a, b, (((0,), (0,)), ((), ())), preferred_element_type=F32)


def attention_body(first_seq, info, q_ref, ga_ref, cos, front, back, *refs):
    keys, values = refs[:4], refs[4:8]
    att, dq, dq_sum, terms = refs[8], refs[9], refs[10], refs[11:]
    seq = pl.program_id(0)
    head = pl.program_id(1)
    scale = HEAD_DIM ** (-0.5)
    length = info[5 + first_seq + seq]
    q = q_ref[...]
    ga = ga_ref[...]
    row_place = info[1] * 256 + lax.broadcasted_iota(jnp.int32, (256, 256), 0)
    column = lax.broadcasted_iota(jnp.int32, (256, 256), 1)
    scores = []
    masks = []
    for r in range(4):
        key_place = info[1 + r] * 256 + column
        allowed = (key_place <= row_place) & (key_place < length)
        masks.append(allowed)
        scores.append(jnp.where(allowed, nt(q, keys[r][...]) * scale, FLOOR))
    top = jnp.max(jnp.maximum(jnp.maximum(scores[0], scores[1]), jnp.maximum(scores[2], scores[3])), -1, keepdims=True)
    weights = [jnp.where(m, jnp.exp(s - top), 0.0) for s, m in zip(scores, masks)]
    total = jnp.sum(weights[0] + weights[1] + weights[2] + weights[3], -1, keepdims=True)
    inverse = 1.0 / total
    probs = [w * inverse for w in weights]
    low = [p.astype(BF) for p in probs]
    out = jnp.zeros((256, 256), F32)
    for r in range(4):
        out += jnp.dot(low[r], values[r][...], preferred_element_type=F32)
    att[...] = out.astype(BF)
    grad_probs = [nt(ga, values[r][...]) for r in range(4)]
    products = [p * g for p, g in zip(probs, grad_probs)]
    delta = jnp.sum(products[0] + products[1] + products[2] + products[3], -1, keepdims=True)
    grad_q = jnp.zeros((256, 256), F32)
    key_columns = pl.ds(pl.multiple_of(head * 256, 256), 256)
    value_columns = pl.ds(pl.multiple_of(head * 256 + 512, 256), 256)
    for r in range(4):
        grad_scores = (probs[r] * (grad_probs[r] - delta)).astype(BF)
        grad_q += jnp.dot(grad_scores, keys[r][...], preferred_element_type=F32)
        terms[r][:, key_columns] = (tn(grad_scores, q) * scale).astype(BF)
        terms[r][:, value_columns] = tn(low[r], ga).astype(BF)
    grad_q = turn(grad_q * scale, cos[...], -front[...], -back[...])
    dq[...] = grad_q.astype(BF)
    dq_sum[...] = jnp.sum(grad_q, 0, keepdims=True)[None, None]


def branch_body(info, att, act, *refs):
    w_att, w_act, out = refs[:8], refs[8:16], refs[16]
    for r in range(8):
        start = pl.multiple_of((info[0] ^ r) * 256, 256)
        part = nt(att[...], w_att[r][...]) + nt(act[...], w_act[r][...])
        out[:, pl.ds(start, 256)] = part.astype(BF)


def weight_send_body(places, info, x, h, out):
    for i, r in enumerate(places):
        out[i * 256 : (i + 1) * 256, :] = tn(columns(x, info, r), h[...]).astype(BF)


def weight_add_body(places, info, x, h, received, send, keep):
    for i, r in enumerate(places):
        part = tn(columns(x, info, r), h[...]) + received[i * 256 : (i + 1) * 256, :].astype(F32)
        if i < 2:
            keep[i * 256 : (i + 1) * 256, :] = part.astype(BF)
        else:
            send[(i - 2) * 256 : (i - 1) * 256, :] = part.astype(BF)


def weight_gradient(info, x, h, start, width, x_first):
    rows = x.shape[0]
    order = (0, 1, 4, 5) if x_first else (0, 4, 1, 5)
    tile = 512
    steps = width // tile
    base = start // tile
    cost = dict(flops=2 * rows * 1024 * width, moved=2 * (rows * (2048 + width) + 1024 * width))
    ins = [
        (smem(), info),
        (whole(x), x),
        (block((rows, tile), lambda j: (0, base + j)), h),
    ]
    column = lambda j: (0, j)
    sent = call(
        lambda *refs: weight_send_body([r ^ 2 for r in order], *refs),
        (steps,),
        ins,
        [(block((1024, tile), column), struct((1024, width), BF))],
        **cost,
    )[0]
    received = exchange(sent, "seq", 1)
    send, keep = call(
        lambda *refs: weight_add_body(order, *refs),
        (steps,),
        ins + [(block((1024, tile), column), received)],
        [(block((512, tile), column), struct((512, width), BF))] * 2,
        **cost,
    )
    first, second = (("seq", 2), ("batch", 1)) if x_first else (("batch", 1), ("seq", 2))
    got = exchange(send, *first)
    summed = keep.astype(F32) + got.astype(F32)
    last = exchange(summed[256:].astype(BF), *second)
    return summed[:256] + last.astype(F32)


def input_body(seqs, info, q_low, own, core, far, hid, tok, cos, front, back, gain_a, gain_m, *refs):
    w_qkv, w_up = refs[:8], refs[8:16]
    part, low, kv_sum, sums, gx, xh = refs[16:]
    step = pl.program_id(0)
    t = tok[...].astype(F32)
    centered = t - jnp.mean(t, -1, keepdims=True)
    inverse = lax.rsqrt(jnp.mean(centered * centered, -1, keepdims=True) + EPS)
    xh[...] = centered * inverse
    terms = own[...].astype(F32) + core[...].astype(F32) + far[...].astype(F32)
    pieces = []
    kv_sums = []
    for head in range(2):
        grad_k = turn(terms[:, head * 256 : head * 256 + 256], cos[...], -front[...], -back[...])
        grad_v = terms[:, 512 + head * 256 : 768 + head * 256]
        kv_sums += [jnp.sum(grad_k, 0, keepdims=True), jnp.sum(grad_v, 0, keepdims=True)]
        pieces += [q_low[:, head * 256 : head * 256 + 256], grad_k.astype(BF), grad_v.astype(BF)]
    low[...] = jnp.concatenate(pieces, 1)
    kv_sum[...] = jnp.concatenate(kv_sums, 1)[None]

    @pl.when(step == 0)
    def _():
        sums[...] = jnp.zeros_like(sums)

    for r in range(8):
        there = pl.ds(pl.multiple_of((info[0] ^ r) * 256, 256), 256)
        from_attn = nt(low[...], w_qkv[r][:, :1536])
        from_mlp = nt(hid[...], w_up[r][...])
        xhat = xh[:, there]
        sums[0:1, there] += jnp.sum(from_attn * xhat, 0, keepdims=True)
        sums[1:2, there] += jnp.sum(from_attn, 0, keepdims=True)
        sums[2:3, there] += jnp.sum(from_mlp * xhat, 0, keepdims=True)
        sums[3:4, there] += jnp.sum(from_mlp, 0, keepdims=True)
        gx[:, there] = from_attn * gain_a[:, there] + from_mlp * gain_m[:, there]
    grad = gx[...]
    xhat = xh[...]
    mean = jnp.mean(grad, -1, keepdims=True)
    along = jnp.mean(grad * xhat, -1, keepdims=True)
    part[...] = (inverse * (grad - mean - xhat * along)).astype(BF)


def per_device_links(
    tokens,
    cotangent,
    lengths,
    block_slot,
    gain_attn,
    shift_attn,
    gain_mlp,
    shift_mlp,
    w_qkv,
    b_qkv,
    w_out,
    b_out,
    w_up,
    b_up,
    w_down,
    b_down,
):
    rows = 1024
    seq_id = lax.axis_index("seq")
    slots = [jnp.sum(jnp.where(jnp.arange(4) == (seq_id ^ r), block_slot, 0)) for r in range(4)]
    info = jnp.concatenate(
        [jnp.stack([seq_id * 2 + lax.axis_index("batch"), *slots]), lengths]
    ).astype(jnp.int32)
    tok = tokens.reshape(rows, D)
    cot = cotangent.reshape(rows, D)
    cosine, sine = rotation(slots[0] * 256 + jnp.arange(256, dtype=jnp.int32))
    cosine, sine = cosine[:, 0], sine[:, 0]
    zero = jnp.zeros_like(sine)
    cos_t = jnp.concatenate([cosine, cosine, zero + 1.0, zero + 1.0], 1)
    front_t = jnp.concatenate([-sine, zero, zero, zero], 1)
    back_t = jnp.concatenate([zero, sine, zero, zero], 1)
    tables = [(whole(t), t) for t in (cos_t, front_t, back_t)]
    info_in = (smem(), info)
    gains = [v.reshape(1, D) for v in (gain_attn, shift_attn, gain_mlp, shift_mlp)]

    attn_shard = jnp.concatenate([w_qkv.reshape(256, 1536), w_out.T], 1)
    attn_blocks, mark = gather_blocks(attn_shard)
    up_blocks, mark = gather_blocks(after(w_up, mark))
    down_blocks, mark = gather_blocks(after(w_down.T, mark))

    row_block = lambda n: block((256, n), lambda i: (i, 0))
    row_struct = lambda n, kind=BF: struct((rows, n), kind)
    in_a, in_m, grad_low, grad_sum = call(
        norm_body,
        (4,),
        [info_in, (row_block(D), tok), (row_block(D), cot)] + [(whole(v), v) for v in gains],
        [(row_block(D), row_struct(D))] * 3 + [(block((1, D), lambda i: (0, 0)), struct((1, D), F32))],
        moved=5 * rows * D * 2,
    )

    bias = b_qkv.reshape(1, 1536)
    place = lambda j: (j % 2) * 3 + j // 2
    tall = lambda index: block((256, 256), index)
    q, kv_a, kv_b = call(
        qkv_body,
        (6,),
        [info_in, (whole(in_a), in_a), (block((1, 256), lambda j: (0, place(j))), bias)]
        + tables
        + [(tall(lambda j: (0, place(j))), b) for b in attn_blocks],
        [
            (block((rows, 256), lambda j: (0, jnp.minimum(j, 1))), row_struct(512)),
            (block((512, 256), lambda j: (0, jnp.maximum(j - 2, 0))), struct((512, 1024), BF)),
            (block((512, 256), lambda j: (0, jnp.maximum(j - 2, 0))), struct((512, 1024), BF)),
        ],
        flops=2 * rows * D * 1536,
        moved=2 * (rows * D + D * 1536 + rows * 1536),
    )
    grad_att = call(
        grad_att_body,
        (2,),
        [info_in, (whole(grad_low), grad_low)] + [(tall(lambda j: (0, 6 + j)), b) for b in attn_blocks],
        [(block((rows, 256), lambda j: (0, j)), row_struct(512))],
        flops=2 * rows * D * 512,
        moved=2 * (rows * D + D * 512 + rows * 512),
    )[0]

    def spread(own):
        far = exchange(own, "seq", 2)
        return [own, exchange(own, "seq", 1), far, exchange(far, "seq", 1)]

    kv = [spread(kv_a), spread(kv_b)]

    act, slope = call(
        up_body,
        (8,),
        [info_in, (whole(in_m), in_m), (block((1, 256), lambda j: (0, j)), b_up.reshape(1, -1))]
        + [(tall(lambda j: (0, j)), b) for b in up_blocks],
        [(block((rows, 256), lambda j: (0, j)), row_struct(2048))] * 2,
        flops=2 * rows * D * 2048,
        moved=2 * (rows * D + D * 2048 + 2 * rows * 2048),
    )

    def attention(part):
        base = part * 2
        spot = lambda offset: block((256, 256), lambda s, h: (s + base, h + offset))
        local = lambda offset: block((256, 256), lambda s, h: (s, h + offset))
        return call(
            lambda *refs: attention_body(base, *refs),
            (2, 2),
            [info_in, (spot(0), q), (spot(0), grad_att)]
            + tables
            + [(local(0), b) for b in kv[part]]
            + [(local(2), b) for b in kv[part]],
            [
                (local(0), struct((512, 512), BF)),
                (local(0), struct((512, 512), BF)),
                (block((1, 1, 1, 256), lambda s, h: (s, h, 0, 0)), struct((2, 2, 1, 256), F32)),
            ]
            + [(block((256, 1024), lambda s, h: (s, 0)), struct((512, 1024), BF))] * 4,
            flops=4 * 6 * 2 * 256 * 1024 * 256,
            moved=4 * 2 * 256 * 256 * 24,
        )

    att = []
    dq = []
    dq_sums = []
    branch = []
    kv_terms = []
    for part in range(2):
        att_p, dq_p, dq_sum, *terms = attention(part)
        att.append(att_p)
        dq.append(dq_p)
        dq_sums.append(dq_sum)
        branch.append(
            call(
                branch_body,
                (2,),
                [info_in, (row_block(512), att_p), (block((256, 2048), lambda i, part=part: (i + 2 * part, 0)), act)]
                + [(block((256, 512), lambda i: (0, 3)), b) for b in attn_blocks]
                + [(whole(b), b) for b in down_blocks],
                [(row_block(D), struct((512, D), BF))],
                flops=2 * 512 * D * 2560,
                moved=2 * (512 * 2560 + D * 2560 + 512 * D),
            )[0]
        )
        from_core = exchange(terms[1], "seq", 1)
        far_core = exchange(terms[3], "seq", 1)
        far = exchange((terms[2].astype(F32) + far_core.astype(F32)).astype(BF), "seq", 2)
        kv_terms.append((terms[0], from_core, far))

    hidden_low, b_up_sum = call(
        hidden_body,
        (8,),
        [info_in, (whole(grad_low), grad_low), (block((rows, 256), lambda j: (0, j)), slope)]
        + [(tall(lambda j: (0, j)), b) for b in down_blocks],
        [
            (block((rows, 256), lambda j: (0, j)), row_struct(2048)),
            (block((1, 256), lambda j: (0, j)), struct((1, 2048), F32)),
        ],
        flops=2 * rows * D * 2048,
        moved=2 * (rows * D + D * 2048 + 2 * rows * 2048),
    )

    branch_sum = lax.psum(jnp.concatenate(branch, 0), "tensor")

    parts = []
    lows = []
    kv_sums = []
    norm_sums = []
    for part in range(2):
        shifted = lambda n, part=part: block((256, n), lambda i: (i + 2 * part, 0))
        own, core, far = kv_terms[part]
        part_p, low_p, kv_sum, sums = call(
            lambda *refs: input_body(2, *refs),
            (2,),
            [
                info_in,
                (row_block(512), dq[part]),
                (row_block(1024), own),
                (row_block(1024), core),
                (row_block(1024), far),
                (shifted(2048), hidden_low),
                (shifted(D), tok),
            ]
            + tables
            + [(whole(v), v) for v in (gains[0], gains[2])]
            + [(whole(b), b) for b in attn_blocks]
            + [(whole(b), b) for b in up_blocks],
            [
                (row_block(D), struct((512, D), BF)),
                (row_block(1536), struct((512, 1536), BF)),
                (block((1, 1, 1024), lambda i: (i, 0, 0)), struct((2, 1, 1024), F32)),
                (block((8, D), lambda i: (0, 0)), struct((8, D), F32)),
            ],
            scratch=[pltpu.VMEM((256, D), F32), pltpu.VMEM((256, D), F32)],
            flops=2 * 512 * D * 3584,
            moved=2 * (512 * 8192 + D * 3584),
        )
        parts.append(part_p)
        lows.append(low_p)
        kv_sums.append(kv_sum)
        norm_sums.append(sums)

    project_low = jnp.concatenate(lows, 0)
    attended = jnp.concatenate(att, 0)
    down_grad = weight_gradient(info, grad_low, act, 0, 2048, False)
    up_grad = weight_gradient(info, in_m, hidden_low, 0, 2048, True)
    qkv_grad_a = weight_gradient(info, in_a, project_low, 0, 1024, True)
    qkv_grad_b = weight_gradient(info, in_a, project_low, 1024, 512, False)
    out_grad = weight_gradient(info, grad_low, attended, 0, 512, False)

    input_part = after(jnp.concatenate(parts, 0), branch_sum)
    input_sum = lax.psum(input_part, "tensor")

    q_sums = (dq_sums[0] + dq_sums[1]).sum(0).reshape(2, 1, 256)
    kv_total = (kv_sums[0] + kv_sums[1]).sum(0).reshape(2, 2, 256)
    bias_qkv = jnp.concatenate([q_sums, kv_total], 1).reshape(-1)
    norm_total = (norm_sums[0] + norm_sums[1])[:4].reshape(-1)
    small = jnp.concatenate([norm_total, bias_qkv, grad_sum[0], b_up_sum[0]]).reshape(-1, 128)
    for axis, flip in (("seq", 1), ("seq", 2), ("batch", 1)):
        small = small + exchange(small, axis, flip)
    norms = small[:64]
    for flip in (1, 2):
        norms = norms + exchange(norms, "tensor", flip)
    norms = norms.reshape(4, D)
    small = small[64:].reshape(-1)

    mixed = (tok.astype(F32) + branch_sum.astype(F32) + b_out + b_down).astype(BF)
    tokens_grad = grad_low.astype(F32) + input_sum.astype(F32)
    bias_out = small[1536 : 1536 + D]
    return (
        mixed.reshape(tokens.shape),
        tokens_grad.reshape(tokens.shape),
        norms[0],
        norms[1],
        norms[2],
        norms[3],
        jnp.concatenate([qkv_grad_a, qkv_grad_b], 1).reshape(w_qkv.shape),
        small[:1536].reshape(b_qkv.shape),
        out_grad.T,
        bias_out,
        up_grad,
        small[1536 + D :],
        down_grad.T,
        bias_out,
    )


def solution(mesh):
    in_specs = (
        P("batch", "seq", None),
        P("batch", "seq", None),
        P("batch"),
        P(),
        P(),
        P(),
        P(),
        P(),
        P(("seq", "batch"), "tensor", None),
        P("tensor", None),
        P("tensor", ("seq", "batch")),
        P(),
        P(("seq", "batch"), "tensor"),
        P("tensor"),
        P("tensor", ("seq", "batch")),
        P(),
    )
    out_specs = (
        P("batch", "seq", None),
        P("batch", "seq", None),
        P(),
        P(),
        P(),
        P(),
        P(("seq", "batch"), "tensor", None),
        P("tensor", None),
        P("tensor", ("seq", "batch")),
        P(),
        P(("seq", "batch"), "tensor"),
        P("tensor"),
        P("tensor", ("seq", "batch")),
        P(),
    )
    links = tuple(mesh.shape[axis] for axis in ("seq", "batch", "tensor"))
    per_device = per_device_links if links == (4, 2, 4) else per_device_any
    return jax.shard_map(
        per_device, mesh=mesh, in_specs=in_specs, out_specs=out_specs, check_vma=False
    )
```

```python
import jax
import jax.numpy as jnp
from jax import lax
from jax.experimental import pallas as pl
from jax.experimental.pallas import tpu as pltpu
from jax.sharding import PartitionSpec as P

D = 2048
HEAD_DIM = 256
ROT = 64
EPS = 1e-05
FLOOR = -1e30
BF = jnp.bfloat16
F32 = jnp.float32


def dot(a, b, dims):
    return lax.dot_general(a, b, (dims, ((), ())), preferred_element_type=F32)


def rotation(places):
    half_rot = ROT // 2
    frequency = 10000.0 ** (jnp.arange(half_rot, dtype=F32) * (-2.0 / ROT))
    angles = places.astype(F32)[:, None] * frequency[None, :]
    return jnp.cos(angles)[:, None, :], jnp.sin(angles)[:, None, :]


def rotate(field, cosine, sine):
    half_rot = ROT // 2
    front = field[..., :half_rot]
    back = field[..., half_rot:ROT]
    return jnp.concatenate(
        [front * cosine - back * sine, back * cosine + front * sine, field[..., ROT:]], -1
    )


def gelu_pair(z):
    phi_cdf = 0.5 * (1.0 + lax.erf(z * 0.7071067811865476))
    density = 0.3989422804014327 * jnp.exp(-0.5 * z * z)
    return z * phi_cdf, phi_cdf + z * density


def per_device_any(
    tokens,
    cotangent,
    lengths,
    block_slot,
    gain_attn,
    shift_attn,
    gain_mlp,
    shift_mlp,
    w_qkv,
    b_qkv,
    w_out,
    b_out,
    w_up,
    b_up,
    w_down,
    b_down,
):
    seqs, block_rows, _ = tokens.shape
    rows = seqs * block_rows
    shard = w_qkv.shape[0]
    heads = w_qkv.shape[1]
    width_qkv = heads * 3 * HEAD_DIM
    width_att = heads * HEAD_DIM
    units = w_up.shape[1]
    fsdp = ("seq", "batch")
    scale = HEAD_DIM ** (-0.5)
    seq_count = lax.axis_size("seq")
    device_ids = jnp.arange(seq_count, dtype=jnp.int32)
    own_slot = jnp.sum(jnp.where(device_ids == lax.axis_index("seq"), block_slot, 0))
    offsets = jnp.arange(block_rows, dtype=jnp.int32)
    query_places = own_slot * block_rows + offsets
    key_places = (block_slot[:, None] * block_rows + offsets[None, :]).reshape(-1)

    attn_shard = jnp.concatenate([w_qkv.reshape(shard, width_qkv), w_out.T], 1)
    mlp_shard = jnp.concatenate([w_up, w_down.T], 1)
    attn_full = lax.all_gather(attn_shard, fsdp, axis=0, tiled=True)
    mlp_full = lax.all_gather(mlp_shard, fsdp, axis=0, tiled=True)
    full_qkv = attn_full[:, :width_qkv]
    full_out_t = attn_full[:, width_qkv:]
    full_up = mlp_full[:, :units]
    full_down_t = mlp_full[:, units:]

    token_rows = tokens.astype(F32).reshape(rows, D)
    centered = token_rows - jnp.mean(token_rows, -1, keepdims=True)
    inverse = lax.rsqrt(jnp.mean(jnp.square(centered), -1, keepdims=True) + EPS)
    xhat = centered * inverse
    input_attn = (xhat * gain_attn + shift_attn).astype(BF)
    input_mlp = (xhat * gain_mlp + shift_mlp).astype(BF)

    valid = (query_places[None, :] < lengths[:, None]).astype(F32)
    grad_rows = (cotangent.astype(F32) * valid[..., None]).reshape(rows, D)
    grad_low = grad_rows.astype(BF)

    project = dot(input_attn, full_qkv, ((1,), (0,))).reshape(
        seqs, block_rows, heads, 3 * HEAD_DIM
    ) + b_qkv
    cosine, sine = rotation(query_places)
    queries = rotate(project[..., :HEAD_DIM], cosine, sine).astype(BF)
    keys = rotate(project[..., HEAD_DIM : 2 * HEAD_DIM], cosine, sine).astype(BF)
    values = project[..., 2 * HEAD_DIM :].astype(BF)
    pair = jnp.concatenate([keys, values], -1)
    gathered = lax.all_gather(pair, "seq", axis=0, tiled=False)
    gathered = jnp.transpose(gathered, (1, 3, 0, 2, 4)).reshape(
        seqs, heads, seq_count * block_rows, 2 * HEAD_DIM
    )
    all_keys = gathered[..., :HEAD_DIM]
    all_values = gathered[..., HEAD_DIM:]

    hidden_pre = dot(input_mlp, full_up, ((1,), (0,))) + b_up
    gelu, slope = gelu_pair(hidden_pre)
    activated = gelu.astype(BF)
    grad_hidden = dot(grad_low, full_down_t, ((1,), (0,))) * slope
    hidden_low = grad_hidden.astype(BF)
    bias_up_sum = jnp.sum(grad_hidden, 0)

    grad_att = dot(grad_low, full_out_t, ((1,), (0,))).reshape(
        seqs, block_rows, heads, HEAD_DIM
    ).astype(BF)

    causal = key_places[None, None, :] <= query_places[None, :, None]
    inside = key_places[None, None, :] < lengths[:, None, None]
    mask = (causal & inside)[:, None]
    scores = jnp.einsum("schd,shtd->shct", queries, all_keys, preferred_element_type=F32) * scale
    scores = jnp.where(mask, scores, FLOOR)
    top = jnp.max(scores, -1, keepdims=True)
    weights = jnp.where(mask, jnp.exp(scores - top), 0.0)
    probs = weights / jnp.sum(weights, -1, keepdims=True)
    prob_low = probs.astype(BF)
    attended = jnp.einsum("shct,shtd->schd", prob_low, all_values, preferred_element_type=F32)
    attended = attended.astype(BF).reshape(rows, width_att)

    partial = dot(attended, full_out_t, ((1,), (1,))) + dot(activated, full_down_t, ((1,), (1,)))
    branch = lax.psum(partial.astype(BF), "tensor").astype(F32)

    grad_mlp_weights = jnp.concatenate(
        [dot(input_mlp, hidden_low, ((0,), (0,))), dot(grad_low, activated, ((0,), (0,)))], 1
    ).astype(BF)
    mlp_reduced = lax.psum_scatter(
        grad_mlp_weights, fsdp, scatter_dimension=0, tiled=True
    ).astype(F32)

    grad_probs = jnp.einsum("schd,shtd->shct", grad_att, all_values, preferred_element_type=F32)
    delta = jnp.sum(probs * grad_probs, -1, keepdims=True)
    grad_scores = (probs * (grad_probs - delta)).astype(BF)
    grad_query = jnp.einsum("shct,shtd->schd", grad_scores, all_keys, preferred_element_type=F32) * scale
    key_term = jnp.einsum("shct,schd->tshd", grad_scores, queries, preferred_element_type=F32) * scale
    value_term = jnp.einsum("shct,schd->tshd", prob_low, grad_att, preferred_element_type=F32)
    terms = jnp.concatenate([key_term, value_term], -1).astype(BF)
    own_terms = lax.psum_scatter(terms, "seq", scatter_dimension=0, tiled=True).astype(F32)
    own_terms = jnp.swapaxes(own_terms, 0, 1)
    grad_key = own_terms[..., :HEAD_DIM]
    grad_value = own_terms[..., HEAD_DIM:]
    grad_project = jnp.concatenate(
        [rotate(grad_query, cosine, -sine), rotate(grad_key, cosine, -sine), grad_value], -1
    ).reshape(rows, width_qkv)
    bias_qkv_sum = jnp.sum(grad_project, 0)
    project_low = grad_project.astype(BF)

    grad_norm_attn = dot(project_low, full_qkv, ((1,), (1,)))
    grad_norm_mlp = dot(hidden_low, full_up, ((1,), (1,)))
    norm_sums = jnp.stack(
        [
            jnp.sum(grad_norm_attn * xhat, 0),
            jnp.sum(grad_norm_attn, 0),
            jnp.sum(grad_norm_mlp * xhat, 0),
            jnp.sum(grad_norm_mlp, 0),
        ]
    )
    grad_xhat = grad_norm_attn * gain_attn + grad_norm_mlp * gain_mlp
    input_part = inverse * (
        grad_xhat
        - jnp.mean(grad_xhat, -1, keepdims=True)
        - xhat * jnp.mean(grad_xhat * xhat, -1, keepdims=True)
    )
    input_part, branch = lax.optimization_barrier((input_part.astype(BF), branch))
    input_sum = lax.psum(input_part, "tensor").astype(F32)
    mixed = (token_rows + branch + b_out + b_down).astype(BF).reshape(tokens.shape)
    tokens_grad = (grad_rows + input_sum).reshape(tokens.shape)

    grad_attn_weights = jnp.concatenate(
        [dot(input_attn, project_low, ((0,), (0,))), dot(grad_low, attended, ((0,), (0,)))], 1
    ).astype(BF)
    attn_reduced = lax.psum_scatter(
        grad_attn_weights, fsdp, scatter_dimension=0, tiled=True
    ).astype(F32)

    norm_sums = lax.psum(norm_sums, "tensor").reshape(-1)
    small = lax.psum(
        jnp.concatenate([norm_sums, bias_qkv_sum, jnp.sum(grad_rows, 0), bias_up_sum]), fsdp
    )
    norm_sums = small[: 4 * D].reshape(4, D)
    small = small[4 * D :]
    bias_qkv_sum = small[:width_qkv].reshape(b_qkv.shape)
    bias_out_sum = small[width_qkv : width_qkv + D]
    bias_up_sum = small[width_qkv + D :]
    return (
        mixed,
        tokens_grad,
        norm_sums[0],
        norm_sums[1],
        norm_sums[2],
        norm_sums[3],
        attn_reduced[:, :width_qkv].reshape(w_qkv.shape),
        bias_qkv_sum,
        attn_reduced[:, width_qkv:].T,
        bias_out_sum,
        mlp_reduced[:, :units],
        bias_up_sum,
        mlp_reduced[:, units:].T,
        bias_out_sum,
    )


def exchange(array, axis, flip):
    size = lax.axis_size(axis)
    return lax.ppermute(array, axis, [(i, i ^ flip) for i in range(size)])


def after(array, *others):
    return lax.optimization_barrier((array, *others))[0]


def along_x(array):
    return exchange(array, "seq", 2)


def along_y(array):
    return exchange(array, "batch", 1)


def to_core(array):
    return exchange(array, "seq", 1)


ORDER = (0, 2, 4, 6, 1, 3, 5, 7)


def block_ins(blocks, width, column):
    return [(pl.BlockSpec((256, width), lambda j: (0, column(j))), b) for b in blocks]


def both_cores(own, by_x, by_y, far, *others):
    own_c, by_x_c, by_y_c, far_c = others
    return (own, by_y, own_c, by_y_c, by_x, far, by_x_c, far_c)


def call(body, grid, ins, outs, scratch=(), flops=0, moved=0, vmem=60, aliases={}):
    return pl.pallas_call(
        body,
        grid=grid,
        in_specs=[spec for spec, _ in ins],
        out_specs=[spec for spec, _ in outs],
        out_shape=[shape for _, shape in outs],
        scratch_shapes=list(scratch),
        input_output_aliases=aliases,
        compiler_params=pltpu.CompilerParams(vmem_limit_bytes=vmem * 1024 * 1024),
        cost_estimate=pl.CostEstimate(flops=flops, bytes_accessed=moved, transcendentals=0),
    )(*[array for _, array in ins])


def call_placed(body, grid, info, ins, outs, scratch=(), flops=0, moved=0, vmem=60):
    return pl.pallas_call(
        body,
        grid_spec=pltpu.PrefetchScalarGridSpec(
            num_scalar_prefetch=1,
            grid=grid,
            in_specs=[spec for spec, _ in ins],
            out_specs=[spec for spec, _ in outs],
            scratch_shapes=list(scratch),
        ),
        out_shape=[shape for _, shape in outs],
        compiler_params=pltpu.CompilerParams(vmem_limit_bytes=vmem * 1024 * 1024),
        cost_estimate=pl.CostEstimate(flops=flops, bytes_accessed=moved, transcendentals=0),
    )(info, *[array for _, array in ins])


def smem():
    return pl.BlockSpec(memory_space=pltpu.SMEM)


def any_place():
    return pl.BlockSpec(memory_space=pl.ANY)


def whole(array):
    dims = len(array.shape)
    return pl.BlockSpec(array.shape, lambda *_: (0,) * dims, pipeline_mode=pl.Buffered(1))


def block(shape, index):
    return pl.BlockSpec(shape, index)


def struct(shape, dtype):
    return jax.ShapeDtypeStruct(shape, dtype)


def columns(ref, info, place):
    start = pl.multiple_of((info[0] ^ place) * 256, 256)
    return ref[:, pl.ds(start, 256)]


def norm_body(info, tok, cot, gain_a, shift_a, gain_m, shift_m, in_a, in_m, grad, grad_sum):
    step = pl.program_id(0)
    t = tok[...].astype(F32)
    centered = t - jnp.mean(t, -1, keepdims=True)
    xhat = centered * lax.rsqrt(jnp.mean(centered * centered, -1, keepdims=True) + EPS)
    in_a[...] = (xhat * gain_a[...] + shift_a[...]).astype(BF)
    in_m[...] = (xhat * gain_m[...] + shift_m[...]).astype(BF)
    place = info[1] * 256 + lax.broadcasted_iota(jnp.int32, t.shape, 0)
    g = jnp.where(place < info[5 + step], cot[...].astype(F32), 0.0)
    grad[...] = g.astype(BF)

    @pl.when(step == 0)
    def _():
        grad_sum[...] = jnp.zeros_like(grad_sum)

    grad_sum[...] += jnp.sum(g, 0, keepdims=True)


def matched(x, blocks, info):
    left = jnp.concatenate([columns(x, info, r) for r in range(8)], 1)
    right = jnp.concatenate([b[...] for b in blocks], 0)
    return jnp.dot(left, right, preferred_element_type=F32)


def turn(z, cos, front, back):
    first = z[:, :128]
    first = (
        first * cos
        + pltpu.roll(first, 96, 1) * front
        + pltpu.roll(first, 32, 1) * back
    )
    return jnp.concatenate([first, z[:, 128:]], 1)


def qkv_body(info, x, bias, cos, front, back, *refs):
    blocks, (q, kv_a, kv_b) = (refs[:8], refs[8:16]), refs[16:]
    step = pl.program_id(0)
    heads = [matched(x, blocks[h], info) + bias[h : h + 1] for h in range(2)]

    def turned():
        c, f, b = (jnp.concatenate([t[...]] * 4, 0) for t in (cos, front, back))
        return jnp.concatenate([turn(z, c, f, b) for z in heads], 1).astype(BF)

    @pl.when(step == 0)
    def _():
        q[...] = turned()

    @pl.when(step == 1)
    def _():
        k = turned()
        kv_a[...] = k[:512]
        kv_b[...] = k[512:]

    @pl.when(step == 2)
    def _():
        v = jnp.concatenate(heads, 1).astype(BF)
        kv_a[...] = v[:512]
        kv_b[...] = v[512:]


def grad_att_body(info, g, *refs):
    refs[16][...] = jnp.concatenate(
        [matched(g, refs[:8], info), matched(g, refs[8:16], info)], 1
    ).astype(BF)


def up_body(info, x, bias, *refs):
    blocks, (act, slope) = refs[:8], refs[8:]
    z = matched(x, blocks, info) + bias[...]
    gelu, steep = gelu_pair(z)
    act[...] = gelu.astype(BF)
    slope[...] = steep.astype(BF)


def hidden_body(info, g, slope, *refs):
    low, total = refs[8:]
    grad = matched(g, refs[:8], info) * slope[...].astype(F32)
    low[...] = grad.astype(BF)
    total[...] = jnp.sum(grad, 0, keepdims=True)


def nt(a, b):
    return lax.dot_general(a, b, (((1,), (1,)), ((), ())), preferred_element_type=F32)


def tn(a, b):
    return lax.dot_general(a, b, (((0,), (0,)), ((), ())), preferred_element_type=F32)


def attention_body(first_seq, info, q_ref, ga_ref, cos, front, back, *refs):
    keys, values = refs[:4], refs[4:8]
    att, dq, dq_sum, keep, send = refs[8:]
    terms = (keep.at[0], send.at[0], keep.at[1], send.at[1])
    seq = pl.program_id(0)
    head = pl.program_id(1)
    scale = HEAD_DIM ** (-0.5)
    length = info[5 + first_seq + seq]
    q = q_ref[...]
    ga = ga_ref[...]
    row_place = info[1] * 256 + lax.broadcasted_iota(jnp.int32, (256, 256), 0)
    column = lax.broadcasted_iota(jnp.int32, (256, 256), 1)
    scores = []
    masks = []
    for r in range(4):
        key_place = info[1 + r] * 256 + column
        allowed = (key_place <= row_place) & (key_place < length)
        masks.append(allowed)
        scores.append(jnp.where(allowed, nt(q, keys[r][...]) * scale, FLOOR))
    top = jnp.max(jnp.maximum(jnp.maximum(scores[0], scores[1]), jnp.maximum(scores[2], scores[3])), -1, keepdims=True)
    weights = [jnp.where(m, jnp.exp(s - top), 0.0) for s, m in zip(scores, masks)]
    total = jnp.sum(weights[0] + weights[1] + weights[2] + weights[3], -1, keepdims=True)
    inverse = 1.0 / total
    probs = [w * inverse for w in weights]
    low = [p.astype(BF) for p in probs]
    out = jnp.zeros((256, 256), F32)
    for r in range(4):
        out += jnp.dot(low[r], values[r][...], preferred_element_type=F32)
    att[...] = out.astype(BF)
    grad_probs = [nt(ga, values[r][...]) for r in range(4)]
    products = [p * g for p, g in zip(probs, grad_probs)]
    delta = jnp.sum(products[0] + products[1] + products[2] + products[3], -1, keepdims=True)
    grad_q = jnp.zeros((256, 256), F32)
    key_columns = pl.ds(pl.multiple_of(head * 256, 256), 256)
    value_columns = pl.ds(pl.multiple_of(head * 256 + 512, 256), 256)
    for r in range(4):
        grad_scores = (probs[r] * (grad_probs[r] - delta)).astype(BF)
        grad_q += jnp.dot(grad_scores, keys[r][...], preferred_element_type=F32)
        terms[r][:, key_columns] = (tn(grad_scores, q) * scale).astype(BF)
        terms[r][:, value_columns] = tn(low[r], ga).astype(BF)
    grad_q = turn(grad_q * scale, cos[...], -front[...], -back[...])
    dq[...] = grad_q.astype(BF)
    dq_sum[...] = jnp.sum(grad_q, 0, keepdims=True)[None, None]


def streamed(blocks, width, column):
    return [
        (pl.BlockSpec((256, width), lambda *ids: (0, column), pipeline_mode=pl.Buffered(1)), blocks[r])
        for r in ORDER
    ]


def branch_body(info, att, act, *refs):
    w_att = (refs[:8], refs[8:16])
    w_act, outs = refs[16:24], refs[24:]
    for i, r in enumerate(ORDER):
        there = pl.ds(pl.multiple_of((info[0] ^ r) * 256, 256), 256)
        part = nt(att[:, :256], w_att[0][i][...]) + nt(att[:, 256:], w_att[1][i][...])
        part = (part + nt(act[...], w_act[i][...])).astype(BF)
        outs[0][:, there] = part[:256]
        outs[1][:, there] = part[256:]


def weight_part(refs):
    products = [tn(refs[i][...], refs[i + 1][...]) for i in range(0, len(refs), 2)]
    return products[0] if len(products) == 1 else jnp.concatenate(products, 1)


def weight_send_body(info, *refs):
    refs[-1][...] = weight_part(refs[:-1]).astype(BF)


def weight_add_body(info, *refs):
    received, outs = refs[-5], refs[-4:]
    step = pl.program_id(0)
    part = (weight_part(refs[:-5]) + received[...].astype(F32)).astype(BF)
    for i, out in enumerate(outs):

        @pl.when(step == i)
        def _():
            out[...] = part


def weight_first(info, pairs, x_first):
    width = 2048
    last, first = (4, 1) if not x_first else (1, 4)
    order = (first, first | last, 0, last)
    cost = dict(flops=2 * 1024 * 1024 * width, moved=2 * (1024 * 1024 + 1024 * width * 2))

    def places(flip):
        def index(i, info):
            place = jnp.where(
                i == 0, order[0], jnp.where(i == 1, order[1], jnp.where(i == 2, order[2], order[3]))
            )
            return 0, info[0] ^ place ^ flip

        return index

    fixed = lambda array: pl.BlockSpec(array.shape, lambda i, info: (0, 0), pipeline_mode=pl.Buffered(1))

    def left(flip):
        return [
            operand
            for x, h in pairs
            for operand in ((block((1024, 256), places(flip)), x), (fixed(h), h))
        ]

    row = lambda i, info: (i, 0)
    sent = call_placed(
        weight_send_body,
        (4,),
        info,
        left(2),
        [(block((256, width), row), struct((1024, width), BF))],
        **cost,
    )[0]

    def second(received):
        return call_placed(
            weight_add_body,
            (4,),
            info,
            left(0) + [(block((256, width), row), received)],
            [(block((256, width), lambda i, info: (0, 0)), struct((256, width), BF))] * 4,
            **cost,
        )

    return sent, second


def project_body(info, q, own, core, far, cos, front, back, low, kv_sum):
    c, f, b = (jnp.concatenate([t[...]] * 2, 0) for t in (cos, front, back))
    for head in range(2):
        mine = slice(head * 256, head * 256 + 256)
        low[:, head * 768 : head * 768 + 256] = q[:, mine]
        for kind in range(2):
            cut = slice(kind * 512 + head * 256, kind * 512 + head * 256 + 256)
            grad = own[:, cut].astype(F32) + core[:, cut].astype(F32) + far[:, cut].astype(F32)
            if kind == 0:
                grad = turn(grad, c, -f, -b)
            kv_sum[:, head * 512 + kind * 256 : head * 512 + kind * 256 + 256] = jnp.sum(grad, 0, keepdims=True)
            start = head * 768 + 256 + kind * 256
            low[:, start : start + 256] = grad.astype(BF)


def input_body(info, low, hid, tok, gain_a, gain_m, *refs):
    w_qkv = (refs[:8], refs[8:16])
    w_up, parts, sums, (gx, xh) = refs[16:24], refs[24:26], refs[26], refs[27:]
    t = tok[...].astype(F32)
    centered = t - jnp.mean(t, -1, keepdims=True)
    inverse = lax.rsqrt(jnp.mean(centered * centered, -1, keepdims=True) + EPS)
    xh[...] = centered * inverse
    for i, r in enumerate(ORDER):
        there = pl.ds(pl.multiple_of((info[0] ^ r) * 256, 256), 256)
        from_attn = nt(low[:, :768], w_qkv[0][i][:, :768]) + nt(low[:, 768:], w_qkv[1][i][:, :768])
        from_mlp = nt(hid[...], w_up[i][...])
        xhat = xh[:, there]
        sums[0:1, there] = jnp.sum(from_attn * xhat, 0, keepdims=True)
        sums[1:2, there] = jnp.sum(from_attn, 0, keepdims=True)
        sums[2:3, there] = jnp.sum(from_mlp * xhat, 0, keepdims=True)
        sums[3:4, there] = jnp.sum(from_mlp, 0, keepdims=True)
        gx[:, there] = from_attn * gain_a[:, there] + from_mlp * gain_m[:, there]
    grad = gx[...]
    xhat = xh[...]
    mean = jnp.mean(grad, -1, keepdims=True)
    along = jnp.mean(grad * xhat, -1, keepdims=True)
    out = (inverse * (grad - mean - xhat * along)).astype(BF)
    parts[0][...] = out[:256]
    parts[1][...] = out[256:]


ENDS_IN = [(0, 1), (3, 2)]
MIDDLE = [(1, 2), (2, 1)]
ENDS_OUT = [(1, 0), (2, 3)]


def plus(a, b):
    return (a.astype(F32) + b.astype(F32)).astype(BF)


def bar(*arrays):
    return lax.optimization_barrier(arrays)


class Hops:
    def __init__(self, info, rows_of, tok, grad, bias):
        self.info = info
        self.rows_of = rows_of
        self.given = (tok, grad, bias)
        self.mine, self.came, self.pair, self.crossed, self.total, self.back = ({} for _ in range(6))
        self.out = [None, None]

    def send(self, k, block):
        self.mine[k] = block
        self.came[k] = lax.ppermute(block, "tensor", ENDS_IN)

    def flying(self, k):
        return [group[i] for group, i in ((self.came, k), (self.crossed, k - 1), (self.back, k - 2)) if i in group]

    def land(self, k, *arrived):
        arrived = list(arrived)
        tok, grad, bias = self.given
        ins, outs, kinds, aliases = [(smem(), self.info)], [], [], {}
        half = lambda array: (block((128, D), lambda i: (i, 0)), array)
        for kind, (group, i) in enumerate(((self.came, k), (self.crossed, k - 1), (self.back, k - 2))):
            if i not in group:
                continue
            came = arrived.pop(0)
            if kind < 2:
                ins += [half((self.mine, self.pair)[kind][i]), half(came)]
                outs.append((block((128, D), lambda i: (i, 0)), struct((256, D), BF)))
            else:
                place, which = i % 4, i // 4
                kept = (block((128, D), lambda i, place=place: (2 * place + i, 0)), grad if which else tok)
                ins += [half(self.total[i]), half(came), kept]
                if not which:
                    ins.append((whole(bias), bias))
                shape = struct((1024, D), F32 if which else BF)
                outs.append((kept[0], shape))
                kind += which
            kinds.append(kind)
        old = self.out[kinds[-1] - 2] if kinds[-1] >= 2 else None
        if old is not None:
            aliases[len(ins)] = len(outs) - 1
            ins.append((any_place(), old))
        made = call(lambda *refs: land_body(kinds, *refs), (2,), ins, outs, aliases=aliases)
        for kind, array in zip(kinds, made):
            if kind == 0:
                self.pair[k] = array
                self.crossed[k] = lax.ppermute(array, "tensor", MIDDLE)
            elif kind == 1:
                self.total[k - 1] = array
                self.back[k - 1] = lax.ppermute(array, "tensor", ENDS_OUT)
            else:
                self.out[kind - 2] = array
        return made


def land_body(kinds, info, *refs):
    refs = list(refs)
    outs = refs[-len(kinds) :]
    for kind, out in zip(kinds, outs):
        if kind < 2:
            a, b = refs.pop(0), refs.pop(0)
            out[...] = (a[...].astype(F32) + b[...].astype(F32)).astype(BF)
            continue
        total, came, kept = refs.pop(0), refs.pop(0), refs.pop(0)
        summed = jnp.where(info[9] > 0, total[...], came[...]).astype(F32) + kept[...].astype(F32)
        out[...] = (summed + refs.pop(0)[...]).astype(BF) if kind == 2 else summed


def per_device_links(
    tokens,
    cotangent,
    lengths,
    block_slot,
    gain_attn,
    shift_attn,
    gain_mlp,
    shift_mlp,
    w_qkv,
    b_qkv,
    w_out,
    b_out,
    w_up,
    b_up,
    w_down,
    b_down,
):
    rows = 1024
    seq_id = lax.axis_index("seq")
    slots = [jnp.sum(jnp.where(jnp.arange(4) == (seq_id ^ r), block_slot, 0)) for r in range(4)]
    tensor_id = lax.axis_index("tensor")
    inner = ((tensor_id == 1) | (tensor_id == 2)).astype(jnp.int32)
    me = seq_id * 2 + lax.axis_index("batch")
    info = jnp.concatenate([jnp.stack([me, *slots]), lengths, inner.reshape(1)]).astype(jnp.int32)
    tok = tokens.reshape(rows, D)
    cot = cotangent.reshape(rows, D)
    cosine, sine = rotation(slots[0] * 256 + jnp.arange(256, dtype=jnp.int32))
    cosine, sine = cosine[:, 0], sine[:, 0]
    zero = jnp.zeros_like(sine)
    cos_t = jnp.concatenate([cosine, cosine, zero + 1.0, zero + 1.0], 1)
    front_t = jnp.concatenate([-sine, zero, zero, zero], 1)
    back_t = jnp.concatenate([zero, sine, zero, zero], 1)
    tables = [(whole(t), t) for t in (cos_t, front_t, back_t)]
    gains = [v.reshape(1, D) for v in (gain_attn, shift_attn, gain_mlp, shift_mlp)]

    def info_in(*tokens_before):
        return (smem(), after(info, *tokens_before) if tokens_before else info)

    row_block = lambda n: block((256, n), lambda i: (i, 0))
    row_struct = lambda n, kind=BF: struct((rows, n), kind)
    tall = lambda n, index: block((256, n), index)

    head_own = jnp.concatenate(
        [w for h in range(2) for w in (w_qkv[:, h], w_out[h * 256 : (h + 1) * 256].T)], 1
    )
    head_x, head_y = along_x(head_own), along_y(head_own)
    head_c = to_core(head_own)
    in_a, in_m, grad_low, grad_sum = call(
        norm_body,
        (4,),
        [info_in(), (row_block(D), tok), (row_block(D), cot)] + [(whole(v), v) for v in gains],
        [(row_block(D), row_struct(D))] * 3 + [(block((1, D), lambda i: (0, 0)), struct((1, D), F32))],
        moved=5 * rows * D * 2,
    )
    down_own = w_down.T
    head_x, head_y, head_c, in_a, in_m, grad_low, down_own = bar(
        head_x, head_y, head_c, in_a, in_m, grad_low, down_own
    )

    far_y, far_x = along_y(head_x[:128]), along_x(head_y[128:])
    others = [head_c, to_core(head_x), to_core(head_y)]
    far_y, far_x, up_own, *others = bar(far_y, far_x, w_up, *others)

    up_x, up_y = along_x(up_own), along_y(up_own)
    far = jnp.concatenate([far_y, far_x], 0)
    heads = both_cores(head_own, head_x, head_y, far, *others, to_core(far))
    bias = jnp.swapaxes(b_qkv.reshape(2, 3, 256), 0, 1)
    q, kv_a, kv_b = call(
        lambda info, x, bias, *refs: qkv_body(info, x, bias.at[0], *refs),
        (3,),
        [info_in(), (whole(in_a), in_a), (block((1, 2, 256), lambda j: (j, 0, 0)), bias)]
        + tables
        + block_ins(heads, 256, lambda j: j)
        + block_ins(heads, 256, lambda j: j + 4),
        [
            (block((rows, 512), lambda j: (0, 0)), row_struct(512)),
            (block((512, 512), lambda j: (0, jnp.maximum(j - 1, 0))), struct((512, 1024), BF)),
            (block((512, 512), lambda j: (0, jnp.maximum(j - 1, 0))), struct((512, 1024), BF)),
        ],
        flops=2 * rows * D * 1536,
        moved=2 * (rows * D + D * 1536 + rows * 1536),
    )
    kv_x = along_x(kv_a)
    grad_att = call(
        grad_att_body,
        (1,),
        [info_in(q), (whole(grad_low), grad_low)]
        + block_ins(heads, 256, lambda j: 3)
        + block_ins(heads, 256, lambda j: 7),
        [(block((rows, 512), lambda j: (0, 0)), row_struct(512))],
        flops=2 * rows * D * 512,
        moved=2 * (rows * D + D * 512 + rows * 512),
    )[0]
    up_c = to_core(after(up_own, q))
    up_x, up_y, up_c, grad_att = bar(up_x, up_y, up_c, grad_att)

    up_far = along_y(up_x)
    others = [up_c, to_core(up_x), to_core(up_y)]
    down_own = after(down_own, *others)
    down_x, down_y = along_x(down_own), along_y(down_own)
    up_far, kv_x, kv_a, *others = bar(up_far, kv_x, kv_a, *others)
    ups = both_cores(up_own, up_x, up_y, up_far, *others, to_core(up_far))

    def kv_refs(own, by_x):
        both = to_core(jnp.concatenate([own, by_x], 0))
        return [(own, 0), (both, 0), (by_x, 0), (both, 2)]

    kv = [kv_refs(kv_a, kv_x)]
    act, slope = call(
        up_body,
        (4,),
        [info_in(grad_att), (whole(in_m), in_m), (block((1, 512), lambda j: (0, j)), b_up.reshape(1, -1))]
        + block_ins(ups, 512, lambda j: j),
        [(block((rows, 512), lambda j: (0, j)), row_struct(2048))] * 2,
        flops=2 * rows * D * 2048,
        moved=2 * (rows * D + D * 2048 + 2 * rows * 2048),
    )
    down_c = to_core(after(down_own, ups[7]))
    down_x, down_y, down_c, act, slope = bar(down_x, down_y, down_c, act, slope)

    def attention(part, *before):
        base = part * 2
        spot = lambda offset: block((256, 256), lambda s, h: (s + base, h + offset))
        local = lambda offset, row=0: block((256, 256), lambda s, h: (s + row, h + offset))
        return call(
            lambda *refs: attention_body(base, *refs),
            (2, 2),
            [info_in(*before), (spot(0), q), (spot(0), grad_att)]
            + tables
            + [(local(0, row), b) for b, row in kv[part]]
            + [(local(2, row), b) for b, row in kv[part]],
            [
                (local(0), struct((512, 512), BF)),
                (local(0), struct((512, 512), BF)),
                (block((1, 1, 1, 256), lambda s, h: (s, h, 0, 0)), struct((2, 2, 1, 256), F32)),
            ]
            + [(block((2, 256, 1024), lambda s, h: (0, s, 0)), struct((2, 512, 1024), BF))] * 2,
            flops=4 * 6 * 2 * 256 * 1024 * 256,
            moved=4 * 2 * 256 * 256 * 24,
        )

    def branch(part, att, *before):
        return call(
            branch_body,
            (1,),
            [info_in(*before), (whole(att), att), (block((512, 2048), lambda i: (part, 0)), act)]
            + streamed(heads, 256, 3)
            + streamed(heads, 256, 7)
            + streamed(downs, 2048, 0),
            [(block((256, D), lambda i: (0, 0)), struct((256, D), BF))] * 2,
            flops=2 * 512 * D * 2560,
            moved=2 * (512 * 2560 + D * 2560 + 512 * D),
        )

    far_y, far_x = along_y(down_x[:128]), along_x(down_y[128:])
    others = [down_c, to_core(down_x), to_core(down_y)]
    att_a, dq_a, dq_sum_a, keep_a, send_a = attention(0, down_x)
    far_y, far_x, att_a, kv_b, send_a, *others = bar(far_y, far_x, att_a, kv_b, send_a, *others)

    far = jnp.concatenate([far_y, far_x], 0)
    downs = both_cores(down_own, down_x, down_y, far, *others, to_core(far))
    kv_x = along_x(kv_b)
    received_a = to_core(send_a)
    branch_a = branch(0, att_a)
    kv_x, received_a, *branch_a = bar(kv_x, received_a, *branch_a)

    hops = Hops(info, 256, tok, grad_low, (b_out + b_down).reshape(1, D))
    attended = None

    def hidden_call(before):
        return call(
            hidden_body,
            (4,),
            [info_in(before), (whole(grad_low), grad_low), (block((rows, 512), lambda j: (0, j)), slope)]
            + block_ins(downs, 512, lambda j: j),
            [
                (block((rows, 512), lambda j: (0, j)), row_struct(2048)),
                (block((1, 512), lambda j: (0, j)), struct((1, 2048), F32)),
            ],
            flops=2 * rows * D * 2048,
            moved=2 * (rows * D + D * 2048 + 2 * rows * 2048),
        )

    def project(dq, keep, came, far, before):
        return call(
            project_body,
            (1,),
            [info_in(before), (whole(dq), dq)]
            + [(pl.BlockSpec((None, 512, 1024), lambda i: (0, 0, 0)), t) for t in (keep, came)]
            + [(whole(far), far)]
            + tables,
            [
                (block((512, 1536), lambda i: (0, 0)), struct((512, 1536), BF)),
                (block((1, 1024), lambda i: (0, 0)), struct((1, 1024), F32)),
            ],
            moved=2 * 512 * 5000,
        )

    def input_part(half, low, before):
        fixed = lambda shape, row=0: pl.BlockSpec(shape, lambda i: (row, 0), pipeline_mode=pl.Buffered(1))
        return call(
            input_body,
            (1,),
            [info_in(before), (whole(low), low)]
            + [(fixed((512, 2048), half), t) for t in (hidden_low, tok)]
            + [(whole(t), t) for t in (gains[0], gains[2])]
            + streamed(heads, 1024, 0)
            + streamed(heads, 1024, 1)
            + streamed(ups, 2048, 0),
            [(block((256, D), lambda i: (0, 0)), struct((256, D), BF))] * 2
            + [(block((8, D), lambda i: (0, 0)), struct((8, D), F32))],
            scratch=[pltpu.VMEM((512, D), F32), pltpu.VMEM((512, D), F32)],
            flops=2 * 512 * D * 3584,
            moved=2 * (512 * 6000 + D * 3584),
        )

    hops.send(0, branch_a[0])
    kv.append(kv_refs(kv_b, kv_x))
    far_a = along_x(plus(keep_a[1], received_a[1]))
    hidden_low, b_up_sum = hidden_call(branch_a[0])
    att_b, dq_b, dq_sum_b, keep_b, send_b = attention(1, hidden_low)
    flown, far_a, att_b, send_b = bar(hops.flying(0), far_a, att_b, send_b)

    pair, = hops.land(0, *flown)
    hops.send(1, after(branch_a[1], pair))
    received_b = to_core(after(send_b, pair))
    branch_b = branch(1, att_b, pair)
    down_sent, down_second = weight_first(after(info, branch_b[0]), [(grad_low, act)], False)
    flown, received_b, down_sent, *branch_b = bar(hops.flying(1), received_b, down_sent, *branch_b)

    pair, *_ = hops.land(1, *flown)
    hops.send(2, after(branch_b[0], pair))
    far_b = along_x(plus(after(keep_b[1], pair), received_b[1]))
    down_received = to_core(after(down_sent, pair))
    low_a, kv_sum_a = project(dq_a, keep_a, received_a, far_a, pair)
    first, second, norm_sum_a = input_part(0, low_a, low_a)
    flown, far_b, down_received, first, second = bar(hops.flying(2), far_b, down_received, first, second)

    pair, *_ = hops.land(2, *flown)
    hops.send(3, after(branch_b[1], pair))
    low_b, kv_sum_b = project(dq_b, keep_b, received_b, far_b, pair)
    third, fourth, norm_sum_b = input_part(1, low_b, low_b)
    project_low = jnp.concatenate([low_a, after(low_b, third)], 0)
    attended = jnp.concatenate([att_a, after(att_b, third)], 0)
    q_sums = (dq_sum_a + dq_sum_b).sum(0).reshape(2, 1, 256)
    kv_total = (kv_sum_a + kv_sum_b).reshape(2, 2, 256)
    bias_qkv = jnp.concatenate([q_sums, kv_total], 1).reshape(-1)
    norm_sums = (norm_sum_a + norm_sum_b)[:4].reshape(-1)
    small = jnp.concatenate([norm_sums, bias_qkv, grad_sum[0], b_up_sum[0]]).reshape(-1, 128)
    flown, third, fourth, small, project_low, attended = bar(
        hops.flying(3), third, fourth, small, project_low, attended
    )

    pair, *_ = hops.land(3, *flown)
    hops.send(4, after(first, pair))
    small = after(small, pair)
    small = small + to_core(small)
    down = down_second(after(down_received, pair))
    small = small + along_x(small)
    up_sent, up_second = weight_first(after(info, down[0], small), [(in_m, hidden_low)], True)
    flown, up_sent, small, *down = bar(hops.flying(4), up_sent, small, *down)

    pair, *_ = hops.land(4, *flown)
    hops.send(5, after(second, pair))
    down_got = [along_y(after(down[0], pair))]
    up_received = to_core(after(up_sent, pair))
    attn_sent, attn_second = weight_first(
        after(info, pair), [(in_a, project_low), (grad_low, attended)], False
    )
    up = up_second(after(up_received, attn_sent))
    flown, down_got[0], attn_sent, *up = bar(hops.flying(5), down_got[0], attn_sent, *up)

    pair, *_ = hops.land(5, *flown)
    hops.send(6, after(third, pair))
    attn_received = to_core(after(attn_sent, pair))
    down_got.append(along_y(after(down[1], pair)))
    up_got = [along_x(after(up[0], pair))]
    attn = attn_second(after(attn_received, pair))
    flown, down_got[1], up_got[0], *attn = bar(hops.flying(6), down_got[1], up_got[0], *attn)

    pair, *_ = hops.land(6, *flown)
    hops.send(7, after(fourth, pair))
    up_got.append(along_x(after(up[1], pair)))
    attn_got = [along_y(after(attn[0], pair))]
    down_leaving = plus(after(down[3], pair), down_got[1])
    flown, up_got[1], attn_got[0], down_leaving = bar(hops.flying(7), up_got[1], attn_got[0], down_leaving)

    pair, *_ = hops.land(7, *flown)
    down_last = along_x(after(down_leaving, pair))
    attn_got.append(along_y(after(attn[1], pair)))
    small = after(small, pair)
    small = small + along_y(small)
    up_leaving = plus(after(up[3], pair), up_got[1])
    flown, down_last, attn_got[1], small, up_leaving = bar(
        hops.flying(8), down_last, attn_got[1], small, up_leaving
    )

    sum_8, *_ = hops.land(8, *flown)
    attn_last = along_x(plus(after(attn[3], sum_8), attn_got[1]))
    up_last = along_y(after(up_leaving, sum_8))
    norms = after(small[:64], sum_8)
    for flip in (1, 2):
        norms = norms + exchange(norms, "tensor", flip)

    def total(keep, got, last):
        return keep.astype(F32) + got.astype(F32) + last.astype(F32)

    down_grad = total(after(down[2], sum_8), down_got[0], down_last).T
    flown, attn_last, norms, up_last, down_grad = bar(hops.flying(9), attn_last, norms, up_last, down_grad)
    hops.land(9, *flown)
    mixed, tokens_grad = hops.out

    norms = norms.reshape(4, D)
    small = small[64:].reshape(-1)
    bias_out = small[1536 : 1536 + D]

    attn_grad = total(attn[2], attn_got[0], attn_last)
    return (
        mixed.reshape(tokens.shape),
        tokens_grad.reshape(tokens.shape),
        norms[0],
        norms[1],
        norms[2],
        norms[3],
        attn_grad[:, :1536].reshape(w_qkv.shape),
        small[:1536].reshape(b_qkv.shape),
        attn_grad[:, 1536:].T,
        bias_out,
        total(up[2], up_got[0], up_last),
        small[1536 + D :],
        down_grad,
        bias_out,
    )


def solution(mesh):
    in_specs = (
        P("batch", "seq", None),
        P("batch", "seq", None),
        P("batch"),
        P(),
        P(),
        P(),
        P(),
        P(),
        P(("seq", "batch"), "tensor", None),
        P("tensor", None),
        P("tensor", ("seq", "batch")),
        P(),
        P(("seq", "batch"), "tensor"),
        P("tensor"),
        P("tensor", ("seq", "batch")),
        P(),
    )
    out_specs = (
        P("batch", "seq", None),
        P("batch", "seq", None),
        P(),
        P(),
        P(),
        P(),
        P(("seq", "batch"), "tensor", None),
        P("tensor", None),
        P("tensor", ("seq", "batch")),
        P(),
        P(("seq", "batch"), "tensor"),
        P("tensor"),
        P("tensor", ("seq", "batch")),
        P(),
    )
    links = tuple(mesh.shape[axis] for axis in ("seq", "batch", "tensor"))
    per_device = per_device_links if links == (4, 2, 4) else per_device_any
    return jax.shard_map(
        per_device, mesh=mesh, in_specs=in_specs, out_specs=out_specs, check_vma=False
    )
```

```python
import jax
import jax.numpy as jnp
from jax import lax
from jax.experimental import pallas as pl
from jax.experimental.pallas import tpu as pltpu
from jax.sharding import PartitionSpec as P

D = 2048
HEAD_DIM = 256
ROT = 64
EPS = 1e-05
FLOOR = -1e30
BF = jnp.bfloat16
F32 = jnp.float32


def dot(a, b, dims):
    return lax.dot_general(a, b, (dims, ((), ())), preferred_element_type=F32)


def rotation(places):
    half_rot = ROT // 2
    frequency = 10000.0 ** (jnp.arange(half_rot, dtype=F32) * (-2.0 / ROT))
    angles = places.astype(F32)[:, None] * frequency[None, :]
    return jnp.cos(angles)[:, None, :], jnp.sin(angles)[:, None, :]


def rotate(field, cosine, sine):
    half_rot = ROT // 2
    front = field[..., :half_rot]
    back = field[..., half_rot:ROT]
    return jnp.concatenate(
        [front * cosine - back * sine, back * cosine + front * sine, field[..., ROT:]], -1
    )


def gelu_pair(z):
    phi_cdf = 0.5 * (1.0 + lax.erf(z * 0.7071067811865476))
    density = 0.3989422804014327 * jnp.exp(-0.5 * z * z)
    return z * phi_cdf, phi_cdf + z * density


def per_device_any(
    tokens,
    cotangent,
    lengths,
    block_slot,
    gain_attn,
    shift_attn,
    gain_mlp,
    shift_mlp,
    w_qkv,
    b_qkv,
    w_out,
    b_out,
    w_up,
    b_up,
    w_down,
    b_down,
):
    seqs, block_rows, _ = tokens.shape
    rows = seqs * block_rows
    shard = w_qkv.shape[0]
    heads = w_qkv.shape[1]
    width_qkv = heads * 3 * HEAD_DIM
    width_att = heads * HEAD_DIM
    units = w_up.shape[1]
    fsdp = ("seq", "batch")
    scale = HEAD_DIM ** (-0.5)
    seq_count = lax.axis_size("seq")
    device_ids = jnp.arange(seq_count, dtype=jnp.int32)
    own_slot = jnp.sum(jnp.where(device_ids == lax.axis_index("seq"), block_slot, 0))
    offsets = jnp.arange(block_rows, dtype=jnp.int32)
    query_places = own_slot * block_rows + offsets
    key_places = (block_slot[:, None] * block_rows + offsets[None, :]).reshape(-1)

    attn_shard = jnp.concatenate([w_qkv.reshape(shard, width_qkv), w_out.T], 1)
    mlp_shard = jnp.concatenate([w_up, w_down.T], 1)
    attn_full = lax.all_gather(attn_shard, fsdp, axis=0, tiled=True)
    mlp_full = lax.all_gather(mlp_shard, fsdp, axis=0, tiled=True)
    full_qkv = attn_full[:, :width_qkv]
    full_out_t = attn_full[:, width_qkv:]
    full_up = mlp_full[:, :units]
    full_down_t = mlp_full[:, units:]

    token_rows = tokens.astype(F32).reshape(rows, D)
    centered = token_rows - jnp.mean(token_rows, -1, keepdims=True)
    inverse = lax.rsqrt(jnp.mean(jnp.square(centered), -1, keepdims=True) + EPS)
    xhat = centered * inverse
    input_attn = (xhat * gain_attn + shift_attn).astype(BF)
    input_mlp = (xhat * gain_mlp + shift_mlp).astype(BF)

    valid = (query_places[None, :] < lengths[:, None]).astype(F32)
    grad_rows = (cotangent.astype(F32) * valid[..., None]).reshape(rows, D)
    grad_low = grad_rows.astype(BF)

    project = dot(input_attn, full_qkv, ((1,), (0,))).reshape(
        seqs, block_rows, heads, 3 * HEAD_DIM
    ) + b_qkv
    cosine, sine = rotation(query_places)
    queries = rotate(project[..., :HEAD_DIM], cosine, sine).astype(BF)
    keys = rotate(project[..., HEAD_DIM : 2 * HEAD_DIM], cosine, sine).astype(BF)
    values = project[..., 2 * HEAD_DIM :].astype(BF)
    pair = jnp.concatenate([keys, values], -1)
    gathered = lax.all_gather(pair, "seq", axis=0, tiled=False)
    gathered = jnp.transpose(gathered, (1, 3, 0, 2, 4)).reshape(
        seqs, heads, seq_count * block_rows, 2 * HEAD_DIM
    )
    all_keys = gathered[..., :HEAD_DIM]
    all_values = gathered[..., HEAD_DIM:]

    hidden_pre = dot(input_mlp, full_up, ((1,), (0,))) + b_up
    gelu, slope = gelu_pair(hidden_pre)
    activated = gelu.astype(BF)
    grad_hidden = dot(grad_low, full_down_t, ((1,), (0,))) * slope
    hidden_low = grad_hidden.astype(BF)
    bias_up_sum = jnp.sum(grad_hidden, 0)

    grad_att = dot(grad_low, full_out_t, ((1,), (0,))).reshape(
        seqs, block_rows, heads, HEAD_DIM
    ).astype(BF)

    causal = key_places[None, None, :] <= query_places[None, :, None]
    inside = key_places[None, None, :] < lengths[:, None, None]
    mask = (causal & inside)[:, None]
    scores = jnp.einsum("schd,shtd->shct", queries, all_keys, preferred_element_type=F32) * scale
    scores = jnp.where(mask, scores, FLOOR)
    top = jnp.max(scores, -1, keepdims=True)
    weights = jnp.where(mask, jnp.exp(scores - top), 0.0)
    probs = weights / jnp.sum(weights, -1, keepdims=True)
    prob_low = probs.astype(BF)
    attended = jnp.einsum("shct,shtd->schd", prob_low, all_values, preferred_element_type=F32)
    attended = attended.astype(BF).reshape(rows, width_att)

    partial = dot(attended, full_out_t, ((1,), (1,))) + dot(activated, full_down_t, ((1,), (1,)))
    branch = lax.psum(partial.astype(BF), "tensor").astype(F32)

    grad_mlp_weights = jnp.concatenate(
        [dot(input_mlp, hidden_low, ((0,), (0,))), dot(grad_low, activated, ((0,), (0,)))], 1
    ).astype(BF)
    mlp_reduced = lax.psum_scatter(
        grad_mlp_weights, fsdp, scatter_dimension=0, tiled=True
    ).astype(F32)

    grad_probs = jnp.einsum("schd,shtd->shct", grad_att, all_values, preferred_element_type=F32)
    delta = jnp.sum(probs * grad_probs, -1, keepdims=True)
    grad_scores = (probs * (grad_probs - delta)).astype(BF)
    grad_query = jnp.einsum("shct,shtd->schd", grad_scores, all_keys, preferred_element_type=F32) * scale
    key_term = jnp.einsum("shct,schd->tshd", grad_scores, queries, preferred_element_type=F32) * scale
    value_term = jnp.einsum("shct,schd->tshd", prob_low, grad_att, preferred_element_type=F32)
    terms = jnp.concatenate([key_term, value_term], -1).astype(BF)
    own_terms = lax.psum_scatter(terms, "seq", scatter_dimension=0, tiled=True).astype(F32)
    own_terms = jnp.swapaxes(own_terms, 0, 1)
    grad_key = own_terms[..., :HEAD_DIM]
    grad_value = own_terms[..., HEAD_DIM:]
    grad_project = jnp.concatenate(
        [rotate(grad_query, cosine, -sine), rotate(grad_key, cosine, -sine), grad_value], -1
    ).reshape(rows, width_qkv)
    bias_qkv_sum = jnp.sum(grad_project, 0)
    project_low = grad_project.astype(BF)

    grad_norm_attn = dot(project_low, full_qkv, ((1,), (1,)))
    grad_norm_mlp = dot(hidden_low, full_up, ((1,), (1,)))
    norm_sums = jnp.stack(
        [
            jnp.sum(grad_norm_attn * xhat, 0),
            jnp.sum(grad_norm_attn, 0),
            jnp.sum(grad_norm_mlp * xhat, 0),
            jnp.sum(grad_norm_mlp, 0),
        ]
    )
    grad_xhat = grad_norm_attn * gain_attn + grad_norm_mlp * gain_mlp
    input_part = inverse * (
        grad_xhat
        - jnp.mean(grad_xhat, -1, keepdims=True)
        - xhat * jnp.mean(grad_xhat * xhat, -1, keepdims=True)
    )
    input_part, branch = lax.optimization_barrier((input_part.astype(BF), branch))
    input_sum = lax.psum(input_part, "tensor").astype(F32)
    mixed = (token_rows + branch + b_out + b_down).astype(BF).reshape(tokens.shape)
    tokens_grad = (grad_rows + input_sum).reshape(tokens.shape)

    grad_attn_weights = jnp.concatenate(
        [dot(input_attn, project_low, ((0,), (0,))), dot(grad_low, attended, ((0,), (0,)))], 1
    ).astype(BF)
    attn_reduced = lax.psum_scatter(
        grad_attn_weights, fsdp, scatter_dimension=0, tiled=True
    ).astype(F32)

    norm_sums = lax.psum(norm_sums, "tensor").reshape(-1)
    small = lax.psum(
        jnp.concatenate([norm_sums, bias_qkv_sum, jnp.sum(grad_rows, 0), bias_up_sum]), fsdp
    )
    norm_sums = small[: 4 * D].reshape(4, D)
    small = small[4 * D :]
    bias_qkv_sum = small[:width_qkv].reshape(b_qkv.shape)
    bias_out_sum = small[width_qkv : width_qkv + D]
    bias_up_sum = small[width_qkv + D :]
    return (
        mixed,
        tokens_grad,
        norm_sums[0],
        norm_sums[1],
        norm_sums[2],
        norm_sums[3],
        attn_reduced[:, :width_qkv].reshape(w_qkv.shape),
        bias_qkv_sum,
        attn_reduced[:, width_qkv:].T,
        bias_out_sum,
        mlp_reduced[:, :units],
        bias_up_sum,
        mlp_reduced[:, units:].T,
        bias_out_sum,
    )


def exchange(array, axis, flip):
    size = lax.axis_size(axis)
    return lax.ppermute(array, axis, [(i, i ^ flip) for i in range(size)])


def after(array, *others):
    return lax.optimization_barrier((array, *others))[0]


def along_x(array):
    return exchange(array, "seq", 2)


def along_y(array):
    return exchange(array, "batch", 1)


def to_core(array):
    return exchange(array, "seq", 1)


ORDER = (0, 2, 4, 6, 1, 3, 5, 7)


def block_ins(blocks, width, column):
    return [(pl.BlockSpec((256, width), lambda j: (0, column(j))), b) for b in blocks]


def both_cores(own, by_x, by_y, far, *others):
    own_c, by_x_c, by_y_c, far_c = others
    return (own, by_y, own_c, by_y_c, by_x, far, by_x_c, far_c)


def call(body, grid, ins, outs, scratch=(), flops=0, moved=0, vmem=60, aliases={}):
    return pl.pallas_call(
        body,
        grid=grid,
        in_specs=[spec for spec, _ in ins],
        out_specs=[spec for spec, _ in outs],
        out_shape=[shape for _, shape in outs],
        scratch_shapes=list(scratch),
        input_output_aliases=aliases,
        compiler_params=pltpu.CompilerParams(vmem_limit_bytes=vmem * 1024 * 1024),
        cost_estimate=pl.CostEstimate(flops=0, bytes_accessed=0, transcendentals=0),
    )(*[array for _, array in ins])


def call_placed(body, grid, info, ins, outs, scratch=(), flops=0, moved=0, vmem=60):
    return pl.pallas_call(
        body,
        grid_spec=pltpu.PrefetchScalarGridSpec(
            num_scalar_prefetch=1,
            grid=grid,
            in_specs=[spec for spec, _ in ins],
            out_specs=[spec for spec, _ in outs],
            scratch_shapes=list(scratch),
        ),
        out_shape=[shape for _, shape in outs],
        compiler_params=pltpu.CompilerParams(vmem_limit_bytes=vmem * 1024 * 1024),
        cost_estimate=pl.CostEstimate(flops=0, bytes_accessed=0, transcendentals=0),
    )(info, *[array for _, array in ins])


def smem():
    return pl.BlockSpec(memory_space=pltpu.SMEM)


def any_place():
    return pl.BlockSpec(memory_space=pl.ANY)


def whole(array):
    dims = len(array.shape)
    return pl.BlockSpec(array.shape, lambda *_: (0,) * dims, pipeline_mode=pl.Buffered(1))


def block(shape, index):
    return pl.BlockSpec(shape, index)


def struct(shape, dtype):
    return jax.ShapeDtypeStruct(shape, dtype)


def columns(ref, info, place):
    start = pl.multiple_of((info[0] ^ place) * 256, 256)
    return ref[:, pl.ds(start, 256)]


def norm_body(info, tok, cot, gain_a, shift_a, gain_m, shift_m, in_a, in_m, grad, grad_sum):
    step = pl.program_id(0)
    t = tok[...].astype(F32)
    centered = t - jnp.mean(t, -1, keepdims=True)
    xhat = centered * lax.rsqrt(jnp.mean(centered * centered, -1, keepdims=True) + EPS)
    in_a[...] = (xhat * gain_a[...] + shift_a[...]).astype(BF)
    in_m[...] = (xhat * gain_m[...] + shift_m[...]).astype(BF)
    place = info[1] * 256 + lax.broadcasted_iota(jnp.int32, t.shape, 0)
    g = jnp.where(place < info[5 + step], cot[...].astype(F32), 0.0)
    grad[...] = g.astype(BF)

    @pl.when(step == 0)
    def _():
        grad_sum[...] = jnp.zeros_like(grad_sum)

    grad_sum[...] += jnp.sum(g, 0, keepdims=True)


def matched(x, blocks, info):
    left = jnp.concatenate([columns(x, info, r) for r in range(8)], 1)
    right = jnp.concatenate([b[...] for b in blocks], 0)
    return jnp.dot(left, right, preferred_element_type=F32)


def turn(z, cos, front, back):
    first = z[:, :128]
    first = (
        first * cos
        + pltpu.roll(first, 96, 1) * front
        + pltpu.roll(first, 32, 1) * back
    )
    return jnp.concatenate([first, z[:, 128:]], 1)


def qkv_body(info, x, bias, cos, front, back, *refs):
    blocks, (q, kv_a, kv_b) = (refs[:8], refs[8:16]), refs[16:]
    step = pl.program_id(0)
    heads = [matched(x, blocks[h], info) + bias[h : h + 1] for h in range(2)]

    def turned():
        c, f, b = (jnp.concatenate([t[...]] * 4, 0) for t in (cos, front, back))
        return jnp.concatenate([turn(z, c, f, b) for z in heads], 1).astype(BF)

    @pl.when(step == 0)
    def _():
        q[...] = turned()

    @pl.when(step == 1)
    def _():
        k = turned()
        kv_a[...] = k[:512]
        kv_b[...] = k[512:]

    @pl.when(step == 2)
    def _():
        v = jnp.concatenate(heads, 1).astype(BF)
        kv_a[...] = v[:512]
        kv_b[...] = v[512:]


def grad_att_body(info, g, *refs):
    refs[16][...] = jnp.concatenate(
        [matched(g, refs[:8], info), matched(g, refs[8:16], info)], 1
    ).astype(BF)


def up_body(info, x, bias, *refs):
    blocks, (act, slope) = refs[:8], refs[8:]
    z = matched(x, blocks, info) + bias[...]
    gelu, steep = gelu_pair(z)
    act[...] = gelu.astype(BF)
    slope[...] = steep.astype(BF)


def hidden_body(info, g, slope, *refs):
    low, total = refs[8:]
    grad = matched(g, refs[:8], info) * slope[...].astype(F32)
    low[...] = grad.astype(BF)
    total[...] = jnp.sum(grad, 0, keepdims=True)


def nt(a, b):
    return lax.dot_general(a, b, (((1,), (1,)), ((), ())), preferred_element_type=F32)


def tn(a, b):
    return lax.dot_general(a, b, (((0,), (0,)), ((), ())), preferred_element_type=F32)


def attention_body(first_seq, info, q_ref, ga_ref, cos, front, back, *refs):
    keys, values = refs[:4], refs[4:8]
    att, dq, dq_sum, keep, send = refs[8:]
    terms = (keep.at[0], send.at[0], keep.at[1], send.at[1])
    seq = pl.program_id(0)
    head = pl.program_id(1)
    scale = HEAD_DIM ** (-0.5)
    length = info[5 + first_seq + seq]
    q = q_ref[...]
    ga = ga_ref[...]
    row_place = info[1] * 256 + lax.broadcasted_iota(jnp.int32, (256, 256), 0)
    column = lax.broadcasted_iota(jnp.int32, (256, 256), 1)
    scores = []
    masks = []
    for r in range(4):
        key_place = info[1 + r] * 256 + column
        allowed = (key_place <= row_place) & (key_place < length)
        masks.append(allowed)
        scores.append(jnp.where(allowed, nt(q, keys[r][...]) * scale, FLOOR))
    top = jnp.max(jnp.maximum(jnp.maximum(scores[0], scores[1]), jnp.maximum(scores[2], scores[3])), -1, keepdims=True)
    weights = [jnp.where(m, jnp.exp(s - top), 0.0) for s, m in zip(scores, masks)]
    total = jnp.sum(weights[0] + weights[1] + weights[2] + weights[3], -1, keepdims=True)
    inverse = 1.0 / total
    probs = [w * inverse for w in weights]
    low = [p.astype(BF) for p in probs]
    out = jnp.zeros((256, 256), F32)
    for r in range(4):
        out += jnp.dot(low[r], values[r][...], preferred_element_type=F32)
    att[...] = out.astype(BF)
    grad_probs = [nt(ga, values[r][...]) for r in range(4)]
    products = [p * g for p, g in zip(probs, grad_probs)]
    delta = jnp.sum(products[0] + products[1] + products[2] + products[3], -1, keepdims=True)
    grad_q = jnp.zeros((256, 256), F32)
    key_columns = pl.ds(pl.multiple_of(head * 256, 256), 256)
    value_columns = pl.ds(pl.multiple_of(head * 256 + 512, 256), 256)
    for r in range(4):
        grad_scores = (probs[r] * (grad_probs[r] - delta)).astype(BF)
        grad_q += jnp.dot(grad_scores, keys[r][...], preferred_element_type=F32)
        terms[r][:, key_columns] = (tn(grad_scores, q) * scale).astype(BF)
        terms[r][:, value_columns] = tn(low[r], ga).astype(BF)
    grad_q = turn(grad_q * scale, cos[...], -front[...], -back[...])
    dq[...] = grad_q.astype(BF)
    dq_sum[...] = jnp.sum(grad_q, 0, keepdims=True)[None, None]


def streamed(blocks, width, column):
    return [(pl.BlockSpec((256, width), lambda i: (0, column(i))), blocks[r]) for r in ORDER]


def branch_body(info, att, act, *refs):
    w_att, w_act, outs, total = refs[:8], refs[8:16], refs[16:18], refs[18]
    step = pl.program_id(0)

    def part(i):
        return nt(att[...], w_att[i][...]) + nt(act[...], w_act[i][...])

    @pl.when(step == 0)
    def _():
        for i in range(8):
            total[:, i * 256 : (i + 1) * 256] = part(i)

    @pl.when(step == 1)
    def _():
        for i, r in enumerate(ORDER):
            there = pl.ds(pl.multiple_of((info[0] ^ r) * 256, 256), 256)
            done = (total[:, i * 256 : (i + 1) * 256] + part(i)).astype(BF)
            outs[0][:, there] = done[:256]
            outs[1][:, there] = done[256:]


def weight_part(refs):
    products = [tn(refs[i][...], refs[i + 1][...]) for i in range(0, len(refs), 2)]
    return products[0] if len(products) == 1 else jnp.concatenate(products, 1)


def weight_send_body(info, *refs):
    refs[-1][...] = weight_part(refs[:-1]).astype(BF)


def weight_add_body(info, *refs):
    received, outs = refs[-5], refs[-4:]
    step = pl.program_id(0)
    part = (weight_part(refs[:-5]) + received[...].astype(F32)).astype(BF)
    for i, out in enumerate(outs):

        @pl.when(step == i)
        def _():
            out[...] = part


def weight_first(info, pairs, x_first):
    width = 2048
    last, first = (4, 1) if not x_first else (1, 4)
    order = (first, first | last, 0, last)
    cost = dict(flops=2 * 1024 * 1024 * width, moved=2 * (1024 * 1024 + 1024 * width * 2))

    def places(flip):
        def index(i, info):
            place = jnp.where(
                i == 0, order[0], jnp.where(i == 1, order[1], jnp.where(i == 2, order[2], order[3]))
            )
            return 0, info[0] ^ place ^ flip

        return index

    fixed = lambda array: pl.BlockSpec(array.shape, lambda i, info: (0, 0), pipeline_mode=pl.Buffered(1))

    def left(flip):
        return [
            operand
            for x, h in pairs
            for operand in ((block((1024, 256), places(flip)), x), (fixed(h), h))
        ]

    row = lambda i, info: (i, 0)
    sent = call_placed(
        weight_send_body,
        (4,),
        info,
        left(2),
        [(block((256, width), row), struct((1024, width), BF))],
        **cost,
    )[0]

    def second(received):
        return call_placed(
            weight_add_body,
            (4,),
            info,
            left(0) + [(block((256, width), row), received)],
            [(block((256, width), lambda i, info: (0, 0)), struct((256, width), BF))] * 4,
            **cost,
        )

    return sent, second


def project_body(info, q, own, core, far, cos, front, back, low, kv_sum):
    c, f, b = (jnp.concatenate([t[...]] * 2, 0) for t in (cos, front, back))
    for head in range(2):
        mine = slice(head * 256, head * 256 + 256)
        low[:, head * 768 : head * 768 + 256] = q[:, mine]
        for kind in range(2):
            cut = slice(kind * 512 + head * 256, kind * 512 + head * 256 + 256)
            grad = own[:, cut].astype(F32) + core[:, cut].astype(F32) + far[:, cut].astype(F32)
            if kind == 0:
                grad = turn(grad, c, -f, -b)
            kv_sum[:, head * 512 + kind * 256 : head * 512 + kind * 256 + 256] = jnp.sum(grad, 0, keepdims=True)
            start = head * 768 + 256 + kind * 256
            low[:, start : start + 256] = grad.astype(BF)


def input_body(info, low, hid, tok, gain_a, gain_m, *refs):
    w_qkv, w_up, parts, sums, (gx, xh, inv) = refs[:8], refs[8:16], refs[16:18], refs[18], refs[19:]
    step = pl.program_id(0)

    def products(first):
        for i, r in enumerate(ORDER):
            there = pl.ds(pl.multiple_of((info[0] ^ r) * 256, 256), 256)
            from_attn = nt(low[...], w_qkv[i][:, :768])
            from_mlp = nt(hid[...], w_up[i][...])
            xhat = xh[:, there]
            columns_sums = [from_attn * xhat, from_attn, from_mlp * xhat, from_mlp]
            grad = from_attn * gain_a[:, there] + from_mlp * gain_m[:, there]
            for row, values in enumerate(columns_sums):
                added = jnp.sum(values, 0, keepdims=True)
                sums[row : row + 1, there] = added if first else sums[row : row + 1, there] + added
            gx[:, there] = grad if first else gx[:, there] + grad

    @pl.when(step == 0)
    def _():
        t = tok[...].astype(F32)
        centered = t - jnp.mean(t, -1, keepdims=True)
        inverse = lax.rsqrt(jnp.mean(centered * centered, -1, keepdims=True) + EPS)
        xh[...] = centered * inverse
        inv[...] = jnp.broadcast_to(inverse, inv.shape)
        products(True)

    @pl.when(step == 1)
    def _():
        products(False)
        grad = gx[...]
        xhat = xh[...]
        mean = jnp.mean(grad, -1, keepdims=True)
        along = jnp.mean(grad * xhat, -1, keepdims=True)
        out = (inv[:, :1] * (grad - mean - xhat * along)).astype(BF)
        parts[0][...] = out[:256]
        parts[1][...] = out[256:]


def plus(a, b):
    return (a.astype(F32) + b.astype(F32)).astype(BF)


def bar(*arrays):
    return lax.optimization_barrier(arrays)


def finish_body(keep, got, last, up_keep, up_got, up_last, qkv, out, up):
    total = keep[...].astype(F32) + got[...].astype(F32) + last[...].astype(F32)
    for head in range(2):
        qkv[:, head, :] = total[:, head * 768 : head * 768 + 768]
    out[...] = total[:, 1536:].T
    up[...] = up_keep[...].astype(F32) + up_got[...].astype(F32) + up_last[...].astype(F32)


class Hops:
    def __init__(self, info, tok, grad, bias):
        self.info = info
        self.given = (tok, grad, bias)
        self.mine = {}
        self.ready = {}
        self.pair = None
        self.out = [None, None]

    def start(self, block):
        self.leaving = self.mine[0] = block
        return [exchange(block, "tensor", 1)]

    def land(self, j, arrived, next_block=None):
        half = lambda array: (block((128, D), lambda i: (i, 0)), array)
        fresh = (block((128, D), lambda i: (i, 0)), struct((256, D), BF))
        parts, ins, outs = [], [(smem(), self.info)], []
        if j >= 2:
            self.ready[j - 2] = (self.leaving, arrived[0])
        if j < 8:
            parts.append("pair")
            ins += [half(self.mine[j]), half(arrived[0])]
            outs.append(fresh)
        if 1 <= j <= 8:
            parts.append("sum" if next_block is None else "either")
            ins += [half(self.pair), half(arrived[1])]
            if next_block is not None:
                ins.append(half(next_block))
            outs.append(fresh)
        made = list(call(lambda *refs: land_body(parts, *refs), (2,), ins, outs))
        done = made[0]
        if next_block is not None:
            self.mine[j + 1] = next_block
        pair = made.pop(0) if j < 8 else None
        self.leaving = made.pop(0) if j else after(next_block, pair)
        flying = [exchange(self.leaving, "tensor", 1)]
        if pair is not None:
            self.pair = pair
            flying.append(lax.ppermute(pair, "tensor", [(1, 2), (2, 1)]))
        return flying, done

    def write(self, k, before):
        tok, grad, bias = self.given
        which, place = divmod(k, 4)
        half = lambda array: (block((128, D), lambda i: (i, 0)), array)
        kept = (block((128, D), lambda i: (2 * place + i, 0)), (tok, grad)[which])
        ins = [(smem(), after(self.info, before))] + [half(array) for array in self.ready[k]] + [kept]
        if not which:
            ins.append((whole(bias), bias))
        aliases = {}
        if self.out[which] is not None:
            aliases[len(ins)] = 0
            ins.append((any_place(), self.out[which]))
        made = call(
            (mixed_body, tokens_grad_body)[which],
            (2,),
            ins,
            [(kept[0], struct((1024, D), (BF, F32)[which]))],
            aliases=aliases,
        )[0]
        self.out[which] = made
        return made


def land_body(parts, info, *refs):
    refs = list(refs)
    outs = refs[-len(parts) :]
    for part, out in zip(parts, outs):
        a, b = refs.pop(0), refs.pop(0)
        summed = (a[...].astype(F32) + b[...].astype(F32)).astype(BF)
        out[...] = jnp.where(info[9] > 0, summed, refs.pop(0)[...]) if part == "either" else summed


def tokens_grad_body(info, total, came, grad, *refs):
    refs[-1][...] = jnp.where(info[9] > 0, total[...], came[...]).astype(F32) + grad[...].astype(F32)


def mixed_body(info, total, came, tok, bias, *refs):
    summed = jnp.where(info[9] > 0, total[...], came[...]).astype(F32) + tok[...].astype(F32)
    refs[-1][...] = (summed + bias[...]).astype(BF)


def per_device_links(
    tokens,
    cotangent,
    lengths,
    block_slot,
    gain_attn,
    shift_attn,
    gain_mlp,
    shift_mlp,
    w_qkv,
    b_qkv,
    w_out,
    b_out,
    w_up,
    b_up,
    w_down,
    b_down,
):
    rows = 1024
    seq_id = lax.axis_index("seq")
    slots = [jnp.sum(jnp.where(jnp.arange(4) == (seq_id ^ r), block_slot, 0)) for r in range(4)]
    tensor_id = lax.axis_index("tensor")
    inner = ((tensor_id == 1) | (tensor_id == 2)).astype(jnp.int32)
    me = seq_id * 2 + lax.axis_index("batch")
    info = jnp.concatenate([jnp.stack([me, *slots]), lengths, inner.reshape(1)]).astype(jnp.int32)
    tok = tokens.reshape(rows, D)
    cot = cotangent.reshape(rows, D)
    cosine, sine = rotation(slots[0] * 256 + jnp.arange(256, dtype=jnp.int32))
    cosine, sine = cosine[:, 0], sine[:, 0]
    zero = jnp.zeros_like(sine)
    cos_t = jnp.concatenate([cosine, cosine, zero + 1.0, zero + 1.0], 1)
    front_t = jnp.concatenate([-sine, zero, zero, zero], 1)
    back_t = jnp.concatenate([zero, sine, zero, zero], 1)
    tables = [(whole(t), t) for t in (cos_t, front_t, back_t)]
    gains = [v.reshape(1, D) for v in (gain_attn, shift_attn, gain_mlp, shift_mlp)]

    def info_in(*tokens_before):
        return (smem(), after(info, *tokens_before) if tokens_before else info)

    row_block = lambda n: block((256, n), lambda i: (i, 0))
    row_struct = lambda n, kind=BF: struct((rows, n), kind)
    tall = lambda n, index: block((256, n), index)

    head_own = jnp.concatenate(
        [w for h in range(2) for w in (w_qkv[:, h], w_out[h * 256 : (h + 1) * 256].T)], 1
    )
    head_x, head_y = along_x(head_own), along_y(head_own)
    head_c = to_core(head_own)
    in_a, in_m, grad_low, grad_sum = call(
        norm_body,
        (4,),
        [info_in(), (row_block(D), tok), (row_block(D), cot)] + [(whole(v), v) for v in gains],
        [(row_block(D), row_struct(D))] * 3 + [(block((1, D), lambda i: (0, 0)), struct((1, D), F32))],
        moved=5 * rows * D * 2,
    )
    down_own = w_down.T
    head_x, head_y, head_c, in_a, in_m, grad_low, down_own = bar(
        head_x, head_y, head_c, in_a, in_m, grad_low, down_own
    )

    far_y, far_x = along_y(head_x[:128]), along_x(head_y[128:])
    others = [head_c, to_core(head_x), to_core(head_y)]
    far_y, far_x, up_own, *others = bar(far_y, far_x, w_up, *others)

    up_x, up_y = along_x(up_own), along_y(up_own)
    far = jnp.concatenate([far_y, far_x], 0)
    heads = both_cores(head_own, head_x, head_y, far, *others, to_core(far))
    bias = jnp.swapaxes(b_qkv.reshape(2, 3, 256), 0, 1)
    q, kv_a, kv_b = call(
        lambda info, x, bias, *refs: qkv_body(info, x, bias.at[0], *refs),
        (3,),
        [info_in(), (whole(in_a), in_a), (block((1, 2, 256), lambda j: (j, 0, 0)), bias)]
        + tables
        + block_ins(heads, 256, lambda j: j)
        + block_ins(heads, 256, lambda j: j + 4),
        [
            (block((rows, 512), lambda j: (0, 0)), row_struct(512)),
            (block((512, 512), lambda j: (0, jnp.maximum(j - 1, 0))), struct((512, 1024), BF)),
            (block((512, 512), lambda j: (0, jnp.maximum(j - 1, 0))), struct((512, 1024), BF)),
        ],
        flops=2 * rows * D * 1536,
        moved=2 * (rows * D + D * 1536 + rows * 1536),
    )
    kv_x = along_x(kv_a)
    grad_att = call(
        grad_att_body,
        (1,),
        [info_in(q), (whole(grad_low), grad_low)]
        + block_ins(heads, 256, lambda j: 3)
        + block_ins(heads, 256, lambda j: 7),
        [(block((rows, 512), lambda j: (0, 0)), row_struct(512))],
        flops=2 * rows * D * 512,
        moved=2 * (rows * D + D * 512 + rows * 512),
    )[0]
    up_c = to_core(after(up_own, q))
    up_x, up_y, up_c, grad_att = bar(up_x, up_y, up_c, grad_att)

    up_far = along_y(up_x)
    others = [up_c, to_core(up_x), to_core(up_y)]
    down_own = after(down_own, *others)
    down_x, down_y = along_x(down_own), along_y(down_own)
    up_far, kv_x, kv_a, *others = bar(up_far, kv_x, kv_a, *others)
    ups = both_cores(up_own, up_x, up_y, up_far, *others, to_core(up_far))

    def kv_refs(own, by_x):
        both = to_core(jnp.concatenate([own, by_x], 0))
        return [(own, 0), (both, 0), (by_x, 0), (both, 2)]

    kv = [kv_refs(kv_a, kv_x)]
    act, slope = call(
        up_body,
        (4,),
        [info_in(grad_att), (whole(in_m), in_m), (block((1, 512), lambda j: (0, j)), b_up.reshape(1, -1))]
        + block_ins(ups, 512, lambda j: j),
        [(block((rows, 512), lambda j: (0, j)), row_struct(2048))] * 2,
        flops=2 * rows * D * 2048,
        moved=2 * (rows * D + D * 2048 + 2 * rows * 2048),
    )
    down_c = to_core(after(down_own, ups[7]))
    down_x, down_y, down_c, act, slope = bar(down_x, down_y, down_c, act, slope)

    def attention(part, *before):
        base = part * 2
        spot = lambda offset: block((256, 256), lambda s, h: (s + base, h + offset))
        local = lambda offset, row=0: block((256, 256), lambda s, h: (s + row, h + offset))
        return call(
            lambda *refs: attention_body(base, *refs),
            (2, 2),
            [info_in(*before), (spot(0), q), (spot(0), grad_att)]
            + tables
            + [(local(0, row), b) for b, row in kv[part]]
            + [(local(2, row), b) for b, row in kv[part]],
            [
                (local(0), struct((512, 512), BF)),
                (local(0), struct((512, 512), BF)),
                (block((1, 1, 1, 256), lambda s, h: (s, h, 0, 0)), struct((2, 2, 1, 256), F32)),
            ]
            + [(block((2, 256, 1024), lambda s, h: (0, s, 0)), struct((2, 512, 1024), BF))] * 2,
            flops=4 * 6 * 2 * 256 * 1024 * 256,
            moved=4 * 2 * 256 * 256 * 24,
        )

    def branch(part, att, *before):
        return call(
            branch_body,
            (2,),
            [
                info_in(*before),
                (block((512, 256), lambda i: (0, i)), att),
                (block((512, 1024), lambda i: (part, i)), act),
            ]
            + streamed(heads, 256, lambda i: 3 + 4 * i)
            + streamed(downs, 1024, lambda i: i),
            [(block((256, D), lambda i: (0, 0)), struct((256, D), BF))] * 2,
            scratch=[pltpu.VMEM((512, D), F32)],
            flops=2 * 512 * D * 2560,
            moved=2 * (512 * 2560 + D * 2560 + 512 * D),
        )

    far_y, far_x = along_y(down_x[:128]), along_x(down_y[128:])
    others = [down_c, to_core(down_x), to_core(down_y)]
    att_a, dq_a, dq_sum_a, keep_a, send_a = attention(0, down_x)
    far_y, far_x, att_a, kv_b, send_a, *others = bar(far_y, far_x, att_a, kv_b, send_a, *others)

    far = jnp.concatenate([far_y, far_x], 0)
    downs = both_cores(down_own, down_x, down_y, far, *others, to_core(far))
    kv_x = along_x(kv_b)
    received_a = to_core(send_a)
    branch_a = branch(0, att_a)
    received_a, *branch_a = bar(received_a, *branch_a)

    hops = Hops(info, tok, grad_low, (b_out + b_down).reshape(1, D))

    def hidden_call(before):
        return call(
            hidden_body,
            (4,),
            [info_in(before), (whole(grad_low), grad_low), (block((rows, 512), lambda j: (0, j)), slope)]
            + block_ins(downs, 512, lambda j: j),
            [
                (block((rows, 512), lambda j: (0, j)), row_struct(2048)),
                (block((1, 512), lambda j: (0, j)), struct((1, 2048), F32)),
            ],
            flops=2 * rows * D * 2048,
            moved=2 * (rows * D + D * 2048 + 2 * rows * 2048),
        )

    def project(dq, keep, came, far, before):
        return call(
            project_body,
            (1,),
            [info_in(before), (whole(dq), dq)]
            + [(pl.BlockSpec((None, 512, 1024), lambda i: (0, 0, 0)), t) for t in (keep, came)]
            + [(whole(far), far)]
            + tables,
            [
                (block((512, 1536), lambda i: (0, 0)), struct((512, 1536), BF)),
                (block((1, 1024), lambda i: (0, 0)), struct((1, 1024), F32)),
            ],
            moved=2 * 512 * 5000,
        )

    def input_part(half, low, before):
        return call(
            input_body,
            (2,),
            [
                info_in(before),
                (block((512, 768), lambda i: (0, i)), low),
                (block((512, 1024), lambda i: (half, i)), hidden_low),
                (pl.BlockSpec((512, D), lambda i: (half, 0), pipeline_mode=pl.Buffered(1)), tok),
            ]
            + [(whole(t), t) for t in (gains[0], gains[2])]
            + streamed(heads, 1024, lambda i: i)
            + streamed(ups, 1024, lambda i: i),
            [(block((256, D), lambda i: (0, 0)), struct((256, D), BF))] * 2
            + [(block((8, D), lambda i: (0, 0)), struct((8, D), F32))],
            scratch=[pltpu.VMEM((512, D), F32), pltpu.VMEM((512, D), F32), pltpu.VMEM((512, 128), F32)],
            flops=2 * 512 * D * 3584,
            moved=2 * (512 * 6000 + D * 3584),
        )

    flown = hops.start(branch_a[0])
    far_a = along_x(plus(keep_a[1], received_a[1]))
    hidden_low, b_up_sum = hidden_call(branch_a[0])
    down_sent, down_second = weight_first(after(info, hidden_low), [(grad_low, act)], False)
    flown, far_a, kv_x, down_sent = bar(flown, far_a, kv_x, down_sent)

    flown, done = hops.land(0, flown, branch_a[1])
    kv.append(kv_refs(kv_b, after(kv_x, done)))
    down_received = to_core(after(down_sent, done))
    att_b, dq_b, dq_sum_b, keep_b, send_b = attention(1, done)
    branch_b = branch(1, att_b, att_b)
    flown, down_received, send_b, *branch_b = bar(flown, down_received, send_b, *branch_b)

    flown, done = hops.land(1, flown, branch_b[0])
    received_b = to_core(after(send_b, done))
    low_a, kv_sum_a = project(dq_a, keep_a, received_a, far_a, done)
    first, second, norm_sum_a = input_part(0, low_a, low_a)
    flown, received_b, first, second = bar(flown, received_b, first, second)

    flown, done = hops.land(2, flown, branch_b[1])
    far_b = along_x(plus(after(keep_b[1], done), received_b[1]))
    down = down_second(after(down_received, done))
    up_sent, up_second = weight_first(after(info, down[0]), [(in_m, hidden_low)], False)
    flown, far_b, up_sent, *down = bar(flown, far_b, up_sent, *down)

    flown, done = hops.land(3, flown, first)
    down_got = [along_y(after(down[0], done))]
    up_received = to_core(after(up_sent, done))
    low_b, kv_sum_b = project(dq_b, keep_b, received_b, far_b, done)
    third, fourth, norm_sum_b = input_part(1, low_b, low_b)
    q_sums = (dq_sum_a + dq_sum_b).sum(0).reshape(2, 1, 256)
    kv_total = (kv_sum_a + kv_sum_b).reshape(2, 2, 256)
    bias_qkv = jnp.concatenate([q_sums, kv_total], 1).reshape(-1)
    norm_sums = (norm_sum_a + norm_sum_b)[:4].reshape(-1)
    norms = norm_sums.reshape(-1, 128)
    biases = jnp.concatenate([bias_qkv, grad_sum[0], b_up_sum[0]]).reshape(-1, 128)
    flown, down_got[0], up_received, third, fourth, norms, biases = bar(
        flown, down_got[0], up_received, third, fourth, norms, biases
    )

    flown, done = hops.land(4, flown, second)
    down_got.append(along_y(after(down[1], done)))
    norms_z = exchange(after(norms, done), "tensor", 1)
    up = up_second(after(up_received, done))
    project_low = jnp.concatenate([after(low_a, up[0]), low_b], 0)
    attended = jnp.concatenate([after(att_a, up[0]), att_b], 0)
    attn_sent, attn_second = weight_first(
        after(info, up[0]), [(in_a, project_low), (grad_low, attended)], True
    )
    flown, down_got[1], norms_z, attn_sent, *up = bar(flown, down_got[1], norms_z, attn_sent, *up)

    flown, done = hops.land(5, flown, third)
    attn_received = to_core(after(attn_sent, done))
    down_last = along_x(plus(after(down[3], done), down_got[1]))
    up_got = [along_y(after(up[0], done))]
    attn = attn_second(after(attn_received, done))
    hops.write(0, attn[0])
    flown, down_last, up_got[0], *attn = bar(flown, down_last, up_got[0], *attn)

    flown, done = hops.land(6, flown, fourth)
    up_got.append(along_y(after(up[1], done)))
    attn_got = [along_x(after(attn[0], done))]
    norms = after(norms, done) + norms_z
    norms_z = exchange(norms, "tensor", 2)
    written = hops.write(1, done)
    written = hops.write(2, written)

    def total(keep, got, last):
        return keep.astype(F32) + got.astype(F32) + last.astype(F32)

    down_grad = total(after(down[2], written), down_got[0], down_last).T
    flown, up_got[1], attn_got[0], norms_z, down_grad = bar(flown, up_got[1], attn_got[0], norms_z, down_grad)

    flown, done = hops.land(7, flown)
    attn_got.append(along_x(after(attn[1], done)))
    small = jnp.concatenate([after(norms, done) + norms_z, biases], 0)
    small_c = to_core(small)
    up_leaving = plus(after(up[3], done), up_got[1])
    written = hops.write(3, up_leaving)
    small = after(small, written) + small_c
    small_y = along_y(small)
    written = hops.write(4, small)
    small = after(small, written) + small_y
    small_x = along_x(small)
    hops.write(5, small)
    small = small + small_x
    flown, attn_got[1], small, up_leaving, hops.out[1] = bar(
        flown, attn_got[1], small, up_leaving, hops.out[1]
    )

    flown, done = hops.land(8, flown)
    attn_last = along_y(plus(after(attn[3], done), attn_got[1]))
    up_last = along_x(after(up_leaving, done))
    hops.write(6, up_leaving)
    hops.ready[7] = (hops.leaving, flown[0])
    (leaving, came), attn_last, up_last, hops.out[1] = bar(hops.ready[7], attn_last, up_last, hops.out[1])
    hops.ready[7] = (leaving, came)
    hops.write(7, came)
    mixed, tokens_grad = hops.out

    norms = small[:64].reshape(4, D)
    small = small[64:].reshape(-1)
    bias_out = small[1536 : 1536 + D]

    qkv_grad, out_grad, up_grad = call(
        finish_body,
        (1,),
        [(whole(t), t) for t in (attn[2], attn_got[0], attn_last, up[2], up_got[0], up_last)],
        [
            (block((256, 2, 768), lambda i: (0, 0, 0)), struct((256, 2, 768), F32)),
            (block((512, 256), lambda i: (0, 0)), struct((512, 256), F32)),
            (block((256, 2048), lambda i: (0, 0)), struct((256, 2048), F32)),
        ],
    )
    return (
        mixed.reshape(tokens.shape),
        tokens_grad.reshape(tokens.shape),
        norms[0],
        norms[1],
        norms[2],
        norms[3],
        qkv_grad,
        small[:1536].reshape(b_qkv.shape),
        out_grad,
        bias_out,
        up_grad,
        small[1536 + D :],
        down_grad,
        bias_out,
    )


def solution(mesh):
    in_specs = (
        P("batch", "seq", None),
        P("batch", "seq", None),
        P("batch"),
        P(),
        P(),
        P(),
        P(),
        P(),
        P(("seq", "batch"), "tensor", None),
        P("tensor", None),
        P("tensor", ("seq", "batch")),
        P(),
        P(("seq", "batch"), "tensor"),
        P("tensor"),
        P("tensor", ("seq", "batch")),
        P(),
    )
    out_specs = (
        P("batch", "seq", None),
        P("batch", "seq", None),
        P(),
        P(),
        P(),
        P(),
        P(("seq", "batch"), "tensor", None),
        P("tensor", None),
        P("tensor", ("seq", "batch")),
        P(),
        P(("seq", "batch"), "tensor"),
        P("tensor"),
        P("tensor", ("seq", "batch")),
        P(),
    )
    links = tuple(mesh.shape[axis] for axis in ("seq", "batch", "tensor"))
    per_device = per_device_links if links == (4, 2, 4) else per_device_any
    return jax.shard_map(
        per_device, mesh=mesh, in_specs=in_specs, out_specs=out_specs, check_vma=False
    )
```

```python
import jax
import jax.numpy as jnp
from jax import lax
from jax.experimental import pallas as pl
from jax.experimental.pallas import tpu as pltpu
from jax.sharding import PartitionSpec as P

D = 2048
HEAD_DIM = 256
ROT = 64
EPS = 1e-05
FLOOR = -1e30
BF = jnp.bfloat16
F32 = jnp.float32


def dot(a, b, dims):
    return lax.dot_general(a, b, (dims, ((), ())), preferred_element_type=F32)


def rotation(places):
    half_rot = ROT // 2
    frequency = 10000.0 ** (jnp.arange(half_rot, dtype=F32) * (-2.0 / ROT))
    angles = places.astype(F32)[:, None] * frequency[None, :]
    return jnp.cos(angles)[:, None, :], jnp.sin(angles)[:, None, :]


def rotate(field, cosine, sine):
    half_rot = ROT // 2
    front = field[..., :half_rot]
    back = field[..., half_rot:ROT]
    return jnp.concatenate(
        [front * cosine - back * sine, back * cosine + front * sine, field[..., ROT:]], -1
    )


def gelu_pair(z):
    phi_cdf = 0.5 * (1.0 + lax.erf(z * 0.7071067811865476))
    density = 0.3989422804014327 * jnp.exp(-0.5 * z * z)
    return z * phi_cdf, phi_cdf + z * density


def per_device_any(
    tokens,
    cotangent,
    lengths,
    block_slot,
    gain_attn,
    shift_attn,
    gain_mlp,
    shift_mlp,
    w_qkv,
    b_qkv,
    w_out,
    b_out,
    w_up,
    b_up,
    w_down,
    b_down,
):
    seqs, block_rows, _ = tokens.shape
    rows = seqs * block_rows
    shard = w_qkv.shape[0]
    heads = w_qkv.shape[1]
    width_qkv = heads * 3 * HEAD_DIM
    width_att = heads * HEAD_DIM
    units = w_up.shape[1]
    fsdp = ("seq", "batch")
    scale = HEAD_DIM ** (-0.5)
    seq_count = lax.axis_size("seq")
    device_ids = jnp.arange(seq_count, dtype=jnp.int32)
    own_slot = jnp.sum(jnp.where(device_ids == lax.axis_index("seq"), block_slot, 0))
    offsets = jnp.arange(block_rows, dtype=jnp.int32)
    query_places = own_slot * block_rows + offsets
    key_places = (block_slot[:, None] * block_rows + offsets[None, :]).reshape(-1)

    attn_shard = jnp.concatenate([w_qkv.reshape(shard, width_qkv), w_out.T], 1)
    mlp_shard = jnp.concatenate([w_up, w_down.T], 1)
    attn_full = lax.all_gather(attn_shard, fsdp, axis=0, tiled=True)
    mlp_full = lax.all_gather(mlp_shard, fsdp, axis=0, tiled=True)
    full_qkv = attn_full[:, :width_qkv]
    full_out_t = attn_full[:, width_qkv:]
    full_up = mlp_full[:, :units]
    full_down_t = mlp_full[:, units:]

    token_rows = tokens.astype(F32).reshape(rows, D)
    centered = token_rows - jnp.mean(token_rows, -1, keepdims=True)
    inverse = lax.rsqrt(jnp.mean(jnp.square(centered), -1, keepdims=True) + EPS)
    xhat = centered * inverse
    input_attn = (xhat * gain_attn + shift_attn).astype(BF)
    input_mlp = (xhat * gain_mlp + shift_mlp).astype(BF)

    valid = (query_places[None, :] < lengths[:, None]).astype(F32)
    grad_rows = (cotangent.astype(F32) * valid[..., None]).reshape(rows, D)
    grad_low = grad_rows.astype(BF)

    project = dot(input_attn, full_qkv, ((1,), (0,))).reshape(
        seqs, block_rows, heads, 3 * HEAD_DIM
    ) + b_qkv
    cosine, sine = rotation(query_places)
    queries = rotate(project[..., :HEAD_DIM], cosine, sine).astype(BF)
    keys = rotate(project[..., HEAD_DIM : 2 * HEAD_DIM], cosine, sine).astype(BF)
    values = project[..., 2 * HEAD_DIM :].astype(BF)
    pair = jnp.concatenate([keys, values], -1)
    gathered = lax.all_gather(pair, "seq", axis=0, tiled=False)
    gathered = jnp.transpose(gathered, (1, 3, 0, 2, 4)).reshape(
        seqs, heads, seq_count * block_rows, 2 * HEAD_DIM
    )
    all_keys = gathered[..., :HEAD_DIM]
    all_values = gathered[..., HEAD_DIM:]

    hidden_pre = dot(input_mlp, full_up, ((1,), (0,))) + b_up
    gelu, slope = gelu_pair(hidden_pre)
    activated = gelu.astype(BF)
    grad_hidden = dot(grad_low, full_down_t, ((1,), (0,))) * slope
    hidden_low = grad_hidden.astype(BF)
    bias_up_sum = jnp.sum(grad_hidden, 0)

    grad_att = dot(grad_low, full_out_t, ((1,), (0,))).reshape(
        seqs, block_rows, heads, HEAD_DIM
    ).astype(BF)

    causal = key_places[None, None, :] <= query_places[None, :, None]
    inside = key_places[None, None, :] < lengths[:, None, None]
    mask = (causal & inside)[:, None]
    scores = jnp.einsum("schd,shtd->shct", queries, all_keys, preferred_element_type=F32) * scale
    scores = jnp.where(mask, scores, FLOOR)
    top = jnp.max(scores, -1, keepdims=True)
    weights = jnp.where(mask, jnp.exp(scores - top), 0.0)
    probs = weights / jnp.sum(weights, -1, keepdims=True)
    prob_low = probs.astype(BF)
    attended = jnp.einsum("shct,shtd->schd", prob_low, all_values, preferred_element_type=F32)
    attended = attended.astype(BF).reshape(rows, width_att)

    partial = dot(attended, full_out_t, ((1,), (1,))) + dot(activated, full_down_t, ((1,), (1,)))
    branch = lax.psum(partial.astype(BF), "tensor").astype(F32)

    grad_mlp_weights = jnp.concatenate(
        [dot(input_mlp, hidden_low, ((0,), (0,))), dot(grad_low, activated, ((0,), (0,)))], 1
    ).astype(BF)
    mlp_reduced = lax.psum_scatter(
        grad_mlp_weights, fsdp, scatter_dimension=0, tiled=True
    ).astype(F32)

    grad_probs = jnp.einsum("schd,shtd->shct", grad_att, all_values, preferred_element_type=F32)
    delta = jnp.sum(probs * grad_probs, -1, keepdims=True)
    grad_scores = (probs * (grad_probs - delta)).astype(BF)
    grad_query = jnp.einsum("shct,shtd->schd", grad_scores, all_keys, preferred_element_type=F32) * scale
    key_term = jnp.einsum("shct,schd->tshd", grad_scores, queries, preferred_element_type=F32) * scale
    value_term = jnp.einsum("shct,schd->tshd", prob_low, grad_att, preferred_element_type=F32)
    terms = jnp.concatenate([key_term, value_term], -1).astype(BF)
    own_terms = lax.psum_scatter(terms, "seq", scatter_dimension=0, tiled=True).astype(F32)
    own_terms = jnp.swapaxes(own_terms, 0, 1)
    grad_key = own_terms[..., :HEAD_DIM]
    grad_value = own_terms[..., HEAD_DIM:]
    grad_project = jnp.concatenate(
        [rotate(grad_query, cosine, -sine), rotate(grad_key, cosine, -sine), grad_value], -1
    ).reshape(rows, width_qkv)
    bias_qkv_sum = jnp.sum(grad_project, 0)
    project_low = grad_project.astype(BF)

    grad_norm_attn = dot(project_low, full_qkv, ((1,), (1,)))
    grad_norm_mlp = dot(hidden_low, full_up, ((1,), (1,)))
    norm_sums = jnp.stack(
        [
            jnp.sum(grad_norm_attn * xhat, 0),
            jnp.sum(grad_norm_attn, 0),
            jnp.sum(grad_norm_mlp * xhat, 0),
            jnp.sum(grad_norm_mlp, 0),
        ]
    )
    grad_xhat = grad_norm_attn * gain_attn + grad_norm_mlp * gain_mlp
    input_part = inverse * (
        grad_xhat
        - jnp.mean(grad_xhat, -1, keepdims=True)
        - xhat * jnp.mean(grad_xhat * xhat, -1, keepdims=True)
    )
    input_part, branch = lax.optimization_barrier((input_part.astype(BF), branch))
    input_sum = lax.psum(input_part, "tensor").astype(F32)
    mixed = (token_rows + branch + b_out + b_down).astype(BF).reshape(tokens.shape)
    tokens_grad = (grad_rows + input_sum).reshape(tokens.shape)

    grad_attn_weights = jnp.concatenate(
        [dot(input_attn, project_low, ((0,), (0,))), dot(grad_low, attended, ((0,), (0,)))], 1
    ).astype(BF)
    attn_reduced = lax.psum_scatter(
        grad_attn_weights, fsdp, scatter_dimension=0, tiled=True
    ).astype(F32)

    norm_sums = lax.psum(norm_sums, "tensor").reshape(-1)
    small = lax.psum(
        jnp.concatenate([norm_sums, bias_qkv_sum, jnp.sum(grad_rows, 0), bias_up_sum]), fsdp
    )
    norm_sums = small[: 4 * D].reshape(4, D)
    small = small[4 * D :]
    bias_qkv_sum = small[:width_qkv].reshape(b_qkv.shape)
    bias_out_sum = small[width_qkv : width_qkv + D]
    bias_up_sum = small[width_qkv + D :]
    return (
        mixed,
        tokens_grad,
        norm_sums[0],
        norm_sums[1],
        norm_sums[2],
        norm_sums[3],
        attn_reduced[:, :width_qkv].reshape(w_qkv.shape),
        bias_qkv_sum,
        attn_reduced[:, width_qkv:].T,
        bias_out_sum,
        mlp_reduced[:, :units],
        bias_up_sum,
        mlp_reduced[:, units:].T,
        bias_out_sum,
    )


def exchange(array, axis, flip):
    size = lax.axis_size(axis)
    return lax.ppermute(array, axis, [(i, i ^ flip) for i in range(size)])


def after(array, *others):
    return lax.optimization_barrier((array, *others))[0]


def along_x(array):
    return exchange(array, "seq", 2)


def along_y(array):
    return exchange(array, "batch", 1)


def to_core(array):
    return exchange(array, "seq", 1)


ORDER = (0, 2, 4, 6, 1, 3, 5, 7)


def block_ins(blocks, width, column):
    return [(pl.BlockSpec((256, width), lambda j: (0, column(j))), b) for b in blocks]


def both_cores(own, by_x, by_y, far, *others):
    own_c, by_x_c, by_y_c, far_c = others
    return (own, by_y, own_c, by_y_c, by_x, far, by_x_c, far_c)


def call(body, grid, ins, outs, scratch=(), flops=0, moved=0, vmem=60, aliases={}):
    return pl.pallas_call(
        body,
        grid=grid,
        in_specs=[spec for spec, _ in ins],
        out_specs=[spec for spec, _ in outs],
        out_shape=[shape for _, shape in outs],
        scratch_shapes=list(scratch),
        input_output_aliases=aliases,
        compiler_params=pltpu.CompilerParams(vmem_limit_bytes=vmem * 1024 * 1024),
        cost_estimate=pl.CostEstimate(flops=0, bytes_accessed=0, transcendentals=0),
    )(*[array for _, array in ins])


def call_placed(body, grid, info, ins, outs, scratch=(), flops=0, moved=0, vmem=60):
    return pl.pallas_call(
        body,
        grid_spec=pltpu.PrefetchScalarGridSpec(
            num_scalar_prefetch=1,
            grid=grid,
            in_specs=[spec for spec, _ in ins],
            out_specs=[spec for spec, _ in outs],
            scratch_shapes=list(scratch),
        ),
        out_shape=[shape for _, shape in outs],
        compiler_params=pltpu.CompilerParams(vmem_limit_bytes=vmem * 1024 * 1024),
        cost_estimate=pl.CostEstimate(flops=0, bytes_accessed=0, transcendentals=0),
    )(info, *[array for _, array in ins])


def smem():
    return pl.BlockSpec(memory_space=pltpu.SMEM)


def any_place():
    return pl.BlockSpec(memory_space=pl.ANY)


def whole(array):
    dims = len(array.shape)
    return pl.BlockSpec(array.shape, lambda *_: (0,) * dims, pipeline_mode=pl.Buffered(1))


def block(shape, index):
    return pl.BlockSpec(shape, index)


def struct(shape, dtype):
    return jax.ShapeDtypeStruct(shape, dtype)


def columns(ref, info, place):
    start = pl.multiple_of((info[0] ^ place) * 256, 256)
    return ref[:, pl.ds(start, 256)]


def norm_body(info, tok, cot, gain_a, shift_a, gain_m, shift_m, in_a, in_m, grad, grad_sum):
    step = pl.program_id(0)
    t = tok[...].astype(F32)
    centered = t - jnp.mean(t, -1, keepdims=True)
    xhat = centered * lax.rsqrt(jnp.mean(centered * centered, -1, keepdims=True) + EPS)
    in_a[...] = (xhat * gain_a[...] + shift_a[...]).astype(BF)
    in_m[...] = (xhat * gain_m[...] + shift_m[...]).astype(BF)
    place = info[1] * 256 + lax.broadcasted_iota(jnp.int32, t.shape, 0)
    g = jnp.where(place < info[5 + step], cot[...].astype(F32), 0.0)
    grad[...] = g.astype(BF)

    @pl.when(step == 0)
    def _():
        grad_sum[...] = jnp.zeros_like(grad_sum)

    grad_sum[...] += jnp.sum(g, 0, keepdims=True)


def matched(x, blocks, info):
    left = jnp.concatenate([columns(x, info, r) for r in range(8)], 1)
    right = jnp.concatenate([b[...] for b in blocks], 0)
    return jnp.dot(left, right, preferred_element_type=F32)


def turn(z, cos, front, back):
    first = z[:, :128]
    first = (
        first * cos
        + pltpu.roll(first, 96, 1) * front
        + pltpu.roll(first, 32, 1) * back
    )
    return jnp.concatenate([first, z[:, 128:]], 1)


def qkv_body(info, x, bias, cos, front, back, *refs):
    blocks, (q, kv_a, kv_b) = (refs[:8], refs[8:16]), refs[16:]
    step = pl.program_id(0)
    heads = [matched(x, blocks[h], info) + bias[h : h + 1] for h in range(2)]

    def turned():
        c, f, b = (jnp.concatenate([t[...]] * 4, 0) for t in (cos, front, back))
        return jnp.concatenate([turn(z, c, f, b) for z in heads], 1).astype(BF)

    @pl.when(step == 0)
    def _():
        q[...] = turned()

    @pl.when(step == 1)
    def _():
        k = turned()
        kv_a[...] = k[:512]
        kv_b[...] = k[512:]

    @pl.when(step == 2)
    def _():
        v = jnp.concatenate(heads, 1).astype(BF)
        kv_a[...] = v[:512]
        kv_b[...] = v[512:]


def grad_att_body(info, g, *refs):
    refs[16][...] = jnp.concatenate(
        [matched(g, refs[:8], info), matched(g, refs[8:16], info)], 1
    ).astype(BF)


def up_body(info, x, bias, *refs):
    blocks, (act, slope) = refs[:8], refs[8:]
    z = matched(x, blocks, info) + bias[...]
    gelu, steep = gelu_pair(z)
    act[...] = gelu.astype(BF)
    slope[...] = steep.astype(BF)


def hidden_body(info, g, slope, *refs):
    low, total = refs[8:]
    grad = matched(g, refs[:8], info) * slope[...].astype(F32)
    low[...] = grad.astype(BF)
    total[...] = jnp.sum(grad, 0, keepdims=True)


def nt(a, b):
    return lax.dot_general(a, b, (((1,), (1,)), ((), ())), preferred_element_type=F32)


def tn(a, b):
    return lax.dot_general(a, b, (((0,), (0,)), ((), ())), preferred_element_type=F32)


def attention_body(first_seq, info, q_ref, ga_ref, cos, front, back, *refs):
    keys, values = refs[:4], refs[4:8]
    att, dq, dq_sum, keep, send = refs[8:]
    terms = (keep.at[0], send.at[0], keep.at[1], send.at[1])
    seq = pl.program_id(0)
    head = pl.program_id(1)
    scale = HEAD_DIM ** (-0.5)
    length = info[5 + first_seq + seq]
    q = q_ref[...]
    ga = ga_ref[...]
    row_place = info[1] * 256 + lax.broadcasted_iota(jnp.int32, (256, 256), 0)
    column = lax.broadcasted_iota(jnp.int32, (256, 256), 1)
    scores = []
    masks = []
    for r in range(4):
        key_place = info[1 + r] * 256 + column
        allowed = (key_place <= row_place) & (key_place < length)
        masks.append(allowed)
        scores.append(jnp.where(allowed, nt(q, keys[r][...]) * scale, FLOOR))
    top = jnp.max(jnp.maximum(jnp.maximum(scores[0], scores[1]), jnp.maximum(scores[2], scores[3])), -1, keepdims=True)
    weights = [jnp.where(m, jnp.exp(s - top), 0.0) for s, m in zip(scores, masks)]
    total = jnp.sum(weights[0] + weights[1] + weights[2] + weights[3], -1, keepdims=True)
    inverse = 1.0 / total
    probs = [w * inverse for w in weights]
    low = [p.astype(BF) for p in probs]
    out = jnp.zeros((256, 256), F32)
    for r in range(4):
        out += jnp.dot(low[r], values[r][...], preferred_element_type=F32)
    att[...] = out.astype(BF)
    grad_probs = [nt(ga, values[r][...]) for r in range(4)]
    products = [p * g for p, g in zip(probs, grad_probs)]
    delta = jnp.sum(products[0] + products[1] + products[2] + products[3], -1, keepdims=True)
    grad_q = jnp.zeros((256, 256), F32)
    key_columns = pl.ds(pl.multiple_of(head * 256, 256), 256)
    value_columns = pl.ds(pl.multiple_of(head * 256 + 512, 256), 256)
    for r in range(4):
        grad_scores = (probs[r] * (grad_probs[r] - delta)).astype(BF)
        grad_q += jnp.dot(grad_scores, keys[r][...], preferred_element_type=F32)
        terms[r][:, key_columns] = (tn(grad_scores, q) * scale).astype(BF)
        terms[r][:, value_columns] = tn(low[r], ga).astype(BF)
    grad_q = turn(grad_q * scale, cos[...], -front[...], -back[...])
    dq[...] = grad_q.astype(BF)
    dq_sum[...] = jnp.sum(grad_q, 0, keepdims=True)[None, None]


def streamed(blocks, width, column):
    return [(pl.BlockSpec((256, width), lambda i: (0, column(i))), blocks[r]) for r in ORDER]


def branch_body(info, att, act, *refs):
    w_att, w_act, outs, total = refs[:8], refs[8:16], refs[16:18], refs[18]
    step = pl.program_id(0)

    def part(i):
        return nt(att[...], w_att[i][...]) + nt(act[...], w_act[i][...])

    @pl.when(step == 0)
    def _():
        for i in range(8):
            total[:, i * 256 : (i + 1) * 256] = part(i)

    @pl.when(step == 1)
    def _():
        for i, r in enumerate(ORDER):
            there = pl.ds(pl.multiple_of((info[0] ^ r) * 256, 256), 256)
            done = (total[:, i * 256 : (i + 1) * 256] + part(i)).astype(BF)
            outs[0][:, there] = done[:256]
            outs[1][:, there] = done[256:]


def weight_part(refs):
    products = [tn(refs[i][...], refs[i + 1][...]) for i in range(0, len(refs), 2)]
    return products[0] if len(products) == 1 else jnp.concatenate(products, 1)


def weight_send_body(info, *refs):
    refs[-1][...] = weight_part(refs[:-1]).astype(BF)


def weight_add_body(info, *refs):
    received, over_x, over_y, next_y, next_x, own = refs[-6:]
    step = pl.program_id(0)
    part = (weight_part(refs[:-6]) + received[...].astype(F32)).astype(BF)
    left, right = part[:, :1024], part[:, 1024:]

    @pl.when(step == 0)
    def _():
        over_x[...] = left
        next_x[...] = right

    @pl.when(step == 1)
    def _():
        over_x[...] = left
        over_y[...] = right

    @pl.when(step == 2)
    def _():
        next_y[...] = left
        over_y[...] = right

    @pl.when(step == 3)
    def _():
        own[...] = part


class Scatter:
    def __init__(self, pairs):
        self.pairs = pairs

    def operands(self, flip):
        def index(i, info):
            place = jnp.where(i == 0, 4, jnp.where(i == 1, 5, jnp.where(i == 2, 1, 0)))
            return 0, info[0] ^ place ^ flip

        fixed = lambda array: pl.BlockSpec(array.shape, lambda i, info: (0, 0), pipeline_mode=pl.Buffered(1))
        return [
            operand
            for x, h in self.pairs
            for operand in ((block((1024, 256), index), x), (fixed(h), h))
        ]

    def send(self, info):
        self.sent = call_placed(
            weight_send_body,
            (4,),
            info,
            self.operands(2),
            [(block((256, 2048), lambda i, info: (i, 0)), struct((1024, 2048), BF))],
        )[0]
        return self.sent

    def add(self, info, received):
        clip = lambda first: lambda i, info: (jnp.clip(i - first, 0, 1), 0)
        fixed = lambda width: (block((256, width), lambda i, info: (0, 0)), struct((256, width), BF))
        tall = lambda first: (block((256, 1024), clip(first)), struct((512, 1024), BF))
        made = call_placed(
            weight_add_body,
            (4,),
            info,
            self.operands(0) + [(block((256, 2048), lambda i, info: (i, 0)), received)],
            [tall(0), tall(1), fixed(1024), fixed(1024), fixed(2048)],
        )
        self.over_x, self.over_y, self.next_y, self.next_x, self.own = made
        return self.own

    def first(self, done):
        self.from_x = along_x(after(self.over_x, done))
        self.from_y = along_y(after(self.over_y, done))
        return self.from_x, self.from_y

    def second(self, done):
        self.last_y = along_y(plus(after(self.next_y, done), self.from_x[256:]))
        self.last_x = along_x(plus(after(self.next_x, done), self.from_y[:256]))
        return self.last_y, self.last_x

    def total(self, info, turned=False):
        tall = lambda array, row: (block((256, 1024), lambda i: (row, 0)), array)
        shape = (2048, 256) if turned else (256, 2048)
        return call(
            total_turned_body if turned else total_body,
            (1,),
            [
                (smem(), info),
                (whole(self.own), self.own),
                tall(self.from_x, 0),
                tall(self.last_y, 0),
                tall(self.from_y, 1),
                tall(self.last_x, 0),
            ],
            [(block(shape, lambda i: (0, 0)), struct(shape, F32))],
        )[0]


def total_of(own, from_x, last_y, from_y, last_x):
    left = from_x[...].astype(F32) + last_y[...].astype(F32)
    right = from_y[...].astype(F32) + last_x[...].astype(F32)
    return own[...].astype(F32) + jnp.concatenate([left, right], 1)


def total_body(info, *refs):
    refs[-1][...] = total_of(*refs[:-1])


def total_turned_body(info, *refs):
    refs[-1][...] = total_of(*refs[:-1]).T


def project_body(info, q, own, core, far, cos, front, back, low, kv_sum):
    c, f, b = (jnp.concatenate([t[...]] * 2, 0) for t in (cos, front, back))
    for head in range(2):
        mine = slice(head * 256, head * 256 + 256)
        low[:, head * 768 : head * 768 + 256] = q[:, mine]
        for kind in range(2):
            cut = slice(kind * 512 + head * 256, kind * 512 + head * 256 + 256)
            grad = own[:, cut].astype(F32) + core[:, cut].astype(F32) + far[:, cut].astype(F32)
            if kind == 0:
                grad = turn(grad, c, -f, -b)
            kv_sum[:, head * 512 + kind * 256 : head * 512 + kind * 256 + 256] = jnp.sum(grad, 0, keepdims=True)
            start = head * 768 + 256 + kind * 256
            low[:, start : start + 256] = grad.astype(BF)


def input_body(info, low, hid, tok, gain_a, gain_m, *refs):
    w_qkv, w_up, parts, sums, (gx, xh, inv) = refs[:8], refs[8:16], refs[16:18], refs[18], refs[19:]
    step = pl.program_id(0)

    def products(first):
        for i, r in enumerate(ORDER):
            there = pl.ds(pl.multiple_of((info[0] ^ r) * 256, 256), 256)
            from_attn = nt(low[...], w_qkv[i][:, :768])
            from_mlp = nt(hid[...], w_up[i][...])
            xhat = xh[:, there]
            columns_sums = [from_attn * xhat, from_attn, from_mlp * xhat, from_mlp]
            grad = from_attn * gain_a[:, there] + from_mlp * gain_m[:, there]
            for row, values in enumerate(columns_sums):
                added = jnp.sum(values, 0, keepdims=True)
                sums[row : row + 1, there] = added if first else sums[row : row + 1, there] + added
            gx[:, there] = grad if first else gx[:, there] + grad

    @pl.when(step == 0)
    def _():
        t = tok[...].astype(F32)
        centered = t - jnp.mean(t, -1, keepdims=True)
        inverse = lax.rsqrt(jnp.mean(centered * centered, -1, keepdims=True) + EPS)
        xh[...] = centered * inverse
        inv[...] = jnp.broadcast_to(inverse, inv.shape)
        products(True)

    @pl.when(step == 1)
    def _():
        products(False)
        grad = gx[...]
        xhat = xh[...]
        mean = jnp.mean(grad, -1, keepdims=True)
        along = jnp.mean(grad * xhat, -1, keepdims=True)
        out = (inv[:, :1] * (grad - mean - xhat * along)).astype(BF)
        parts[0][...] = out[:256]
        parts[1][...] = out[256:]


def plus(a, b):
    return (a.astype(F32) + b.astype(F32)).astype(BF)


def bar(*arrays):
    return lax.optimization_barrier(arrays)


def finish_body(own, from_x, last_y, from_y, last_x, qkv, out):
    total = total_of(own, from_x, last_y, from_y, last_x)
    for head in range(2):
        qkv[:, head, :] = total[:, head * 768 : head * 768 + 768]
    out[...] = total[:, 1536:].T


class Hops:
    def __init__(self, info, tok, grad, bias):
        self.info = info
        self.given = (tok, grad, bias)
        self.mine = {}
        self.ready = {}
        self.pair = None
        self.out = [None, None]

    def start(self, block):
        self.leaving = self.mine[0] = block
        return [exchange(block, "tensor", 1)]

    def land(self, j, arrived, next_block=None):
        half = lambda array: (block((128, D), lambda i: (i, 0)), array)
        fresh = (block((128, D), lambda i: (i, 0)), struct((256, D), BF))
        parts, ins, outs = [], [(smem(), self.info)], []
        if j >= 2:
            self.ready[j - 2] = (self.leaving, arrived[0])
        if j < 8:
            parts.append("pair")
            ins += [half(self.mine[j]), half(arrived[0])]
            outs.append(fresh)
        if 1 <= j <= 8:
            parts.append("sum" if next_block is None else "either")
            ins += [half(self.pair), half(arrived[1])]
            if next_block is not None:
                ins.append(half(next_block))
            outs.append(fresh)
        made = list(call(lambda *refs: land_body(parts, *refs), (2,), ins, outs))
        done = made[0]
        if next_block is not None:
            self.mine[j + 1] = next_block
        pair = made.pop(0) if j < 8 else None
        self.leaving = made.pop(0) if j else after(next_block, pair)
        flying = [exchange(self.leaving, "tensor", 1)]
        if pair is not None:
            self.pair = pair
            flying.append(lax.ppermute(pair, "tensor", [(1, 2), (2, 1)]))
        return flying, done

    def write(self, k, before):
        tok, grad, bias = self.given
        which, place = divmod(k, 4)
        half = lambda array: (block((128, D), lambda i: (i, 0)), array)
        kept = (block((128, D), lambda i: (2 * place + i, 0)), (tok, grad)[which])
        ins = [(smem(), after(self.info, before))] + [half(array) for array in self.ready[k]] + [kept]
        if not which:
            ins.append((whole(bias), bias))
        aliases = {}
        if self.out[which] is not None:
            aliases[len(ins)] = 0
            ins.append((any_place(), self.out[which]))
        made = call(
            (mixed_body, tokens_grad_body)[which],
            (2,),
            ins,
            [(kept[0], struct((1024, D), (BF, F32)[which]))],
            aliases=aliases,
        )[0]
        self.out[which] = made
        return made


def land_body(parts, info, *refs):
    refs = list(refs)
    outs = refs[-len(parts) :]
    for part, out in zip(parts, outs):
        a, b = refs.pop(0), refs.pop(0)
        summed = (a[...].astype(F32) + b[...].astype(F32)).astype(BF)
        out[...] = jnp.where(info[9] > 0, summed, refs.pop(0)[...]) if part == "either" else summed


def tokens_grad_body(info, total, came, grad, *refs):
    refs[-1][...] = jnp.where(info[9] > 0, total[...], came[...]).astype(F32) + grad[...].astype(F32)


def mixed_body(info, total, came, tok, bias, *refs):
    summed = jnp.where(info[9] > 0, total[...], came[...]).astype(F32) + tok[...].astype(F32)
    refs[-1][...] = (summed + bias[...]).astype(BF)


def per_device_links(
    tokens,
    cotangent,
    lengths,
    block_slot,
    gain_attn,
    shift_attn,
    gain_mlp,
    shift_mlp,
    w_qkv,
    b_qkv,
    w_out,
    b_out,
    w_up,
    b_up,
    w_down,
    b_down,
):
    rows = 1024
    seq_id = lax.axis_index("seq")
    slots = [jnp.sum(jnp.where(jnp.arange(4) == (seq_id ^ r), block_slot, 0)) for r in range(4)]
    tensor_id = lax.axis_index("tensor")
    inner = ((tensor_id == 1) | (tensor_id == 2)).astype(jnp.int32)
    me = seq_id * 2 + lax.axis_index("batch")
    info = jnp.concatenate([jnp.stack([me, *slots]), lengths, inner.reshape(1)]).astype(jnp.int32)
    tok = tokens.reshape(rows, D)
    cot = cotangent.reshape(rows, D)
    cosine, sine = rotation(slots[0] * 256 + jnp.arange(256, dtype=jnp.int32))
    cosine, sine = cosine[:, 0], sine[:, 0]
    zero = jnp.zeros_like(sine)
    cos_t = jnp.concatenate([cosine, cosine, zero + 1.0, zero + 1.0], 1)
    front_t = jnp.concatenate([-sine, zero, zero, zero], 1)
    back_t = jnp.concatenate([zero, sine, zero, zero], 1)
    tables = [(whole(t), t) for t in (cos_t, front_t, back_t)]
    gains = [v.reshape(1, D) for v in (gain_attn, shift_attn, gain_mlp, shift_mlp)]

    def info_in(*tokens_before):
        return (smem(), after(info, *tokens_before) if tokens_before else info)

    row_block = lambda n: block((256, n), lambda i: (i, 0))
    row_struct = lambda n, kind=BF: struct((rows, n), kind)
    tall = lambda n, index: block((256, n), index)

    head_own = jnp.concatenate(
        [w for h in range(2) for w in (w_qkv[:, h], w_out[h * 256 : (h + 1) * 256].T)], 1
    )
    head_x, head_y = along_x(head_own), along_y(head_own)
    head_c = to_core(head_own)
    in_a, in_m, grad_low, grad_sum = call(
        norm_body,
        (4,),
        [info_in(), (row_block(D), tok), (row_block(D), cot)] + [(whole(v), v) for v in gains],
        [(row_block(D), row_struct(D))] * 3 + [(block((1, D), lambda i: (0, 0)), struct((1, D), F32))],
        moved=5 * rows * D * 2,
    )
    down_own = w_down.T
    head_x, head_y, head_c, in_a, in_m, grad_low, down_own = bar(
        head_x, head_y, head_c, in_a, in_m, grad_low, down_own
    )

    far_y, far_x = along_y(head_x[:128]), along_x(head_y[128:])
    others = [head_c, to_core(head_x), to_core(head_y)]
    far_y, far_x, up_own, *others = bar(far_y, far_x, w_up, *others)

    up_x, up_y = along_x(up_own), along_y(up_own)
    far = jnp.concatenate([far_y, far_x], 0)
    heads = both_cores(head_own, head_x, head_y, far, *others, to_core(far))
    bias = jnp.swapaxes(b_qkv.reshape(2, 3, 256), 0, 1)
    q, kv_a, kv_b = call(
        lambda info, x, bias, *refs: qkv_body(info, x, bias.at[0], *refs),
        (3,),
        [info_in(), (whole(in_a), in_a), (block((1, 2, 256), lambda j: (j, 0, 0)), bias)]
        + tables
        + block_ins(heads, 256, lambda j: j)
        + block_ins(heads, 256, lambda j: j + 4),
        [
            (block((rows, 512), lambda j: (0, 0)), row_struct(512)),
            (block((512, 512), lambda j: (0, jnp.maximum(j - 1, 0))), struct((512, 1024), BF)),
            (block((512, 512), lambda j: (0, jnp.maximum(j - 1, 0))), struct((512, 1024), BF)),
        ],
        flops=2 * rows * D * 1536,
        moved=2 * (rows * D + D * 1536 + rows * 1536),
    )
    kv_x = along_x(kv_a)
    grad_att = call(
        grad_att_body,
        (1,),
        [info_in(q), (whole(grad_low), grad_low)]
        + block_ins(heads, 256, lambda j: 3)
        + block_ins(heads, 256, lambda j: 7),
        [(block((rows, 512), lambda j: (0, 0)), row_struct(512))],
        flops=2 * rows * D * 512,
        moved=2 * (rows * D + D * 512 + rows * 512),
    )[0]
    up_c = to_core(after(up_own, q))
    up_x, up_y, up_c, grad_att = bar(up_x, up_y, up_c, grad_att)

    up_far = along_y(up_x)
    others = [up_c, to_core(up_x), to_core(up_y)]
    down_own = after(down_own, *others)
    down_x, down_y = along_x(down_own), along_y(down_own)
    up_far, kv_x, kv_a, *others = bar(up_far, kv_x, kv_a, *others)
    ups = both_cores(up_own, up_x, up_y, up_far, *others, to_core(up_far))

    def kv_refs(own, by_x):
        both = to_core(jnp.concatenate([own, by_x], 0))
        return [(own, 0), (both, 0), (by_x, 0), (both, 2)]

    kv = [kv_refs(kv_a, kv_x)]
    act, slope = call(
        up_body,
        (4,),
        [info_in(grad_att), (whole(in_m), in_m), (block((1, 512), lambda j: (0, j)), b_up.reshape(1, -1))]
        + block_ins(ups, 512, lambda j: j),
        [(block((rows, 512), lambda j: (0, j)), row_struct(2048))] * 2,
        flops=2 * rows * D * 2048,
        moved=2 * (rows * D + D * 2048 + 2 * rows * 2048),
    )
    down_c = to_core(after(down_own, ups[7]))
    down_x, down_y, down_c, act, slope = bar(down_x, down_y, down_c, act, slope)

    def attention(part, *before):
        base = part * 2
        spot = lambda offset: block((256, 256), lambda s, h: (s + base, h + offset))
        local = lambda offset, row=0: block((256, 256), lambda s, h: (s + row, h + offset))
        return call(
            lambda *refs: attention_body(base, *refs),
            (2, 2),
            [info_in(*before), (spot(0), q), (spot(0), grad_att)]
            + tables
            + [(local(0, row), b) for b, row in kv[part]]
            + [(local(2, row), b) for b, row in kv[part]],
            [
                (local(0), struct((512, 512), BF)),
                (local(0), struct((512, 512), BF)),
                (block((1, 1, 1, 256), lambda s, h: (s, h, 0, 0)), struct((2, 2, 1, 256), F32)),
            ]
            + [(block((2, 256, 1024), lambda s, h: (0, s, 0)), struct((2, 512, 1024), BF))] * 2,
            flops=4 * 6 * 2 * 256 * 1024 * 256,
            moved=4 * 2 * 256 * 256 * 24,
        )

    def branch(part, att, *before):
        return call(
            branch_body,
            (2,),
            [
                info_in(*before),
                (block((512, 256), lambda i: (0, i)), att),
                (block((512, 1024), lambda i: (part, i)), act),
            ]
            + streamed(heads, 256, lambda i: 3 + 4 * i)
            + streamed(downs, 1024, lambda i: i),
            [(block((256, D), lambda i: (0, 0)), struct((256, D), BF))] * 2,
            scratch=[pltpu.VMEM((512, D), F32)],
            flops=2 * 512 * D * 2560,
            moved=2 * (512 * 2560 + D * 2560 + 512 * D),
        )

    far_y, far_x = along_y(down_x[:128]), along_x(down_y[128:])
    others = [down_c, to_core(down_x), to_core(down_y)]
    att_a, dq_a, dq_sum_a, keep_a, send_a = attention(0, down_x)
    far_y, far_x, att_a, kv_b, send_a, *others = bar(far_y, far_x, att_a, kv_b, send_a, *others)

    far = jnp.concatenate([far_y, far_x], 0)
    downs = both_cores(down_own, down_x, down_y, far, *others, to_core(far))
    kv_x = along_x(kv_b)
    received_a = to_core(send_a)
    branch_a = branch(0, att_a)
    received_a, *branch_a = bar(received_a, *branch_a)

    hops = Hops(info, tok, grad_low, (b_out + b_down).reshape(1, D))

    def hidden_call(before):
        return call(
            hidden_body,
            (4,),
            [info_in(before), (whole(grad_low), grad_low), (block((rows, 512), lambda j: (0, j)), slope)]
            + block_ins(downs, 512, lambda j: j),
            [
                (block((rows, 512), lambda j: (0, j)), row_struct(2048)),
                (block((1, 512), lambda j: (0, j)), struct((1, 2048), F32)),
            ],
            flops=2 * rows * D * 2048,
            moved=2 * (rows * D + D * 2048 + 2 * rows * 2048),
        )

    def project(dq, keep, came, far, before):
        return call(
            project_body,
            (1,),
            [info_in(before), (whole(dq), dq)]
            + [(pl.BlockSpec((None, 512, 1024), lambda i: (0, 0, 0)), t) for t in (keep, came)]
            + [(whole(far), far)]
            + tables,
            [
                (block((512, 1536), lambda i: (0, 0)), struct((512, 1536), BF)),
                (block((1, 1024), lambda i: (0, 0)), struct((1, 1024), F32)),
            ],
            moved=2 * 512 * 5000,
        )

    def input_part(half, low, before):
        return call(
            input_body,
            (2,),
            [
                info_in(before),
                (block((512, 768), lambda i: (0, i)), low),
                (block((512, 1024), lambda i: (half, i)), hidden_low),
                (pl.BlockSpec((512, D), lambda i: (half, 0), pipeline_mode=pl.Buffered(1)), tok),
            ]
            + [(whole(t), t) for t in (gains[0], gains[2])]
            + streamed(heads, 1024, lambda i: i)
            + streamed(ups, 1024, lambda i: i),
            [(block((256, D), lambda i: (0, 0)), struct((256, D), BF))] * 2
            + [(block((8, D), lambda i: (0, 0)), struct((8, D), F32))],
            scratch=[pltpu.VMEM((512, D), F32), pltpu.VMEM((512, D), F32), pltpu.VMEM((512, 128), F32)],
            flops=2 * 512 * D * 3584,
            moved=2 * (512 * 6000 + D * 3584),
        )

    flown = hops.start(branch_a[0])
    far_a = along_x(plus(keep_a[1], received_a[1]))
    hidden_low, b_up_sum = hidden_call(branch_a[0])
    down = Scatter([(grad_low, act)])
    down_sent = down.send(after(info, hidden_low))
    flown, far_a, kv_x, down_sent = bar(flown, far_a, kv_x, down_sent)

    flown, done = hops.land(0, flown, branch_a[1])
    kv.append(kv_refs(kv_b, after(kv_x, done)))
    down_received = to_core(after(down_sent, done))
    att_b, dq_b, dq_sum_b, keep_b, send_b = attention(1, done)
    branch_b = branch(1, att_b, att_b)
    flown, down_received, send_b, *branch_b = bar(flown, down_received, send_b, *branch_b)

    flown, done = hops.land(1, flown, branch_b[0])
    received_b = to_core(after(send_b, done))
    low_a, kv_sum_a = project(dq_a, keep_a, received_a, far_a, done)
    first, second, norm_sum_a = input_part(0, low_a, low_a)
    flown, received_b, first, second = bar(flown, received_b, first, second)

    flown, done = hops.land(2, flown, branch_b[1])
    far_b = along_x(plus(after(keep_b[1], done), received_b[1]))
    token = down.add(after(info, done), down_received)
    up = Scatter([(in_m, hidden_low)])
    up_sent = up.send(after(info, token))
    flown, far_b, up_sent = bar(flown, far_b, up_sent)

    flown, done = hops.land(3, flown, first)
    down_first = down.first(done)
    up_received = to_core(after(up_sent, done))
    low_b, kv_sum_b = project(dq_b, keep_b, received_b, far_b, done)
    third, fourth, norm_sum_b = input_part(1, low_b, low_b)
    q_sums = (dq_sum_a + dq_sum_b).sum(0).reshape(2, 1, 256)
    kv_total = (kv_sum_a + kv_sum_b).reshape(2, 2, 256)
    bias_qkv = jnp.concatenate([q_sums, kv_total], 1).reshape(-1)
    norm_sums = (norm_sum_a + norm_sum_b)[:4].reshape(-1)
    small = jnp.concatenate([norm_sums, bias_qkv, grad_sum[0], b_up_sum[0]]).reshape(-1, 128)
    flown, (down.from_x, down.from_y), up_received, third, fourth, small = bar(
        flown, down_first, up_received, third, fourth, small
    )

    flown, done = hops.land(4, flown, second)
    small_c = to_core(after(small, done))
    down_second = down.second(done)
    token = up.add(after(info, done), up_received)
    hops.write(0, token)
    project_low = jnp.concatenate([after(low_a, token), low_b], 0)
    attended = jnp.concatenate([after(att_a, token), att_b], 0)
    flown, (down.last_y, down.last_x), small_c, project_low, attended = bar(
        flown, down_second, small_c, project_low, attended
    )

    flown, done = hops.land(5, flown, third)
    up_first = up.first(done)
    attn = Scatter([(in_a, project_low), (grad_low, attended)])
    attn_sent = attn.send(after(info, done))
    small = after(small, attn_sent) + small_c
    norms = small[:64]
    norms_z = exchange(norms, "tensor", 1)
    written = hops.write(1, attn_sent)
    flown, (up.from_x, up.from_y), attn_sent, norms_z, hops.out[0] = bar(
        flown, up_first, attn_sent, norms_z, written
    )

    flown, done = hops.land(6, flown, fourth)
    attn_received = to_core(after(attn_sent, done))
    up_second = up.second(done)
    norms = after(norms, done) + norms_z
    written = hops.write(2, done)
    token = attn.add(after(info, written), attn_received)
    down_grad = down.total(after(info, token), True)
    flown, (up.last_y, up.last_x), norms, down_grad = bar(flown, up_second, norms, down_grad)

    flown, done = hops.land(7, flown)
    attn_first = attn.first(done)
    norms_z = exchange(after(norms, done), "tensor", 2)
    written = hops.write(3, done)
    written = hops.write(4, written)
    written = hops.write(5, written)
    up_grad = up.total(after(info, written))
    flown, (attn.from_x, attn.from_y), norms_z, up_grad, hops.out[1] = bar(
        flown, attn_first, norms_z, up_grad, hops.out[1]
    )

    flown, done = hops.land(8, flown)
    attn_second = attn.second(done)
    written = hops.write(6, done)
    small = jnp.concatenate([after(norms, written) + norms_z, small[64:]], 0)
    small = small + along_y(small)
    small = small + along_x(small)
    hops.ready[7] = (hops.leaving, flown[0])
    (leaving, came), (attn.last_y, attn.last_x), hops.out[1] = bar(hops.ready[7], attn_second, hops.out[1])
    hops.ready[7] = (leaving, came)
    hops.write(7, came)
    mixed, tokens_grad = hops.out

    norms = small[:64].reshape(4, D)
    small = small[64:].reshape(-1)
    bias_out = small[1536 : 1536 + D]

    tall = lambda array, row: (block((256, 1024), lambda i: (row, 0)), array)
    qkv_grad, out_grad = call(
        finish_body,
        (1,),
        [
            (whole(attn.own), attn.own),
            tall(attn.from_x, 0),
            tall(attn.last_y, 0),
            tall(attn.from_y, 1),
            tall(attn.last_x, 0),
        ],
        [
            (block((256, 2, 768), lambda i: (0, 0, 0)), struct((256, 2, 768), F32)),
            (block((512, 256), lambda i: (0, 0)), struct((512, 256), F32)),
        ],
    )
    return (
        mixed.reshape(tokens.shape),
        tokens_grad.reshape(tokens.shape),
        norms[0],
        norms[1],
        norms[2],
        norms[3],
        qkv_grad,
        small[:1536].reshape(b_qkv.shape),
        out_grad,
        bias_out,
        up_grad,
        small[1536 + D :],
        down_grad,
        bias_out,
    )


def solution(mesh):
    in_specs = (
        P("batch", "seq", None),
        P("batch", "seq", None),
        P("batch"),
        P(),
        P(),
        P(),
        P(),
        P(),
        P(("seq", "batch"), "tensor", None),
        P("tensor", None),
        P("tensor", ("seq", "batch")),
        P(),
        P(("seq", "batch"), "tensor"),
        P("tensor"),
        P("tensor", ("seq", "batch")),
        P(),
    )
    out_specs = (
        P("batch", "seq", None),
        P("batch", "seq", None),
        P(),
        P(),
        P(),
        P(),
        P(("seq", "batch"), "tensor", None),
        P("tensor", None),
        P("tensor", ("seq", "batch")),
        P(),
        P(("seq", "batch"), "tensor"),
        P("tensor"),
        P("tensor", ("seq", "batch")),
        P(),
    )
    links = tuple(mesh.shape[axis] for axis in ("seq", "batch", "tensor"))
    per_device = per_device_links if links == (4, 2, 4) else per_device_any
    return jax.shard_map(
        per_device, mesh=mesh, in_specs=in_specs, out_specs=out_specs, check_vma=False
    )
```

```python
import jax
import jax.numpy as jnp
from jax import lax
from jax.experimental import pallas as pl
from jax.experimental.pallas import tpu as pltpu
from jax.sharding import PartitionSpec as P

D = 2048
HEAD_DIM = 256
ROT = 64
EPS = 1e-05
FLOOR = -1e30
BF = jnp.bfloat16
F32 = jnp.float32


def dot(a, b, dims):
    return lax.dot_general(a, b, (dims, ((), ())), preferred_element_type=F32)


def rotation(places):
    half_rot = ROT // 2
    frequency = 10000.0 ** (jnp.arange(half_rot, dtype=F32) * (-2.0 / ROT))
    angles = places.astype(F32)[:, None] * frequency[None, :]
    return jnp.cos(angles)[:, None, :], jnp.sin(angles)[:, None, :]


def rotate(field, cosine, sine):
    half_rot = ROT // 2
    front = field[..., :half_rot]
    back = field[..., half_rot:ROT]
    return jnp.concatenate(
        [front * cosine - back * sine, back * cosine + front * sine, field[..., ROT:]], -1
    )


def gelu_pair(z):
    phi_cdf = 0.5 * (1.0 + lax.erf(z * 0.7071067811865476))
    density = 0.3989422804014327 * jnp.exp(-0.5 * z * z)
    return z * phi_cdf, phi_cdf + z * density


def per_device_any(
    tokens,
    cotangent,
    lengths,
    block_slot,
    gain_attn,
    shift_attn,
    gain_mlp,
    shift_mlp,
    w_qkv,
    b_qkv,
    w_out,
    b_out,
    w_up,
    b_up,
    w_down,
    b_down,
):
    seqs, block_rows, _ = tokens.shape
    rows = seqs * block_rows
    shard = w_qkv.shape[0]
    heads = w_qkv.shape[1]
    width_qkv = heads * 3 * HEAD_DIM
    width_att = heads * HEAD_DIM
    units = w_up.shape[1]
    fsdp = ("seq", "batch")
    scale = HEAD_DIM ** (-0.5)
    seq_count = lax.axis_size("seq")
    device_ids = jnp.arange(seq_count, dtype=jnp.int32)
    own_slot = jnp.sum(jnp.where(device_ids == lax.axis_index("seq"), block_slot, 0))
    offsets = jnp.arange(block_rows, dtype=jnp.int32)
    query_places = own_slot * block_rows + offsets
    key_places = (block_slot[:, None] * block_rows + offsets[None, :]).reshape(-1)

    attn_shard = jnp.concatenate([w_qkv.reshape(shard, width_qkv), w_out.T], 1)
    mlp_shard = jnp.concatenate([w_up, w_down.T], 1)
    attn_full = lax.all_gather(attn_shard, fsdp, axis=0, tiled=True)
    mlp_full = lax.all_gather(mlp_shard, fsdp, axis=0, tiled=True)
    full_qkv = attn_full[:, :width_qkv]
    full_out_t = attn_full[:, width_qkv:]
    full_up = mlp_full[:, :units]
    full_down_t = mlp_full[:, units:]

    token_rows = tokens.astype(F32).reshape(rows, D)
    centered = token_rows - jnp.mean(token_rows, -1, keepdims=True)
    inverse = lax.rsqrt(jnp.mean(jnp.square(centered), -1, keepdims=True) + EPS)
    xhat = centered * inverse
    input_attn = (xhat * gain_attn + shift_attn).astype(BF)
    input_mlp = (xhat * gain_mlp + shift_mlp).astype(BF)

    valid = (query_places[None, :] < lengths[:, None]).astype(F32)
    grad_rows = (cotangent.astype(F32) * valid[..., None]).reshape(rows, D)
    grad_low = grad_rows.astype(BF)

    project = dot(input_attn, full_qkv, ((1,), (0,))).reshape(
        seqs, block_rows, heads, 3 * HEAD_DIM
    ) + b_qkv
    cosine, sine = rotation(query_places)
    queries = rotate(project[..., :HEAD_DIM], cosine, sine).astype(BF)
    keys = rotate(project[..., HEAD_DIM : 2 * HEAD_DIM], cosine, sine).astype(BF)
    values = project[..., 2 * HEAD_DIM :].astype(BF)
    pair = jnp.concatenate([keys, values], -1)
    gathered = lax.all_gather(pair, "seq", axis=0, tiled=False)
    gathered = jnp.transpose(gathered, (1, 3, 0, 2, 4)).reshape(
        seqs, heads, seq_count * block_rows, 2 * HEAD_DIM
    )
    all_keys = gathered[..., :HEAD_DIM]
    all_values = gathered[..., HEAD_DIM:]

    hidden_pre = dot(input_mlp, full_up, ((1,), (0,))) + b_up
    gelu, slope = gelu_pair(hidden_pre)
    activated = gelu.astype(BF)
    grad_hidden = dot(grad_low, full_down_t, ((1,), (0,))) * slope
    hidden_low = grad_hidden.astype(BF)
    bias_up_sum = jnp.sum(grad_hidden, 0)

    grad_att = dot(grad_low, full_out_t, ((1,), (0,))).reshape(
        seqs, block_rows, heads, HEAD_DIM
    ).astype(BF)

    causal = key_places[None, None, :] <= query_places[None, :, None]
    inside = key_places[None, None, :] < lengths[:, None, None]
    mask = (causal & inside)[:, None]
    scores = jnp.einsum("schd,shtd->shct", queries, all_keys, preferred_element_type=F32) * scale
    scores = jnp.where(mask, scores, FLOOR)
    top = jnp.max(scores, -1, keepdims=True)
    weights = jnp.where(mask, jnp.exp(scores - top), 0.0)
    probs = weights / jnp.sum(weights, -1, keepdims=True)
    prob_low = probs.astype(BF)
    attended = jnp.einsum("shct,shtd->schd", prob_low, all_values, preferred_element_type=F32)
    attended = attended.astype(BF).reshape(rows, width_att)

    partial = dot(attended, full_out_t, ((1,), (1,))) + dot(activated, full_down_t, ((1,), (1,)))
    branch = lax.psum(partial.astype(BF), "tensor").astype(F32)

    grad_mlp_weights = jnp.concatenate(
        [dot(input_mlp, hidden_low, ((0,), (0,))), dot(grad_low, activated, ((0,), (0,)))], 1
    ).astype(BF)
    mlp_reduced = lax.psum_scatter(
        grad_mlp_weights, fsdp, scatter_dimension=0, tiled=True
    ).astype(F32)

    grad_probs = jnp.einsum("schd,shtd->shct", grad_att, all_values, preferred_element_type=F32)
    delta = jnp.sum(probs * grad_probs, -1, keepdims=True)
    grad_scores = (probs * (grad_probs - delta)).astype(BF)
    grad_query = jnp.einsum("shct,shtd->schd", grad_scores, all_keys, preferred_element_type=F32) * scale
    key_term = jnp.einsum("shct,schd->tshd", grad_scores, queries, preferred_element_type=F32) * scale
    value_term = jnp.einsum("shct,schd->tshd", prob_low, grad_att, preferred_element_type=F32)
    terms = jnp.concatenate([key_term, value_term], -1).astype(BF)
    own_terms = lax.psum_scatter(terms, "seq", scatter_dimension=0, tiled=True).astype(F32)
    own_terms = jnp.swapaxes(own_terms, 0, 1)
    grad_key = own_terms[..., :HEAD_DIM]
    grad_value = own_terms[..., HEAD_DIM:]
    grad_project = jnp.concatenate(
        [rotate(grad_query, cosine, -sine), rotate(grad_key, cosine, -sine), grad_value], -1
    ).reshape(rows, width_qkv)
    bias_qkv_sum = jnp.sum(grad_project, 0)
    project_low = grad_project.astype(BF)

    grad_norm_attn = dot(project_low, full_qkv, ((1,), (1,)))
    grad_norm_mlp = dot(hidden_low, full_up, ((1,), (1,)))
    norm_sums = jnp.stack(
        [
            jnp.sum(grad_norm_attn * xhat, 0),
            jnp.sum(grad_norm_attn, 0),
            jnp.sum(grad_norm_mlp * xhat, 0),
            jnp.sum(grad_norm_mlp, 0),
        ]
    )
    grad_xhat = grad_norm_attn * gain_attn + grad_norm_mlp * gain_mlp
    input_part = inverse * (
        grad_xhat
        - jnp.mean(grad_xhat, -1, keepdims=True)
        - xhat * jnp.mean(grad_xhat * xhat, -1, keepdims=True)
    )
    input_part, branch = lax.optimization_barrier((input_part.astype(BF), branch))
    input_sum = lax.psum(input_part, "tensor").astype(F32)
    mixed = (token_rows + branch + b_out + b_down).astype(BF).reshape(tokens.shape)
    tokens_grad = (grad_rows + input_sum).reshape(tokens.shape)

    grad_attn_weights = jnp.concatenate(
        [dot(input_attn, project_low, ((0,), (0,))), dot(grad_low, attended, ((0,), (0,)))], 1
    ).astype(BF)
    attn_reduced = lax.psum_scatter(
        grad_attn_weights, fsdp, scatter_dimension=0, tiled=True
    ).astype(F32)

    norm_sums = lax.psum(norm_sums, "tensor").reshape(-1)
    small = lax.psum(
        jnp.concatenate([norm_sums, bias_qkv_sum, jnp.sum(grad_rows, 0), bias_up_sum]), fsdp
    )
    norm_sums = small[: 4 * D].reshape(4, D)
    small = small[4 * D :]
    bias_qkv_sum = small[:width_qkv].reshape(b_qkv.shape)
    bias_out_sum = small[width_qkv : width_qkv + D]
    bias_up_sum = small[width_qkv + D :]
    return (
        mixed,
        tokens_grad,
        norm_sums[0],
        norm_sums[1],
        norm_sums[2],
        norm_sums[3],
        attn_reduced[:, :width_qkv].reshape(w_qkv.shape),
        bias_qkv_sum,
        attn_reduced[:, width_qkv:].T,
        bias_out_sum,
        mlp_reduced[:, :units],
        bias_up_sum,
        mlp_reduced[:, units:].T,
        bias_out_sum,
    )


def exchange(array, axis, flip):
    size = lax.axis_size(axis)
    return lax.ppermute(array, axis, [(i, i ^ flip) for i in range(size)])


def after(array, *others):
    return lax.optimization_barrier((array, *others))[0]


def along_x(array):
    return exchange(array, "seq", 2)


def along_y(array):
    return exchange(array, "batch", 1)


def to_core(array):
    return exchange(array, "seq", 1)


ORDER = (0, 2, 4, 6, 1, 3, 5, 7)


def block_ins(blocks, width, column):
    return [(pl.BlockSpec((256, width), lambda j: (0, column(j))), b) for b in blocks]


def both_cores(own, by_x, by_y, far, *others):
    own_c, by_x_c, by_y_c, far_c = others
    return (own, by_y, own_c, by_y_c, by_x, far, by_x_c, far_c)


def call(body, grid, ins, outs, scratch=(), flops=0, moved=0, vmem=60, aliases={}):
    return pl.pallas_call(
        body,
        grid=grid,
        in_specs=[spec for spec, _ in ins],
        out_specs=[spec for spec, _ in outs],
        out_shape=[shape for _, shape in outs],
        scratch_shapes=list(scratch),
        input_output_aliases=aliases,
        compiler_params=pltpu.CompilerParams(vmem_limit_bytes=vmem * 1024 * 1024),
        cost_estimate=pl.CostEstimate(flops=0, bytes_accessed=0, transcendentals=0),
    )(*[array for _, array in ins])


def call_placed(body, grid, info, ins, outs, scratch=(), flops=0, moved=0, vmem=60):
    return pl.pallas_call(
        body,
        grid_spec=pltpu.PrefetchScalarGridSpec(
            num_scalar_prefetch=1,
            grid=grid,
            in_specs=[spec for spec, _ in ins],
            out_specs=[spec for spec, _ in outs],
            scratch_shapes=list(scratch),
        ),
        out_shape=[shape for _, shape in outs],
        compiler_params=pltpu.CompilerParams(vmem_limit_bytes=vmem * 1024 * 1024),
        cost_estimate=pl.CostEstimate(flops=0, bytes_accessed=0, transcendentals=0),
    )(info, *[array for _, array in ins])


def smem():
    return pl.BlockSpec(memory_space=pltpu.SMEM)


def any_place():
    return pl.BlockSpec(memory_space=pl.ANY)


def whole(array):
    dims = len(array.shape)
    return pl.BlockSpec(array.shape, lambda *_: (0,) * dims, pipeline_mode=pl.Buffered(1))


def block(shape, index):
    return pl.BlockSpec(shape, index)


def struct(shape, dtype):
    return jax.ShapeDtypeStruct(shape, dtype)


def columns(ref, info, place):
    start = pl.multiple_of((info[0] ^ place) * 256, 256)
    return ref[:, pl.ds(start, 256)]


def norm_body(info, tok, cot, gain_a, shift_a, gain_m, shift_m, in_a, in_m, grad, grad_sum):
    step = pl.program_id(0)
    t = tok[...].astype(F32)
    centered = t - jnp.mean(t, -1, keepdims=True)
    xhat = centered * lax.rsqrt(jnp.mean(centered * centered, -1, keepdims=True) + EPS)
    in_a[...] = (xhat * gain_a[...] + shift_a[...]).astype(BF)
    in_m[...] = (xhat * gain_m[...] + shift_m[...]).astype(BF)
    place = info[1] * 256 + lax.broadcasted_iota(jnp.int32, t.shape, 0)
    g = jnp.where(place < info[5 + step], cot[...].astype(F32), 0.0)
    grad[...] = g.astype(BF)

    @pl.when(step == 0)
    def _():
        grad_sum[...] = jnp.zeros_like(grad_sum)

    grad_sum[...] += jnp.sum(g, 0, keepdims=True)


def matched(x, blocks, info):
    left = jnp.concatenate([columns(x, info, r) for r in range(8)], 1)
    right = jnp.concatenate([b[...] for b in blocks], 0)
    return jnp.dot(left, right, preferred_element_type=F32)


def turn(z, cos, front, back):
    first = z[:, :128]
    first = (
        first * cos
        + pltpu.roll(first, 96, 1) * front
        + pltpu.roll(first, 32, 1) * back
    )
    return jnp.concatenate([first, z[:, 128:]], 1)


def qkv_body(info, x, bias, cos, front, back, *refs):
    blocks, (q, kv_a, kv_b) = (refs[:8], refs[8:16]), refs[16:]
    step = pl.program_id(0)
    heads = [matched(x, blocks[h], info) + bias[h : h + 1] for h in range(2)]

    def turned():
        c, f, b = (jnp.concatenate([t[...]] * 4, 0) for t in (cos, front, back))
        return jnp.concatenate([turn(z, c, f, b) for z in heads], 1).astype(BF)

    @pl.when(step == 0)
    def _():
        q[...] = turned()

    @pl.when(step == 1)
    def _():
        k = turned()
        kv_a[...] = k[:512]
        kv_b[...] = k[512:]

    @pl.when(step == 2)
    def _():
        v = jnp.concatenate(heads, 1).astype(BF)
        kv_a[...] = v[:512]
        kv_b[...] = v[512:]


def grad_att_body(info, g, *refs):
    refs[16][...] = jnp.concatenate(
        [matched(g, refs[:8], info), matched(g, refs[8:16], info)], 1
    ).astype(BF)


def up_body(info, x, bias, *refs):
    blocks, (act, slope) = refs[:8], refs[8:]
    z = matched(x, blocks, info) + bias[...]
    gelu, steep = gelu_pair(z)
    act[...] = gelu.astype(BF)
    slope[...] = steep.astype(BF)


def hidden_body(info, g, slope, *refs):
    low, total = refs[8:]
    grad = matched(g, refs[:8], info) * slope[...].astype(F32)
    low[...] = grad.astype(BF)
    total[...] = jnp.sum(grad, 0, keepdims=True)


def nt(a, b):
    return lax.dot_general(a, b, (((1,), (1,)), ((), ())), preferred_element_type=F32)


def tn(a, b):
    return lax.dot_general(a, b, (((0,), (0,)), ((), ())), preferred_element_type=F32)


def attention_body(first_seq, info, q_ref, ga_ref, cos, front, back, *refs):
    keys, values = refs[:4], refs[4:8]
    att, dq, dq_sum, keep, send = refs[8:]
    terms = (keep.at[0], send.at[0], keep.at[1], send.at[1])
    seq = pl.program_id(0)
    head = pl.program_id(1)
    scale = HEAD_DIM ** (-0.5)
    length = info[5 + first_seq + seq]
    q = q_ref[...] * jnp.asarray(scale, BF)
    ga = ga_ref[...]
    last_seen = jnp.minimum(
        info[1] * 256 + lax.broadcasted_iota(jnp.int32, (256, 256), 0), length - 1
    )
    column = lax.broadcasted_iota(jnp.int32, (256, 256), 1)
    scores = [
        jnp.where(info[1 + r] * 256 + column <= last_seen, nt(q, keys[r][...]), FLOOR) for r in range(4)
    ]
    top = jnp.max(jnp.maximum(jnp.maximum(scores[0], scores[1]), jnp.maximum(scores[2], scores[3])), -1, keepdims=True)
    weights = [jnp.exp(s - top) for s in scores]
    total = jnp.sum(weights[0] + weights[1] + weights[2] + weights[3], -1, keepdims=True)
    inverse = 1.0 / total
    probs = [w * inverse for w in weights]
    low = [p.astype(BF) for p in probs]
    out = jnp.zeros((256, 256), F32)
    for r in range(4):
        out += jnp.dot(low[r], values[r][...], preferred_element_type=F32)
    att[...] = out.astype(BF)
    grad_probs = [nt(ga, values[r][...]) for r in range(4)]
    products = [p * g for p, g in zip(probs, grad_probs)]
    delta = jnp.sum(products[0] + products[1] + products[2] + products[3], -1, keepdims=True)
    grad_q = jnp.zeros((256, 256), F32)
    key_columns = pl.ds(pl.multiple_of(head * 256, 256), 256)
    value_columns = pl.ds(pl.multiple_of(head * 256 + 512, 256), 256)
    for r in range(4):
        grad_scores = (probs[r] * (grad_probs[r] - delta)).astype(BF)
        grad_q += jnp.dot(grad_scores, keys[r][...], preferred_element_type=F32)
        terms[r][:, key_columns] = tn(grad_scores, q).astype(BF)
        terms[r][:, value_columns] = tn(low[r], ga).astype(BF)
    grad_q = turn(grad_q * scale, cos[...], -front[...], -back[...])
    dq[...] = grad_q.astype(BF)
    dq_sum[...] = jnp.sum(grad_q, 0, keepdims=True)[None, None]


def streamed(blocks, width, column):
    return [(pl.BlockSpec((256, width), lambda i: (0, column(i))), blocks[r]) for r in ORDER]


def branch_body(info, att, act, *refs):
    w_att, w_act, outs, total = refs[:8], refs[8:16], refs[16:18], refs[18]
    step = pl.program_id(0)

    def part(i):
        return nt(att[...], w_att[i][...]) + nt(act[...], w_act[i][...])

    @pl.when(step == 0)
    def _():
        for i in range(8):
            total[:, i * 256 : (i + 1) * 256] = part(i)

    @pl.when(step == 1)
    def _():
        for i, r in enumerate(ORDER):
            there = pl.ds(pl.multiple_of((info[0] ^ r) * 256, 256), 256)
            done = (total[:, i * 256 : (i + 1) * 256] + part(i)).astype(BF)
            outs[0][:, there] = done[:256]
            outs[1][:, there] = done[256:]


def weight_part(refs):
    products = [tn(refs[i][...], refs[i + 1][...]) for i in range(0, len(refs), 2)]
    return products[0] if len(products) == 1 else jnp.concatenate(products, 1)


def weight_send_body(info, *refs):
    refs[-1][...] = weight_part(refs[:-1]).astype(BF)


def weight_add_body(info, *refs):
    received, over_x, over_y, next_y, next_x, own = refs[-6:]
    step = pl.program_id(0)
    part = (weight_part(refs[:-6]) + received[...].astype(F32)).astype(BF)
    left, right = part[:, :1024], part[:, 1024:]

    @pl.when(step == 0)
    def _():
        over_x[...] = left
        next_x[...] = right

    @pl.when(step == 1)
    def _():
        over_x[...] = left
        over_y[...] = right

    @pl.when(step == 2)
    def _():
        next_y[...] = left
        over_y[...] = right

    @pl.when(step == 3)
    def _():
        own[...] = part


class Scatter:
    def __init__(self, pairs):
        self.pairs = pairs

    def operands(self, flip):
        def index(i, info):
            place = jnp.where(i == 0, 4, jnp.where(i == 1, 5, jnp.where(i == 2, 1, 0)))
            return 0, info[0] ^ place ^ flip

        fixed = lambda array: pl.BlockSpec(array.shape, lambda i, info: (0, 0), pipeline_mode=pl.Buffered(1))
        return [
            operand
            for x, h in self.pairs
            for operand in ((block((1024, 256), index), x), (fixed(h), h))
        ]

    def send(self, info):
        self.sent = call_placed(
            weight_send_body,
            (4,),
            info,
            self.operands(2),
            [(block((256, 2048), lambda i, info: (i, 0)), struct((1024, 2048), BF))],
        )[0]
        return self.sent

    def add(self, info, received):
        clip = lambda first: lambda i, info: (jnp.clip(i - first, 0, 1), 0)
        fixed = lambda width: (block((256, width), lambda i, info: (0, 0)), struct((256, width), BF))
        tall = lambda first: (block((256, 1024), clip(first)), struct((512, 1024), BF))
        made = call_placed(
            weight_add_body,
            (4,),
            info,
            self.operands(0) + [(block((256, 2048), lambda i, info: (i, 0)), received)],
            [tall(0), tall(1), fixed(1024), fixed(1024), fixed(2048)],
        )
        self.over_x, self.over_y, self.next_y, self.next_x, self.own = made
        return self.own

    def first(self, done):
        self.from_x = along_x(after(self.over_x, done))
        self.from_y = along_y(after(self.over_y, done))
        return self.from_x, self.from_y

    def second(self, done):
        self.last_y = along_y(plus(after(self.next_y, done), self.from_x[256:]))
        self.last_x = along_x(plus(after(self.next_x, done), self.from_y[:256]))
        return self.last_y, self.last_x

    def total(self, info, turned=False):
        tall = lambda array, row: (block((256, 1024), lambda i: (row, 0)), array)
        shape = (2048, 256) if turned else (256, 2048)
        return call(
            total_turned_body if turned else total_body,
            (1,),
            [
                (smem(), info),
                (whole(self.own), self.own),
                tall(self.from_x, 0),
                tall(self.last_y, 0),
                tall(self.from_y, 1),
                tall(self.last_x, 0),
            ],
            [(block(shape, lambda i: (0, 0)), struct(shape, F32))],
        )[0]


def total_of(own, from_x, last_y, from_y, last_x):
    left = from_x[...].astype(F32) + last_y[...].astype(F32)
    right = from_y[...].astype(F32) + last_x[...].astype(F32)
    return own[...].astype(F32) + jnp.concatenate([left, right], 1)


def total_body(info, *refs):
    refs[-1][...] = total_of(*refs[:-1])


def total_turned_body(info, *refs):
    refs[-1][...] = total_of(*refs[:-1]).T


def project_body(info, q, own, core, far, cos, front, back, low, kv_sum):
    c, f, b = (jnp.concatenate([t[...]] * 2, 0) for t in (cos, front, back))
    for head in range(2):
        mine = slice(head * 256, head * 256 + 256)
        low[:, head * 768 : head * 768 + 256] = q[:, mine]
        for kind in range(2):
            cut = slice(kind * 512 + head * 256, kind * 512 + head * 256 + 256)
            grad = own[:, cut].astype(F32) + core[:, cut].astype(F32) + far[:, cut].astype(F32)
            if kind == 0:
                grad = turn(grad, c, -f, -b)
            kv_sum[:, head * 512 + kind * 256 : head * 512 + kind * 256 + 256] = jnp.sum(grad, 0, keepdims=True)
            start = head * 768 + 256 + kind * 256
            low[:, start : start + 256] = grad.astype(BF)


def input_body(info, low, hid, tok, gain_a, gain_m, *refs):
    w_qkv, w_up, parts, sums, (gx, xh, inv) = refs[:8], refs[8:16], refs[16:18], refs[18], refs[19:]
    step = pl.program_id(0)

    def products(first):
        for i, r in enumerate(ORDER):
            there = pl.ds(pl.multiple_of((info[0] ^ r) * 256, 256), 256)
            from_attn = nt(low[...], w_qkv[i][:, :768])
            from_mlp = nt(hid[...], w_up[i][...])
            xhat = xh[:, there]
            columns_sums = [from_attn * xhat, from_attn, from_mlp * xhat, from_mlp]
            grad = from_attn * gain_a[:, there] + from_mlp * gain_m[:, there]
            for row, values in enumerate(columns_sums):
                added = jnp.sum(values, 0, keepdims=True)
                sums[row : row + 1, there] = added if first else sums[row : row + 1, there] + added
            gx[:, there] = grad if first else gx[:, there] + grad

    @pl.when(step == 0)
    def _():
        t = tok[...].astype(F32)
        centered = t - jnp.mean(t, -1, keepdims=True)
        inverse = lax.rsqrt(jnp.mean(centered * centered, -1, keepdims=True) + EPS)
        xh[...] = centered * inverse
        inv[...] = jnp.broadcast_to(inverse, inv.shape)
        products(True)

    @pl.when(step == 1)
    def _():
        products(False)
        grad = gx[...]
        xhat = xh[...]
        mean = jnp.mean(grad, -1, keepdims=True)
        along = jnp.mean(grad * xhat, -1, keepdims=True)
        out = (inv[:, :1] * (grad - mean - xhat * along)).astype(BF)
        parts[0][...] = out[:256]
        parts[1][...] = out[256:]


def plus(a, b):
    return (a.astype(F32) + b.astype(F32)).astype(BF)


def bar(*arrays):
    return lax.optimization_barrier(arrays)


def finish_body(info, own, from_x, last_y, from_y, last_x, qkv, out):
    total = total_of(own, from_x, last_y, from_y, last_x)
    for head in range(2):
        qkv[:, head, :] = total[:, head * 768 : head * 768 + 768]
    out[...] = total[:, 1536:].T


class Hops:
    def __init__(self, info, tok, grad, bias):
        self.info = info
        self.given = (tok, grad, bias)
        self.mine = {}
        self.ready = {}
        self.pair = None
        self.out = [None, None]

    def start(self, block):
        self.leaving = self.mine[0] = block
        return [exchange(block, "tensor", 1)]

    def land(self, j, arrived, next_block=None):
        half = lambda array: (block((128, D), lambda i: (i, 0)), array)
        fresh = (block((128, D), lambda i: (i, 0)), struct((256, D), BF))
        parts, ins, outs = [], [(smem(), self.info)], []
        if j >= 2:
            self.ready[j - 2] = (self.leaving, arrived[0])
        if j < 8:
            parts.append("pair")
            ins += [half(self.mine[j]), half(arrived[0])]
            outs.append(fresh)
        if 1 <= j <= 8:
            parts.append("sum" if next_block is None else "either")
            ins += [half(self.pair), half(arrived[1])]
            if next_block is not None:
                ins.append(half(next_block))
            outs.append(fresh)
        made = list(call(lambda *refs: land_body(parts, *refs), (2,), ins, outs))
        done = made[0]
        if next_block is not None:
            self.mine[j + 1] = next_block
        pair = made.pop(0) if j < 8 else None
        self.leaving = made.pop(0) if j else after(next_block, pair)
        flying = [exchange(self.leaving, "tensor", 1)]
        if pair is not None:
            self.pair = pair
            flying.append(lax.ppermute(pair, "tensor", [(1, 2), (2, 1)]))
        return flying, done

    def write(self, k, before):
        tok, grad, bias = self.given
        which, place = divmod(k, 4)
        half = lambda array: (block((128, D), lambda i: (i, 0)), array)
        kept = (block((128, D), lambda i: (2 * place + i, 0)), (tok, grad)[which])
        ins = [(smem(), after(self.info, before))] + [half(array) for array in self.ready[k]] + [kept]
        if not which:
            ins.append((whole(bias), bias))
        aliases = {}
        if self.out[which] is not None:
            aliases[len(ins)] = 0
            ins.append((any_place(), self.out[which]))
        made = call(
            (mixed_body, tokens_grad_body)[which],
            (2,),
            ins,
            [(kept[0], struct((1024, D), (BF, F32)[which]))],
            aliases=aliases,
        )[0]
        self.out[which] = made
        return made


def land_body(parts, info, *refs):
    refs = list(refs)
    outs = refs[-len(parts) :]
    for part, out in zip(parts, outs):
        a, b = refs.pop(0), refs.pop(0)
        summed = (a[...].astype(F32) + b[...].astype(F32)).astype(BF)
        out[...] = jnp.where(info[9] > 0, summed, refs.pop(0)[...]) if part == "either" else summed


def tokens_grad_body(info, total, came, grad, *refs):
    refs[-1][...] = jnp.where(info[9] > 0, total[...], came[...]).astype(F32) + grad[...].astype(F32)


def mixed_body(info, total, came, tok, bias, *refs):
    summed = jnp.where(info[9] > 0, total[...], came[...]).astype(F32) + tok[...].astype(F32)
    refs[-1][...] = (summed + bias[...]).astype(BF)


def per_device_links(
    tokens,
    cotangent,
    lengths,
    block_slot,
    gain_attn,
    shift_attn,
    gain_mlp,
    shift_mlp,
    w_qkv,
    b_qkv,
    w_out,
    b_out,
    w_up,
    b_up,
    w_down,
    b_down,
):
    rows = 1024
    seq_id = lax.axis_index("seq")
    slots = [jnp.sum(jnp.where(jnp.arange(4) == (seq_id ^ r), block_slot, 0)) for r in range(4)]
    tensor_id = lax.axis_index("tensor")
    inner = ((tensor_id == 1) | (tensor_id == 2)).astype(jnp.int32)
    me = seq_id * 2 + lax.axis_index("batch")
    info = jnp.concatenate([jnp.stack([me, *slots]), lengths, inner.reshape(1)]).astype(jnp.int32)
    tok = tokens.reshape(rows, D)
    cot = cotangent.reshape(rows, D)
    cosine, sine = rotation(slots[0] * 256 + jnp.arange(256, dtype=jnp.int32))
    cosine, sine = cosine[:, 0], sine[:, 0]
    zero = jnp.zeros_like(sine)
    cos_t = jnp.concatenate([cosine, cosine, zero + 1.0, zero + 1.0], 1)
    front_t = jnp.concatenate([-sine, zero, zero, zero], 1)
    back_t = jnp.concatenate([zero, sine, zero, zero], 1)
    tables = [(whole(t), t) for t in (cos_t, front_t, back_t)]
    gains = [v.reshape(1, D) for v in (gain_attn, shift_attn, gain_mlp, shift_mlp)]

    def info_in(*tokens_before):
        return (smem(), after(info, *tokens_before) if tokens_before else info)

    row_block = lambda n: block((256, n), lambda i: (i, 0))
    row_struct = lambda n, kind=BF: struct((rows, n), kind)
    tall = lambda n, index: block((256, n), index)

    head_own = jnp.concatenate(
        [w for h in range(2) for w in (w_qkv[:, h], w_out[h * 256 : (h + 1) * 256].T)], 1
    )
    head_x, head_y = along_x(head_own), along_y(head_own)
    head_c = to_core(head_own)
    in_a, in_m, grad_low, grad_sum = call(
        norm_body,
        (4,),
        [info_in(), (row_block(D), tok), (row_block(D), cot)] + [(whole(v), v) for v in gains],
        [(row_block(D), row_struct(D))] * 3 + [(block((1, D), lambda i: (0, 0)), struct((1, D), F32))],
        moved=5 * rows * D * 2,
    )
    down_own = w_down.T
    head_x, head_y, head_c, in_a, in_m, grad_low, down_own = bar(
        head_x, head_y, head_c, in_a, in_m, grad_low, down_own
    )

    far_y, far_x = along_y(head_x[:128]), along_x(head_y[128:])
    others = [head_c, to_core(head_x), to_core(head_y)]
    far_y, far_x, up_own, *others = bar(far_y, far_x, w_up, *others)

    up_x, up_y = along_x(up_own), along_y(up_own)
    far = jnp.concatenate([far_y, far_x], 0)
    heads = both_cores(head_own, head_x, head_y, far, *others, to_core(far))
    bias = jnp.swapaxes(b_qkv.reshape(2, 3, 256), 0, 1)
    q, kv_a, kv_b = call(
        lambda info, x, bias, *refs: qkv_body(info, x, bias.at[0], *refs),
        (3,),
        [info_in(), (whole(in_a), in_a), (block((1, 2, 256), lambda j: (j, 0, 0)), bias)]
        + tables
        + block_ins(heads, 256, lambda j: j)
        + block_ins(heads, 256, lambda j: j + 4),
        [
            (block((rows, 512), lambda j: (0, 0)), row_struct(512)),
            (block((512, 512), lambda j: (0, jnp.maximum(j - 1, 0))), struct((512, 1024), BF)),
            (block((512, 512), lambda j: (0, jnp.maximum(j - 1, 0))), struct((512, 1024), BF)),
        ],
        flops=2 * rows * D * 1536,
        moved=2 * (rows * D + D * 1536 + rows * 1536),
    )
    kv_x = along_x(kv_a)
    grad_att = call(
        grad_att_body,
        (1,),
        [info_in(q), (whole(grad_low), grad_low)]
        + block_ins(heads, 256, lambda j: 3)
        + block_ins(heads, 256, lambda j: 7),
        [(block((rows, 512), lambda j: (0, 0)), row_struct(512))],
        flops=2 * rows * D * 512,
        moved=2 * (rows * D + D * 512 + rows * 512),
    )[0]
    up_c = to_core(after(up_own, q))
    up_x, up_y, up_c, grad_att = bar(up_x, up_y, up_c, grad_att)

    up_far = along_y(up_x)
    others = [up_c, to_core(up_x), to_core(up_y)]
    down_own = after(down_own, *others)
    down_x, down_y = along_x(down_own), along_y(down_own)
    up_far, kv_x, kv_a, *others = bar(up_far, kv_x, kv_a, *others)
    ups = both_cores(up_own, up_x, up_y, up_far, *others, to_core(up_far))

    def kv_refs(own, by_x):
        both = to_core(jnp.concatenate([own, by_x], 0))
        return [(own, 0), (both, 0), (by_x, 0), (both, 2)]

    kv = [kv_refs(kv_a, kv_x)]
    act, slope = call(
        up_body,
        (4,),
        [info_in(grad_att), (whole(in_m), in_m), (block((1, 512), lambda j: (0, j)), b_up.reshape(1, -1))]
        + block_ins(ups, 512, lambda j: j),
        [(block((rows, 512), lambda j: (0, j)), row_struct(2048))] * 2,
        flops=2 * rows * D * 2048,
        moved=2 * (rows * D + D * 2048 + 2 * rows * 2048),
    )
    down_c = to_core(after(down_own, ups[7]))
    down_x, down_y, down_c, act, slope = bar(down_x, down_y, down_c, act, slope)

    def attention(part, *before):
        base = part * 2
        spot = lambda offset: block((256, 256), lambda s, h: (s + base, h + offset))
        local = lambda offset, row=0: block((256, 256), lambda s, h: (s + row, h + offset))
        return call(
            lambda *refs: attention_body(base, *refs),
            (2, 2),
            [info_in(*before), (spot(0), q), (spot(0), grad_att)]
            + tables
            + [(local(0, row), b) for b, row in kv[part]]
            + [(local(2, row), b) for b, row in kv[part]],
            [
                (local(0), struct((512, 512), BF)),
                (local(0), struct((512, 512), BF)),
                (block((1, 1, 1, 256), lambda s, h: (s, h, 0, 0)), struct((2, 2, 1, 256), F32)),
            ]
            + [(block((2, 256, 1024), lambda s, h: (0, s, 0)), struct((2, 512, 1024), BF))] * 2,
            flops=4 * 6 * 2 * 256 * 1024 * 256,
            moved=4 * 2 * 256 * 256 * 24,
        )

    def branch(part, att, *before):
        return call(
            branch_body,
            (2,),
            [
                info_in(*before),
                (block((512, 256), lambda i: (0, i)), att),
                (block((512, 1024), lambda i: (part, i)), act),
            ]
            + streamed(heads, 256, lambda i: 3 + 4 * i)
            + streamed(downs, 1024, lambda i: i),
            [(block((256, D), lambda i: (0, 0)), struct((256, D), BF))] * 2,
            scratch=[pltpu.VMEM((512, D), F32)],
            flops=2 * 512 * D * 2560,
            moved=2 * (512 * 2560 + D * 2560 + 512 * D),
        )

    far_y, far_x = along_y(down_x[:128]), along_x(down_y[128:])
    others = [down_c, to_core(down_x), to_core(down_y)]
    att_a, dq_a, dq_sum_a, keep_a, send_a = attention(0, down_x)
    far_y, far_x, att_a, kv_b, send_a, *others = bar(far_y, far_x, att_a, kv_b, send_a, *others)

    far = jnp.concatenate([far_y, far_x], 0)
    downs = both_cores(down_own, down_x, down_y, far, *others, to_core(far))
    kv_x = along_x(kv_b)
    received_a = to_core(send_a)
    branch_a = branch(0, att_a)
    received_a, *branch_a = bar(received_a, *branch_a)

    hops = Hops(info, tok, grad_low, (b_out + b_down).reshape(1, D))

    def hidden_call(before):
        return call(
            hidden_body,
            (4,),
            [info_in(before), (whole(grad_low), grad_low), (block((rows, 512), lambda j: (0, j)), slope)]
            + block_ins(downs, 512, lambda j: j),
            [
                (block((rows, 512), lambda j: (0, j)), row_struct(2048)),
                (block((1, 512), lambda j: (0, j)), struct((1, 2048), F32)),
            ],
            flops=2 * rows * D * 2048,
            moved=2 * (rows * D + D * 2048 + 2 * rows * 2048),
        )

    def project(dq, keep, came, far, before):
        return call(
            project_body,
            (1,),
            [info_in(before), (whole(dq), dq)]
            + [(pl.BlockSpec((None, 512, 1024), lambda i: (0, 0, 0)), t) for t in (keep, came)]
            + [(whole(far), far)]
            + tables,
            [
                (block((512, 1536), lambda i: (0, 0)), struct((512, 1536), BF)),
                (block((1, 1024), lambda i: (0, 0)), struct((1, 1024), F32)),
            ],
            moved=2 * 512 * 5000,
        )

    def input_part(half, low, before):
        return call(
            input_body,
            (2,),
            [
                info_in(before),
                (block((512, 768), lambda i: (0, i)), low),
                (block((512, 1024), lambda i: (half, i)), hidden_low),
                (pl.BlockSpec((512, D), lambda i: (half, 0), pipeline_mode=pl.Buffered(1)), tok),
            ]
            + [(whole(t), t) for t in (gains[0], gains[2])]
            + streamed(heads, 1024, lambda i: i)
            + streamed(ups, 1024, lambda i: i),
            [(block((256, D), lambda i: (0, 0)), struct((256, D), BF))] * 2
            + [(block((8, D), lambda i: (0, 0)), struct((8, D), F32))],
            scratch=[pltpu.VMEM((512, D), F32), pltpu.VMEM((512, D), F32), pltpu.VMEM((512, 128), F32)],
            flops=2 * 512 * D * 3584,
            moved=2 * (512 * 6000 + D * 3584),
        )

    flown = hops.start(branch_a[0])
    far_a = along_x(plus(keep_a[1], received_a[1]))
    hidden_low, b_up_sum = hidden_call(branch_a[0])
    down = Scatter([(grad_low, act)])
    down_sent = down.send(after(info, hidden_low))
    flown, kv_x, down_sent = bar(flown, kv_x, down_sent)

    flown, done = hops.land(0, flown, branch_a[1])
    kv.append(kv_refs(kv_b, after(kv_x, done)))
    down_received = to_core(after(down_sent, done))
    att_b, dq_b, dq_sum_b, keep_b, send_b = attention(1, done)
    branch_b = branch(1, att_b, att_b)
    flown, far_a, down_received, send_b, *branch_b = bar(flown, far_a, down_received, send_b, *branch_b)

    flown, done = hops.land(1, flown, branch_b[0])
    received_b = to_core(after(send_b, done))
    low_a, kv_sum_a = project(dq_a, keep_a, received_a, far_a, done)
    first, second, norm_sum_a = input_part(0, low_a, low_a)
    flown, received_b, first, second = bar(flown, received_b, first, second)

    flown, done = hops.land(2, flown, branch_b[1])
    far_b = along_x(plus(after(keep_b[1], done), received_b[1]))
    token = down.add(after(info, done), down_received)
    up = Scatter([(in_m, hidden_low)])
    up_sent = up.send(after(info, token))
    flown, far_b, up_sent = bar(flown, far_b, up_sent)

    flown, done = hops.land(3, flown, first)
    down_first = down.first(done)
    up_received = to_core(after(up_sent, done))
    low_b, kv_sum_b = project(dq_b, keep_b, received_b, far_b, done)
    third, fourth, norm_sum_b = input_part(1, low_b, low_b)
    q_sums = (dq_sum_a + dq_sum_b).sum(0).reshape(2, 1, 256)
    kv_total = (kv_sum_a + kv_sum_b).reshape(2, 2, 256)
    bias_qkv = jnp.concatenate([q_sums, kv_total], 1).reshape(-1)
    norm_sums = (norm_sum_a + norm_sum_b)[:4].reshape(-1)
    small = jnp.concatenate([norm_sums, bias_qkv, grad_sum[0], b_up_sum[0]]).reshape(-1, 128)
    flown, (down.from_x, down.from_y), up_received, third, fourth, small = bar(
        flown, down_first, up_received, third, fourth, small
    )

    flown, done = hops.land(4, flown, second)
    small_c = to_core(after(small, done))
    down_second = down.second(done)
    token = up.add(after(info, done), up_received)
    hops.write(0, token)
    project_low = jnp.concatenate([after(low_a, token), low_b], 0)
    attended = jnp.concatenate([after(att_a, token), att_b], 0)
    flown, (down.last_y, down.last_x), small_c, project_low, attended = bar(
        flown, down_second, small_c, project_low, attended
    )

    flown, done = hops.land(5, flown, third)
    up_first = up.first(done)
    attn = Scatter([(in_a, project_low), (grad_low, attended)])
    attn_sent = attn.send(after(info, done))
    small = after(small, attn_sent) + small_c
    norms = small[:64]
    norms_z = exchange(norms, "tensor", 1)
    written = hops.write(1, attn_sent)
    flown, (up.from_x, up.from_y), attn_sent, norms_z, hops.out[0] = bar(
        flown, up_first, attn_sent, norms_z, written
    )

    flown, done = hops.land(6, flown, fourth)
    attn_received = to_core(after(attn_sent, done))
    up_second = up.second(done)
    token = attn.add(after(info, done), attn_received)
    norms = after(norms, token) + norms_z
    norms_z = exchange(norms, "tensor", 2)
    flown, (up.last_y, up.last_x), norms_z, token = bar(flown, up_second, norms_z, token)

    flown, done = hops.land(7, flown)
    attn_first = attn.first(done)
    down_grad = down.total(after(info, done), True)
    written = hops.write(2, down_grad)
    written = hops.write(3, written)
    written = hops.write(4, written)
    up_grad = up.total(after(info, written))
    flown, (attn.from_x, attn.from_y), up_grad, down_grad, hops.out[1] = bar(
        flown, attn_first, up_grad, down_grad, hops.out[1]
    )

    flown, done = hops.land(8, flown)
    attn_second = attn.second(done)
    written = hops.write(5, done)
    written = hops.write(6, written)
    small = jnp.concatenate([after(norms, written) + norms_z, small[64:]], 0)
    small = small + along_y(small)
    small = small + along_x(small)
    attn.last_y, attn.last_x = attn_second
    tall = lambda array, row: (block((256, 1024), lambda i: (row, 0)), array)
    qkv_grad, out_grad = call(
        finish_body,
        (1,),
        [
            info_in(written),
            (whole(attn.own), attn.own),
            tall(attn.from_x, 0),
            tall(attn.last_y, 0),
            tall(attn.from_y, 1),
            tall(attn.last_x, 0),
        ],
        [
            (block((256, 2, 768), lambda i: (0, 0, 0)), struct((256, 2, 768), F32)),
            (block((512, 256), lambda i: (0, 0)), struct((512, 256), F32)),
        ],
    )
    hops.ready[7] = (hops.leaving, flown[0])
    (leaving, came), qkv_grad, out_grad, small, hops.out[1] = bar(
        hops.ready[7], qkv_grad, out_grad, small, hops.out[1]
    )
    hops.ready[7] = (leaving, came)
    hops.write(7, came)
    mixed, tokens_grad = hops.out

    norms = small[:64].reshape(4, D)
    small = small[64:].reshape(-1)
    bias_out = small[1536 : 1536 + D]

    return (
        mixed.reshape(tokens.shape),
        tokens_grad.reshape(tokens.shape),
        norms[0],
        norms[1],
        norms[2],
        norms[3],
        qkv_grad,
        small[:1536].reshape(b_qkv.shape),
        out_grad,
        bias_out,
        up_grad,
        small[1536 + D :],
        down_grad,
        bias_out,
    )


def solution(mesh):
    in_specs = (
        P("batch", "seq", None),
        P("batch", "seq", None),
        P("batch"),
        P(),
        P(),
        P(),
        P(),
        P(),
        P(("seq", "batch"), "tensor", None),
        P("tensor", None),
        P("tensor", ("seq", "batch")),
        P(),
        P(("seq", "batch"), "tensor"),
        P("tensor"),
        P("tensor", ("seq", "batch")),
        P(),
    )
    out_specs = (
        P("batch", "seq", None),
        P("batch", "seq", None),
        P(),
        P(),
        P(),
        P(),
        P(("seq", "batch"), "tensor", None),
        P("tensor", None),
        P("tensor", ("seq", "batch")),
        P(),
        P(("seq", "batch"), "tensor"),
        P("tensor"),
        P("tensor", ("seq", "batch")),
        P(),
    )
    links = tuple(mesh.shape[axis] for axis in ("seq", "batch", "tensor"))
    per_device = per_device_links if links == (4, 2, 4) else per_device_any
    return jax.shard_map(
        per_device, mesh=mesh, in_specs=in_specs, out_specs=out_specs, check_vma=False
    )
```

```python
import jax
import jax.numpy as jnp
from jax import lax
from jax.experimental import pallas as pl
from jax.experimental.pallas import tpu as pltpu
from jax.sharding import PartitionSpec as P

D = 2048
HEAD_DIM = 256
ROT = 64
EPS = 1e-05
FLOOR = -1e30
BF = jnp.bfloat16
F32 = jnp.float32


def dot(a, b, dims):
    return lax.dot_general(a, b, (dims, ((), ())), preferred_element_type=F32)


def rotation(places):
    half_rot = ROT // 2
    frequency = 10000.0 ** (jnp.arange(half_rot, dtype=F32) * (-2.0 / ROT))
    angles = places.astype(F32)[:, None] * frequency[None, :]
    return jnp.cos(angles)[:, None, :], jnp.sin(angles)[:, None, :]


def rotate(field, cosine, sine):
    half_rot = ROT // 2
    front = field[..., :half_rot]
    back = field[..., half_rot:ROT]
    return jnp.concatenate(
        [front * cosine - back * sine, back * cosine + front * sine, field[..., ROT:]], -1
    )


def gelu_pair(z):
    phi_cdf = 0.5 * (1.0 + lax.erf(z * 0.7071067811865476))
    density = 0.3989422804014327 * jnp.exp(-0.5 * z * z)
    return z * phi_cdf, phi_cdf + z * density


def per_device_any(
    tokens,
    cotangent,
    lengths,
    block_slot,
    gain_attn,
    shift_attn,
    gain_mlp,
    shift_mlp,
    w_qkv,
    b_qkv,
    w_out,
    b_out,
    w_up,
    b_up,
    w_down,
    b_down,
):
    seqs, block_rows, _ = tokens.shape
    rows = seqs * block_rows
    shard = w_qkv.shape[0]
    heads = w_qkv.shape[1]
    width_qkv = heads * 3 * HEAD_DIM
    width_att = heads * HEAD_DIM
    units = w_up.shape[1]
    fsdp = ("seq", "batch")
    scale = HEAD_DIM ** (-0.5)
    seq_count = lax.axis_size("seq")
    device_ids = jnp.arange(seq_count, dtype=jnp.int32)
    own_slot = jnp.sum(jnp.where(device_ids == lax.axis_index("seq"), block_slot, 0))
    offsets = jnp.arange(block_rows, dtype=jnp.int32)
    query_places = own_slot * block_rows + offsets
    key_places = (block_slot[:, None] * block_rows + offsets[None, :]).reshape(-1)

    attn_shard = jnp.concatenate([w_qkv.reshape(shard, width_qkv), w_out.T], 1)
    mlp_shard = jnp.concatenate([w_up, w_down.T], 1)
    attn_full = lax.all_gather(attn_shard, fsdp, axis=0, tiled=True)
    mlp_full = lax.all_gather(mlp_shard, fsdp, axis=0, tiled=True)
    full_qkv = attn_full[:, :width_qkv]
    full_out_t = attn_full[:, width_qkv:]
    full_up = mlp_full[:, :units]
    full_down_t = mlp_full[:, units:]

    token_rows = tokens.astype(F32).reshape(rows, D)
    centered = token_rows - jnp.mean(token_rows, -1, keepdims=True)
    inverse = lax.rsqrt(jnp.mean(jnp.square(centered), -1, keepdims=True) + EPS)
    xhat = centered * inverse
    input_attn = (xhat * gain_attn + shift_attn).astype(BF)
    input_mlp = (xhat * gain_mlp + shift_mlp).astype(BF)

    valid = (query_places[None, :] < lengths[:, None]).astype(F32)
    grad_rows = (cotangent.astype(F32) * valid[..., None]).reshape(rows, D)
    grad_low = grad_rows.astype(BF)

    project = dot(input_attn, full_qkv, ((1,), (0,))).reshape(
        seqs, block_rows, heads, 3 * HEAD_DIM
    ) + b_qkv
    cosine, sine = rotation(query_places)
    queries = rotate(project[..., :HEAD_DIM], cosine, sine).astype(BF)
    keys = rotate(project[..., HEAD_DIM : 2 * HEAD_DIM], cosine, sine).astype(BF)
    values = project[..., 2 * HEAD_DIM :].astype(BF)
    pair = jnp.concatenate([keys, values], -1)
    gathered = lax.all_gather(pair, "seq", axis=0, tiled=False)
    gathered = jnp.transpose(gathered, (1, 3, 0, 2, 4)).reshape(
        seqs, heads, seq_count * block_rows, 2 * HEAD_DIM
    )
    all_keys = gathered[..., :HEAD_DIM]
    all_values = gathered[..., HEAD_DIM:]

    hidden_pre = dot(input_mlp, full_up, ((1,), (0,))) + b_up
    gelu, slope = gelu_pair(hidden_pre)
    activated = gelu.astype(BF)
    grad_hidden = dot(grad_low, full_down_t, ((1,), (0,))) * slope
    hidden_low = grad_hidden.astype(BF)
    bias_up_sum = jnp.sum(grad_hidden, 0)

    grad_att = dot(grad_low, full_out_t, ((1,), (0,))).reshape(
        seqs, block_rows, heads, HEAD_DIM
    ).astype(BF)

    causal = key_places[None, None, :] <= query_places[None, :, None]
    inside = key_places[None, None, :] < lengths[:, None, None]
    mask = (causal & inside)[:, None]
    scores = jnp.einsum("schd,shtd->shct", queries, all_keys, preferred_element_type=F32) * scale
    scores = jnp.where(mask, scores, FLOOR)
    top = jnp.max(scores, -1, keepdims=True)
    weights = jnp.where(mask, jnp.exp(scores - top), 0.0)
    probs = weights / jnp.sum(weights, -1, keepdims=True)
    prob_low = probs.astype(BF)
    attended = jnp.einsum("shct,shtd->schd", prob_low, all_values, preferred_element_type=F32)
    attended = attended.astype(BF).reshape(rows, width_att)

    partial = dot(attended, full_out_t, ((1,), (1,))) + dot(activated, full_down_t, ((1,), (1,)))
    branch = lax.psum(partial.astype(BF), "tensor").astype(F32)

    grad_mlp_weights = jnp.concatenate(
        [dot(input_mlp, hidden_low, ((0,), (0,))), dot(grad_low, activated, ((0,), (0,)))], 1
    ).astype(BF)
    mlp_reduced = lax.psum_scatter(
        grad_mlp_weights, fsdp, scatter_dimension=0, tiled=True
    ).astype(F32)

    grad_probs = jnp.einsum("schd,shtd->shct", grad_att, all_values, preferred_element_type=F32)
    delta = jnp.sum(probs * grad_probs, -1, keepdims=True)
    grad_scores = (probs * (grad_probs - delta)).astype(BF)
    grad_query = jnp.einsum("shct,shtd->schd", grad_scores, all_keys, preferred_element_type=F32) * scale
    key_term = jnp.einsum("shct,schd->tshd", grad_scores, queries, preferred_element_type=F32) * scale
    value_term = jnp.einsum("shct,schd->tshd", prob_low, grad_att, preferred_element_type=F32)
    terms = jnp.concatenate([key_term, value_term], -1).astype(BF)
    own_terms = lax.psum_scatter(terms, "seq", scatter_dimension=0, tiled=True).astype(F32)
    own_terms = jnp.swapaxes(own_terms, 0, 1)
    grad_key = own_terms[..., :HEAD_DIM]
    grad_value = own_terms[..., HEAD_DIM:]
    grad_project = jnp.concatenate(
        [rotate(grad_query, cosine, -sine), rotate(grad_key, cosine, -sine), grad_value], -1
    ).reshape(rows, width_qkv)
    bias_qkv_sum = jnp.sum(grad_project, 0)
    project_low = grad_project.astype(BF)

    grad_norm_attn = dot(project_low, full_qkv, ((1,), (1,)))
    grad_norm_mlp = dot(hidden_low, full_up, ((1,), (1,)))
    norm_sums = jnp.stack(
        [
            jnp.sum(grad_norm_attn * xhat, 0),
            jnp.sum(grad_norm_attn, 0),
            jnp.sum(grad_norm_mlp * xhat, 0),
            jnp.sum(grad_norm_mlp, 0),
        ]
    )
    grad_xhat = grad_norm_attn * gain_attn + grad_norm_mlp * gain_mlp
    input_part = inverse * (
        grad_xhat
        - jnp.mean(grad_xhat, -1, keepdims=True)
        - xhat * jnp.mean(grad_xhat * xhat, -1, keepdims=True)
    )
    input_part, branch = lax.optimization_barrier((input_part.astype(BF), branch))
    input_sum = lax.psum(input_part, "tensor").astype(F32)
    mixed = (token_rows + branch + b_out + b_down).astype(BF).reshape(tokens.shape)
    tokens_grad = (grad_rows + input_sum).reshape(tokens.shape)

    grad_attn_weights = jnp.concatenate(
        [dot(input_attn, project_low, ((0,), (0,))), dot(grad_low, attended, ((0,), (0,)))], 1
    ).astype(BF)
    attn_reduced = lax.psum_scatter(
        grad_attn_weights, fsdp, scatter_dimension=0, tiled=True
    ).astype(F32)

    norm_sums = lax.psum(norm_sums, "tensor").reshape(-1)
    small = lax.psum(
        jnp.concatenate([norm_sums, bias_qkv_sum, jnp.sum(grad_rows, 0), bias_up_sum]), fsdp
    )
    norm_sums = small[: 4 * D].reshape(4, D)
    small = small[4 * D :]
    bias_qkv_sum = small[:width_qkv].reshape(b_qkv.shape)
    bias_out_sum = small[width_qkv : width_qkv + D]
    bias_up_sum = small[width_qkv + D :]
    return (
        mixed,
        tokens_grad,
        norm_sums[0],
        norm_sums[1],
        norm_sums[2],
        norm_sums[3],
        attn_reduced[:, :width_qkv].reshape(w_qkv.shape),
        bias_qkv_sum,
        attn_reduced[:, width_qkv:].T,
        bias_out_sum,
        mlp_reduced[:, :units],
        bias_up_sum,
        mlp_reduced[:, units:].T,
        bias_out_sum,
    )


def exchange(array, axis, flip):
    size = lax.axis_size(axis)
    return lax.ppermute(array, axis, [(i, i ^ flip) for i in range(size)])


def after(array, *others):
    return lax.optimization_barrier((array, *others))[0]


def along_x(array):
    return exchange(array, "seq", 2)


def along_y(array):
    return exchange(array, "batch", 1)


def to_core(array):
    return exchange(array, "seq", 1)


ORDER = (0, 2, 4, 6, 1, 3, 5, 7)


def block_ins(blocks, width, column):
    return [(pl.BlockSpec((256, width), lambda j: (0, column(j))), b) for b in blocks]


def both_cores(own, by_x, by_y, far, *others):
    own_c, by_x_c, by_y_c, far_c = others
    return (own, by_y, own_c, by_y_c, by_x, far, by_x_c, far_c)


def call(body, grid, ins, outs, scratch=(), flops=0, moved=0, vmem=60, aliases={}):
    return pl.pallas_call(
        body,
        grid=grid,
        in_specs=[spec for spec, _ in ins],
        out_specs=[spec for spec, _ in outs],
        out_shape=[shape for _, shape in outs],
        scratch_shapes=list(scratch),
        input_output_aliases=aliases,
        compiler_params=pltpu.CompilerParams(vmem_limit_bytes=vmem * 1024 * 1024),
        cost_estimate=pl.CostEstimate(flops=0, bytes_accessed=0, transcendentals=0),
    )(*[array for _, array in ins])


def call_placed(body, grid, info, ins, outs, scratch=(), flops=0, moved=0, vmem=60):
    return pl.pallas_call(
        body,
        grid_spec=pltpu.PrefetchScalarGridSpec(
            num_scalar_prefetch=1,
            grid=grid,
            in_specs=[spec for spec, _ in ins],
            out_specs=[spec for spec, _ in outs],
            scratch_shapes=list(scratch),
        ),
        out_shape=[shape for _, shape in outs],
        compiler_params=pltpu.CompilerParams(vmem_limit_bytes=vmem * 1024 * 1024),
        cost_estimate=pl.CostEstimate(flops=0, bytes_accessed=0, transcendentals=0),
    )(info, *[array for _, array in ins])


def smem():
    return pl.BlockSpec(memory_space=pltpu.SMEM)


def any_place():
    return pl.BlockSpec(memory_space=pl.ANY)


def whole(array):
    dims = len(array.shape)
    return pl.BlockSpec(array.shape, lambda *_: (0,) * dims, pipeline_mode=pl.Buffered(1))


def block(shape, index):
    return pl.BlockSpec(shape, index)


def struct(shape, dtype):
    return jax.ShapeDtypeStruct(shape, dtype)


def columns(ref, info, place):
    start = pl.multiple_of((info[0] ^ place) * 256, 256)
    return ref[:, pl.ds(start, 256)]


def norm_body(info, tok, cot, gain_a, shift_a, gain_m, shift_m, in_a, in_m, grad, grad_sum):
    step = pl.program_id(0)
    t = tok[...].astype(F32)
    centered = t - jnp.mean(t, -1, keepdims=True)
    xhat = centered * lax.rsqrt(jnp.mean(centered * centered, -1, keepdims=True) + EPS)
    in_a[...] = (xhat * gain_a[...] + shift_a[...]).astype(BF)
    in_m[...] = (xhat * gain_m[...] + shift_m[...]).astype(BF)
    place = info[1] * 256 + lax.broadcasted_iota(jnp.int32, t.shape, 0)
    g = jnp.where(place < info[5 + step], cot[...].astype(F32), 0.0)
    grad[...] = g.astype(BF)

    @pl.when(step == 0)
    def _():
        grad_sum[...] = jnp.zeros_like(grad_sum)

    grad_sum[...] += jnp.sum(g, 0, keepdims=True)


def matched(x, blocks, info):
    left = jnp.concatenate([columns(x, info, r) for r in range(8)], 1)
    right = jnp.concatenate([b[...] for b in blocks], 0)
    return jnp.dot(left, right, preferred_element_type=F32)


def turn(z, cos, front, back):
    first = z[:, :128]
    first = (
        first * cos
        + pltpu.roll(first, 96, 1) * front
        + pltpu.roll(first, 32, 1) * back
    )
    return jnp.concatenate([first, z[:, 128:]], 1)


def qkv_body(info, x, bias, cos, front, back, *refs):
    blocks, (q, kv_a, kv_b) = (refs[:8], refs[8:16]), refs[16:]
    step = pl.program_id(0)
    heads = [matched(x, blocks[h], info) + bias[h : h + 1] for h in range(2)]

    def turned():
        c, f, b = (jnp.concatenate([t[...]] * 4, 0) for t in (cos, front, back))
        return jnp.concatenate([turn(z, c, f, b) for z in heads], 1).astype(BF)

    @pl.when(step == 0)
    def _():
        q[...] = turned()

    @pl.when(step == 1)
    def _():
        k = turned()
        kv_a[...] = k[:512]
        kv_b[...] = k[512:]

    @pl.when(step == 2)
    def _():
        v = jnp.concatenate(heads, 1).astype(BF)
        kv_a[...] = v[:512]
        kv_b[...] = v[512:]


def split_body(from_x, from_y, top, bottom):
    top[...] = from_x[...]
    bottom[...] = from_y[...]


def grad_att_body(info, g, *refs):
    refs[16][...] = jnp.concatenate(
        [matched(g, refs[:8], info), matched(g, refs[8:16], info)], 1
    ).astype(BF)


def up_body(info, x, bias, *refs):
    blocks, (act, slope) = refs[:8], refs[8:]
    z = matched(x, blocks, info) + bias[...]
    gelu, steep = gelu_pair(z)
    act[...] = gelu.astype(BF)
    slope[...] = steep.astype(BF)


def hidden_body(info, g, slope, *refs):
    low, total = refs[8:]
    grad = matched(g, refs[:8], info) * slope[...].astype(F32)
    low[...] = grad.astype(BF)
    total[...] = jnp.sum(grad, 0, keepdims=True)


def nt(a, b):
    return lax.dot_general(a, b, (((1,), (1,)), ((), ())), preferred_element_type=F32)


def tn(a, b):
    return lax.dot_general(a, b, (((0,), (0,)), ((), ())), preferred_element_type=F32)


def attention_body(first_seq, info, q_ref, ga_ref, cos, front, back, *refs):
    keys, values = refs[:4], refs[4:8]
    att, dq, dq_sum, keep, send = refs[8:]
    terms = (keep.at[0], send.at[0], keep.at[1], send.at[1])
    seq = pl.program_id(0)
    head = pl.program_id(1)
    scale = HEAD_DIM ** (-0.5)
    length = info[5 + first_seq + seq]
    q = q_ref[...] * jnp.asarray(scale, BF)
    ga = ga_ref[...]
    last_seen = jnp.minimum(
        info[1] * 256 + lax.broadcasted_iota(jnp.int32, (256, 256), 0), length - 1
    )
    column = lax.broadcasted_iota(jnp.int32, (256, 256), 1)
    scores = [
        jnp.where(info[1 + r] * 256 + column <= last_seen, nt(q, keys[r][...]), FLOOR) for r in range(4)
    ]
    top = jnp.max(jnp.maximum(jnp.maximum(scores[0], scores[1]), jnp.maximum(scores[2], scores[3])), -1, keepdims=True)
    weights = [jnp.exp(s - top) for s in scores]
    total = jnp.sum(weights[0] + weights[1] + weights[2] + weights[3], -1, keepdims=True)
    inverse = 1.0 / total
    probs = [w * inverse for w in weights]
    low = [p.astype(BF) for p in probs]
    out = jnp.zeros((256, 256), F32)
    for r in range(4):
        out += jnp.dot(low[r], values[r][...], preferred_element_type=F32)
    att[...] = out.astype(BF)
    grad_probs = [nt(ga, values[r][...]) for r in range(4)]
    products = [p * g for p, g in zip(probs, grad_probs)]
    delta = jnp.sum(products[0] + products[1] + products[2] + products[3], -1, keepdims=True)
    grad_q = jnp.zeros((256, 256), F32)
    key_columns = pl.ds(pl.multiple_of(head * 256, 256), 256)
    value_columns = pl.ds(pl.multiple_of(head * 256 + 512, 256), 256)
    for r in range(4):
        grad_scores = (probs[r] * (grad_probs[r] - delta)).astype(BF)
        grad_q += jnp.dot(grad_scores, keys[r][...], preferred_element_type=F32)
        terms[r][:, key_columns] = tn(grad_scores, q).astype(BF)
        terms[r][:, value_columns] = tn(low[r], ga).astype(BF)
    grad_q = turn(grad_q * scale, cos[...], -front[...], -back[...])
    dq[...] = grad_q.astype(BF)
    dq_sum[...] = jnp.sum(grad_q, 0, keepdims=True)[None, None]


def streamed(blocks, width, column):
    return [(pl.BlockSpec((256, width), lambda i: (0, column(i))), blocks[r]) for r in ORDER]


def branch_body(info, att, act, *refs):
    w_att, w_act, outs, total = refs[:8], refs[8:16], refs[16:18], refs[18]
    step = pl.program_id(0)

    def part(i):
        return nt(att[...], w_att[i][...]) + nt(act[...], w_act[i][...])

    @pl.when(step == 0)
    def _():
        for i in range(8):
            total[:, i * 256 : (i + 1) * 256] = part(i)

    @pl.when(step == 1)
    def _():
        for i, r in enumerate(ORDER):
            there = pl.ds(pl.multiple_of((info[0] ^ r) * 256, 256), 256)
            done = (total[:, i * 256 : (i + 1) * 256] + part(i)).astype(BF)
            outs[0][:, there] = done[:256]
            outs[1][:, there] = done[256:]


def weight_part(refs):
    products = [tn(refs[i][...], refs[i + 1][...]) for i in range(0, len(refs), 2)]
    return products[0] if len(products) == 1 else jnp.concatenate(products, 1)


def weight_send_body(info, *refs):
    refs[-1][...] = weight_part(refs[:-1]).astype(BF)


def weight_add_body(info, *refs):
    received, over_x, over_y, next_y, next_x, own = refs[-6:]
    step = pl.program_id(0)
    part = (weight_part(refs[:-6]) + received[...].astype(F32)).astype(BF)
    left, right = part[:, :1024], part[:, 1024:]

    @pl.when(step == 0)
    def _():
        over_x[...] = left
        next_x[...] = right

    @pl.when(step == 1)
    def _():
        over_x[...] = left
        over_y[...] = right

    @pl.when(step == 2)
    def _():
        next_y[...] = left
        over_y[...] = right

    @pl.when(step == 3)
    def _():
        own[...] = part


class Scatter:
    def __init__(self, pairs):
        self.pairs = pairs

    def operands(self, flip):
        def index(i, info):
            place = jnp.where(i == 0, 4, jnp.where(i == 1, 5, jnp.where(i == 2, 1, 0)))
            return 0, info[0] ^ place ^ flip

        fixed = lambda array: pl.BlockSpec(array.shape, lambda i, info: (0, 0), pipeline_mode=pl.Buffered(1))
        return [
            operand
            for x, h in self.pairs
            for operand in ((block((1024, 256), index), x), (fixed(h), h))
        ]

    def send(self, info):
        self.sent = call_placed(
            weight_send_body,
            (4,),
            info,
            self.operands(2),
            [(block((256, 2048), lambda i, info: (i, 0)), struct((1024, 2048), BF))],
        )[0]
        return self.sent

    def add(self, info, received):
        clip = lambda first: lambda i, info: (jnp.clip(i - first, 0, 1), 0)
        fixed = lambda width: (block((256, width), lambda i, info: (0, 0)), struct((256, width), BF))
        tall = lambda first: (block((256, 1024), clip(first)), struct((512, 1024), BF))
        made = call_placed(
            weight_add_body,
            (4,),
            info,
            self.operands(0) + [(block((256, 2048), lambda i, info: (i, 0)), received)],
            [tall(0), tall(1), fixed(1024), fixed(1024), fixed(2048)],
        )
        self.over_x, self.over_y, self.next_y, self.next_x, self.own = made
        return self.own

    def first(self, done):
        self.from_x = along_x(after(self.over_x, done))
        self.from_y = along_y(after(self.over_y, done))
        return self.from_x, self.from_y

    def second(self, done):
        self.last_y = along_y(plus(after(self.next_y, done), self.from_x[256:]))
        self.last_x = along_x(plus(after(self.next_x, done), self.from_y[:256]))
        return self.last_y, self.last_x

    def total(self, info, turned=False):
        tall = lambda array, row: (block((256, 1024), lambda i: (row, 0)), array)
        shape = (2048, 256) if turned else (256, 2048)
        return call(
            total_turned_body if turned else total_body,
            (1,),
            [
                (smem(), info),
                (whole(self.own), self.own),
                tall(self.from_x, 0),
                tall(self.last_y, 0),
                tall(self.from_y, 1),
                tall(self.last_x, 0),
            ],
            [(block(shape, lambda i: (0, 0)), struct(shape, F32))],
        )[0]


def total_of(own, from_x, last_y, from_y, last_x):
    left = from_x[...].astype(F32) + last_y[...].astype(F32)
    right = from_y[...].astype(F32) + last_x[...].astype(F32)
    return own[...].astype(F32) + jnp.concatenate([left, right], 1)


def total_body(info, *refs):
    refs[-1][...] = total_of(*refs[:-1])


def total_turned_body(info, *refs):
    refs[-1][...] = total_of(*refs[:-1]).T


def project_body(info, q, own, core, far, cos, front, back, low, kv_sum):
    c, f, b = (jnp.concatenate([t[...]] * 2, 0) for t in (cos, front, back))
    for head in range(2):
        mine = slice(head * 256, head * 256 + 256)
        low[:, head * 768 : head * 768 + 256] = q[:, mine]
        for kind in range(2):
            cut = slice(kind * 512 + head * 256, kind * 512 + head * 256 + 256)
            grad = own[:, cut].astype(F32) + core[:, cut].astype(F32) + far[:, cut].astype(F32)
            if kind == 0:
                grad = turn(grad, c, -f, -b)
            kv_sum[:, head * 512 + kind * 256 : head * 512 + kind * 256 + 256] = jnp.sum(grad, 0, keepdims=True)
            start = head * 768 + 256 + kind * 256
            low[:, start : start + 256] = grad.astype(BF)


def input_body(info, low, hid, tok, gain_a, gain_m, *refs):
    w_qkv, w_up, parts, sums, (gx, xh, inv) = refs[:8], refs[8:16], refs[16:18], refs[18], refs[19:]
    step = pl.program_id(0)

    def products(first):
        for i, r in enumerate(ORDER):
            there = pl.ds(pl.multiple_of((info[0] ^ r) * 256, 256), 256)
            from_attn = nt(low[...], w_qkv[i][:, :768])
            from_mlp = nt(hid[...], w_up[i][...])
            xhat = xh[:, there]
            columns_sums = [from_attn * xhat, from_attn, from_mlp * xhat, from_mlp]
            grad = from_attn * gain_a[:, there] + from_mlp * gain_m[:, there]
            for row, values in enumerate(columns_sums):
                added = jnp.sum(values, 0, keepdims=True)
                sums[row : row + 1, there] = added if first else sums[row : row + 1, there] + added
            gx[:, there] = grad if first else gx[:, there] + grad

    @pl.when(step == 0)
    def _():
        t = tok[...].astype(F32)
        centered = t - jnp.mean(t, -1, keepdims=True)
        inverse = lax.rsqrt(jnp.mean(centered * centered, -1, keepdims=True) + EPS)
        xh[...] = centered * inverse
        inv[...] = jnp.broadcast_to(inverse, inv.shape)
        products(True)

    @pl.when(step == 1)
    def _():
        products(False)
        grad = gx[...]
        xhat = xh[...]
        mean = jnp.mean(grad, -1, keepdims=True)
        along = jnp.mean(grad * xhat, -1, keepdims=True)
        out = (inv[:, :1] * (grad - mean - xhat * along)).astype(BF)
        parts[0][...] = out[:256]
        parts[1][...] = out[256:]


def plus(a, b):
    return (a.astype(F32) + b.astype(F32)).astype(BF)


def bar(*arrays):
    return lax.optimization_barrier(arrays)


def finish_body(info, own, from_x, last_y, from_y, last_x, qkv, out):
    total = total_of(own, from_x, last_y, from_y, last_x)
    for head in range(2):
        qkv[:, head, :] = total[:, head * 768 : head * 768 + 768]
    out[...] = total[:, 1536:].T


class Hops:
    def __init__(self, info, tok, grad, bias):
        self.info = info
        self.given = (tok, grad, bias)
        self.mine = {}
        self.ready = {}
        self.pair = None
        self.out = [None, None]

    def start(self, block):
        self.leaving = self.mine[0] = block
        return [exchange(block, "tensor", 1)]

    def land(self, j, arrived, next_block=None):
        half = lambda array: (block((128, D), lambda i: (i, 0)), array)
        fresh = (block((128, D), lambda i: (i, 0)), struct((256, D), BF))
        parts, ins, outs = [], [(smem(), self.info)], []
        if j >= 2:
            self.ready[j - 2] = (self.leaving, arrived[0])
        if j < 8:
            parts.append("pair")
            ins += [half(self.mine[j]), half(arrived[0])]
            outs.append(fresh)
        if 1 <= j <= 8:
            parts.append("sum" if next_block is None else "either")
            ins += [half(self.pair), half(arrived[1])]
            if next_block is not None:
                ins.append(half(next_block))
            outs.append(fresh)
        made = list(call(lambda *refs: land_body(parts, *refs), (2,), ins, outs))
        done = made[0]
        if next_block is not None:
            self.mine[j + 1] = next_block
        pair = made.pop(0) if j < 8 else None
        self.leaving = made.pop(0) if j else after(next_block, pair)
        flying = [exchange(self.leaving, "tensor", 1)]
        if pair is not None:
            self.pair = pair
            flying.append(lax.ppermute(pair, "tensor", [(1, 2), (2, 1)]))
        return flying, done

    def write(self, k, before):
        tok, grad, bias = self.given
        which, place = divmod(k, 4)
        half = lambda array: (block((128, D), lambda i: (i, 0)), array)
        kept = (block((128, D), lambda i: (2 * place + i, 0)), (tok, grad)[which])
        ins = [(smem(), after(self.info, before))] + [half(array) for array in self.ready[k]] + [kept]
        if not which:
            ins.append((whole(bias), bias))
        aliases = {}
        if self.out[which] is not None:
            aliases[len(ins)] = 0
            ins.append((any_place(), self.out[which]))
        made = call(
            (mixed_body, tokens_grad_body)[which],
            (2,),
            ins,
            [(kept[0], struct((1024, D), (BF, F32)[which]))],
            aliases=aliases,
        )[0]
        self.out[which] = made
        return made


def land_body(parts, info, *refs):
    refs = list(refs)
    outs = refs[-len(parts) :]
    for part, out in zip(parts, outs):
        a, b = refs.pop(0), refs.pop(0)
        summed = (a[...].astype(F32) + b[...].astype(F32)).astype(BF)
        out[...] = jnp.where(info[9] > 0, summed, refs.pop(0)[...]) if part == "either" else summed


def tokens_grad_body(info, total, came, grad, *refs):
    refs[-1][...] = jnp.where(info[9] > 0, total[...], came[...]).astype(F32) + grad[...].astype(F32)


def mixed_body(info, total, came, tok, bias, *refs):
    summed = jnp.where(info[9] > 0, total[...], came[...]).astype(F32) + tok[...].astype(F32)
    refs[-1][...] = (summed + bias[...]).astype(BF)


def per_device_links(
    tokens,
    cotangent,
    lengths,
    block_slot,
    gain_attn,
    shift_attn,
    gain_mlp,
    shift_mlp,
    w_qkv,
    b_qkv,
    w_out,
    b_out,
    w_up,
    b_up,
    w_down,
    b_down,
):
    rows = 1024
    seq_id = lax.axis_index("seq")
    slots = [jnp.sum(jnp.where(jnp.arange(4) == (seq_id ^ r), block_slot, 0)) for r in range(4)]
    tensor_id = lax.axis_index("tensor")
    inner = ((tensor_id == 1) | (tensor_id == 2)).astype(jnp.int32)
    me = seq_id * 2 + lax.axis_index("batch")
    info = jnp.concatenate([jnp.stack([me, *slots]), lengths, inner.reshape(1)]).astype(jnp.int32)
    tok = tokens.reshape(rows, D)
    cot = cotangent.reshape(rows, D)
    cosine, sine = rotation(slots[0] * 256 + jnp.arange(256, dtype=jnp.int32))
    cosine, sine = cosine[:, 0], sine[:, 0]
    zero = jnp.zeros_like(sine)
    cos_t = jnp.concatenate([cosine, cosine, zero + 1.0, zero + 1.0], 1)
    front_t = jnp.concatenate([-sine, zero, zero, zero], 1)
    back_t = jnp.concatenate([zero, sine, zero, zero], 1)
    tables = [cos_t, front_t, back_t]
    gains = [v.reshape(1, D) for v in (gain_attn, shift_attn, gain_mlp, shift_mlp)]

    def info_in(*tokens_before):
        return (smem(), after(info, *tokens_before) if tokens_before else info)

    row_block = lambda n: block((256, n), lambda i: (i, 0))
    row_struct = lambda n, kind=BF: struct((rows, n), kind)
    tall = lambda n, index: block((256, n), index)

    head_own = jnp.concatenate(
        [w for h in range(2) for w in (w_qkv[:, h], w_out[h * 256 : (h + 1) * 256].T)], 1
    )
    head_x, head_y = along_x(head_own), along_y(head_own)
    head_c = to_core(head_own)
    in_a, in_m, grad_low, grad_sum = call(
        norm_body,
        (4,),
        [info_in(), (row_block(D), tok), (row_block(D), cot)] + [(whole(v), v) for v in gains],
        [(row_block(D), row_struct(D))] * 3 + [(block((1, D), lambda i: (0, 0)), struct((1, D), F32))],
        moved=5 * rows * D * 2,
    )
    down_own = w_down.T
    bias = jnp.swapaxes(b_qkv.reshape(2, 3, 256), 0, 1)
    head_x, head_y, head_c, in_a, in_m, grad_low, down_own, bias, *tables = bar(
        head_x, head_y, head_c, in_a, in_m, grad_low, down_own, bias, *tables
    )
    tables = [(whole(t), t) for t in tables]

    far_y, far_x = along_y(head_x[:128]), along_x(head_y[128:])
    others = [head_c, to_core(head_x), to_core(head_y)]
    far_y, far_x, up_own, *others = bar(far_y, far_x, w_up, *others)

    up_x, up_y = along_x(up_own), along_y(up_own)
    far = jnp.concatenate([far_y, far_x], 0)
    heads = both_cores(head_own, head_x, head_y, far, *others, to_core(far))
    q, kv_a, kv_b = call(
        lambda info, x, bias, *refs: qkv_body(info, x, bias.at[0], *refs),
        (3,),
        [info_in(), (whole(in_a), in_a), (block((1, 2, 256), lambda j: (j, 0, 0)), bias)]
        + tables
        + block_ins(heads, 256, lambda j: j)
        + block_ins(heads, 256, lambda j: j + 4),
        [
            (block((rows, 512), lambda j: (0, 0)), row_struct(512)),
            (block((512, 512), lambda j: (0, jnp.maximum(j - 1, 0))), struct((512, 1024), BF)),
            (block((512, 512), lambda j: (0, jnp.maximum(j - 1, 0))), struct((512, 1024), BF)),
        ],
        flops=2 * rows * D * 1536,
        moved=2 * (rows * D + D * 1536 + rows * 1536),
    )
    kv_x = along_x(kv_a)
    grad_att = call(
        grad_att_body,
        (1,),
        [info_in(q), (whole(grad_low), grad_low)]
        + block_ins(heads, 256, lambda j: 3)
        + block_ins(heads, 256, lambda j: 7),
        [(block((rows, 512), lambda j: (0, 0)), row_struct(512))],
        flops=2 * rows * D * 512,
        moved=2 * (rows * D + D * 512 + rows * 512),
    )[0]
    up_c = to_core(after(up_own, q))
    up_x, up_y, up_c, grad_att = bar(up_x, up_y, up_c, grad_att)

    up_far = along_y(up_x)
    others = [up_c, to_core(up_x), to_core(up_y)]
    down_own = after(down_own, *others)
    down_x, down_y = along_x(down_own), along_y(down_own)
    up_far, kv_x, kv_a, *others = bar(up_far, kv_x, kv_a, *others)
    ups = both_cores(up_own, up_x, up_y, up_far, *others, to_core(up_far))

    def kv_refs(own, by_x):
        both = to_core(jnp.concatenate([own, by_x], 0))
        return [(own, 0), (both, 0), (by_x, 0), (both, 2)]

    kv = [kv_refs(kv_a, kv_x)]
    act, slope = call(
        up_body,
        (4,),
        [info_in(grad_att), (whole(in_m), in_m), (block((1, 512), lambda j: (0, j)), b_up.reshape(1, -1))]
        + block_ins(ups, 512, lambda j: j),
        [(block((rows, 512), lambda j: (0, j)), row_struct(2048))] * 2,
        flops=2 * rows * D * 2048,
        moved=2 * (rows * D + D * 2048 + 2 * rows * 2048),
    )
    down_c = to_core(after(down_own, ups[7]))
    down_x, down_y, down_c, act, slope = bar(down_x, down_y, down_c, act, slope)

    def attention(part, *before):
        base = part * 2
        spot = lambda offset: block((256, 256), lambda s, h: (s + base, h + offset))
        local = lambda offset, row=0: block((256, 256), lambda s, h: (s + row, h + offset))
        return call(
            lambda *refs: attention_body(base, *refs),
            (2, 2),
            [info_in(*before), (spot(0), q), (spot(0), grad_att)]
            + tables
            + [(local(0, row), b) for b, row in kv[part]]
            + [(local(2, row), b) for b, row in kv[part]],
            [
                (local(0), struct((512, 512), BF)),
                (local(0), struct((512, 512), BF)),
                (block((1, 1, 1, 256), lambda s, h: (s, h, 0, 0)), struct((2, 2, 1, 256), F32)),
            ]
            + [(block((2, 256, 1024), lambda s, h: (0, s, 0)), struct((2, 512, 1024), BF))] * 2,
            flops=4 * 6 * 2 * 256 * 1024 * 256,
            moved=4 * 2 * 256 * 256 * 24,
        )

    def branch(part, att, *before):
        return call(
            branch_body,
            (2,),
            [
                info_in(*before),
                (block((512, 256), lambda i: (0, i)), att),
                (block((512, 1024), lambda i: (part, i)), act),
            ]
            + streamed(heads, 256, lambda i: 3 + 4 * i)
            + streamed(downs, 1024, lambda i: i),
            [(block((256, D), lambda i: (0, 0)), struct((256, D), BF))] * 2,
            scratch=[pltpu.VMEM((512, D), F32)],
            flops=2 * 512 * D * 2560,
            moved=2 * (512 * 2560 + D * 2560 + 512 * D),
        )

    top, bottom = call(
        split_body,
        (1,),
        [
            (block((128, 2048), lambda i: (0, 0)), down_x),
            (block((128, 2048), lambda i: (1, 0)), down_y),
        ],
        [(block((128, 2048), lambda i: (0, 0)), struct((128, 2048), BF))] * 2,
    )
    far_y, far_x = along_y(top), along_x(bottom)
    others = [down_c, to_core(down_x), to_core(down_y)]
    att_a, dq_a, dq_sum_a, keep_a, send_a = attention(0, top)
    far_y, far_x, att_a, kv_b, send_a, *others = bar(far_y, far_x, att_a, kv_b, send_a, *others)

    far = jnp.concatenate([far_y, far_x], 0)
    downs = both_cores(down_own, down_x, down_y, far, *others, to_core(far))
    kv_x = along_x(kv_b)
    received_a = to_core(send_a)
    branch_a = branch(0, att_a)
    received_a, *branch_a = bar(received_a, *branch_a)

    hops = Hops(info, tok, grad_low, (b_out + b_down).reshape(1, D))

    def hidden_call(before):
        return call(
            hidden_body,
            (4,),
            [info_in(before), (whole(grad_low), grad_low), (block((rows, 512), lambda j: (0, j)), slope)]
            + block_ins(downs, 512, lambda j: j),
            [
                (block((rows, 512), lambda j: (0, j)), row_struct(2048)),
                (block((1, 512), lambda j: (0, j)), struct((1, 2048), F32)),
            ],
            flops=2 * rows * D * 2048,
            moved=2 * (rows * D + D * 2048 + 2 * rows * 2048),
        )

    def project(dq, keep, came, far, before):
        return call(
            project_body,
            (1,),
            [info_in(before), (whole(dq), dq)]
            + [(pl.BlockSpec((None, 512, 1024), lambda i: (0, 0, 0)), t) for t in (keep, came)]
            + [(whole(far), far)]
            + tables,
            [
                (block((512, 1536), lambda i: (0, 0)), struct((512, 1536), BF)),
                (block((1, 1024), lambda i: (0, 0)), struct((1, 1024), F32)),
            ],
            moved=2 * 512 * 5000,
        )

    def input_part(half, low, before):
        return call(
            input_body,
            (2,),
            [
                info_in(before),
                (block((512, 768), lambda i: (0, i)), low),
                (block((512, 1024), lambda i: (half, i)), hidden_low),
                (pl.BlockSpec((512, D), lambda i: (half, 0), pipeline_mode=pl.Buffered(1)), tok),
            ]
            + [(whole(t), t) for t in (gains[0], gains[2])]
            + streamed(heads, 1024, lambda i: i)
            + streamed(ups, 1024, lambda i: i),
            [(block((256, D), lambda i: (0, 0)), struct((256, D), BF))] * 2
            + [(block((8, D), lambda i: (0, 0)), struct((8, D), F32))],
            scratch=[pltpu.VMEM((512, D), F32), pltpu.VMEM((512, D), F32), pltpu.VMEM((512, 128), F32)],
            flops=2 * 512 * D * 3584,
            moved=2 * (512 * 6000 + D * 3584),
        )

    flown = hops.start(branch_a[0])
    far_a = along_x(plus(keep_a[1], received_a[1]))
    hidden_low, b_up_sum = hidden_call(branch_a[0])
    down = Scatter([(grad_low, act)])
    down_sent = down.send(after(info, hidden_low))
    flown, kv_x, down_sent = bar(flown, kv_x, down_sent)

    flown, done = hops.land(0, flown, branch_a[1])
    kv.append(kv_refs(kv_b, after(kv_x, done)))
    down_received = to_core(after(down_sent, done))
    att_b, dq_b, dq_sum_b, keep_b, send_b = attention(1, done)
    branch_b = branch(1, att_b, att_b)
    flown, far_a, down_received, send_b, *branch_b = bar(flown, far_a, down_received, send_b, *branch_b)

    flown, done = hops.land(1, flown, branch_b[0])
    received_b = to_core(after(send_b, done))
    low_a, kv_sum_a = project(dq_a, keep_a, received_a, far_a, done)
    first, second, norm_sum_a = input_part(0, low_a, low_a)
    flown, received_b, first, second = bar(flown, received_b, first, second)

    flown, done = hops.land(2, flown, branch_b[1])
    far_b = along_x(plus(after(keep_b[1], done), received_b[1]))
    token = down.add(after(info, done), down_received)
    up = Scatter([(in_m, hidden_low)])
    up_sent = up.send(after(info, token))
    flown, far_b, up_sent = bar(flown, far_b, up_sent)

    flown, done = hops.land(3, flown, first)
    down_first = down.first(done)
    up_received = to_core(after(up_sent, done))
    low_b, kv_sum_b = project(dq_b, keep_b, received_b, far_b, done)
    third, fourth, norm_sum_b = input_part(1, low_b, low_b)
    q_sums = (dq_sum_a + dq_sum_b).sum(0).reshape(2, 1, 256)
    kv_total = (kv_sum_a + kv_sum_b).reshape(2, 2, 256)
    bias_qkv = jnp.concatenate([q_sums, kv_total], 1).reshape(-1)
    norm_sums = (norm_sum_a + norm_sum_b)[:4].reshape(-1)
    small = jnp.concatenate([norm_sums, bias_qkv, grad_sum[0], b_up_sum[0]]).reshape(-1, 128)
    flown, (down.from_x, down.from_y), up_received, third, fourth, small = bar(
        flown, down_first, up_received, third, fourth, small
    )

    flown, done = hops.land(4, flown, second)
    small_c = to_core(after(small, done))
    down_second = down.second(done)
    token = up.add(after(info, done), up_received)
    hops.write(0, token)
    project_low = jnp.concatenate([after(low_a, token), low_b], 0)
    attended = jnp.concatenate([after(att_a, token), att_b], 0)
    flown, (down.last_y, down.last_x), small_c, project_low, attended = bar(
        flown, down_second, small_c, project_low, attended
    )

    flown, done = hops.land(5, flown, third)
    up_first = up.first(done)
    attn = Scatter([(in_a, project_low), (grad_low, attended)])
    attn_sent = attn.send(after(info, done))
    small = after(small, attn_sent) + small_c
    norms = small[:64]
    norms_z = exchange(norms, "tensor", 1)
    written = hops.write(1, attn_sent)
    flown, (up.from_x, up.from_y), attn_sent, norms_z, hops.out[0] = bar(
        flown, up_first, attn_sent, norms_z, written
    )

    flown, done = hops.land(6, flown, fourth)
    attn_received = to_core(after(attn_sent, done))
    up_second = up.second(done)
    token = attn.add(after(info, done), attn_received)
    norms = after(norms, token) + norms_z
    norms_z = exchange(norms, "tensor", 2)
    flown, (up.last_y, up.last_x), norms_z, token = bar(flown, up_second, norms_z, token)

    flown, done = hops.land(7, flown)
    attn_first = attn.first(done)
    down_grad = down.total(after(info, done), True)
    written = hops.write(2, down_grad)
    written = hops.write(3, written)
    written = hops.write(4, written)
    up_grad = up.total(after(info, written))
    flown, (attn.from_x, attn.from_y), up_grad, down_grad, hops.out[1] = bar(
        flown, attn_first, up_grad, down_grad, hops.out[1]
    )

    flown, done = hops.land(8, flown)
    attn_second = attn.second(done)
    written = hops.write(5, done)
    written = hops.write(6, written)
    small = jnp.concatenate([after(norms, written) + norms_z, small[64:]], 0)
    small = small + along_y(small)
    small = small + along_x(small)
    attn.last_y, attn.last_x = attn_second
    tall = lambda array, row: (block((256, 1024), lambda i: (row, 0)), array)
    qkv_grad, out_grad = call(
        finish_body,
        (1,),
        [
            info_in(written),
            (whole(attn.own), attn.own),
            tall(attn.from_x, 0),
            tall(attn.last_y, 0),
            tall(attn.from_y, 1),
            tall(attn.last_x, 0),
        ],
        [
            (block((256, 2, 768), lambda i: (0, 0, 0)), struct((256, 2, 768), F32)),
            (block((512, 256), lambda i: (0, 0)), struct((512, 256), F32)),
        ],
    )
    hops.ready[7] = (hops.leaving, flown[0])
    (leaving, came), qkv_grad, out_grad, small, hops.out[1] = bar(
        hops.ready[7], qkv_grad, out_grad, small, hops.out[1]
    )
    hops.ready[7] = (leaving, came)
    hops.write(7, came)
    mixed, tokens_grad = hops.out

    norms = small[:64].reshape(4, D)
    small = small[64:].reshape(-1)
    bias_out = small[1536 : 1536 + D]

    return (
        mixed.reshape(tokens.shape),
        tokens_grad.reshape(tokens.shape),
        norms[0],
        norms[1],
        norms[2],
        norms[3],
        qkv_grad,
        small[:1536].reshape(b_qkv.shape),
        out_grad,
        bias_out,
        up_grad,
        small[1536 + D :],
        down_grad,
        bias_out,
    )


def solution(mesh):
    in_specs = (
        P("batch", "seq", None),
        P("batch", "seq", None),
        P("batch"),
        P(),
        P(),
        P(),
        P(),
        P(),
        P(("seq", "batch"), "tensor", None),
        P("tensor", None),
        P("tensor", ("seq", "batch")),
        P(),
        P(("seq", "batch"), "tensor"),
        P("tensor"),
        P("tensor", ("seq", "batch")),
        P(),
    )
    out_specs = (
        P("batch", "seq", None),
        P("batch", "seq", None),
        P(),
        P(),
        P(),
        P(),
        P(("seq", "batch"), "tensor", None),
        P("tensor", None),
        P("tensor", ("seq", "batch")),
        P(),
        P(("seq", "batch"), "tensor"),
        P("tensor"),
        P("tensor", ("seq", "batch")),
        P(),
    )
    links = tuple(mesh.shape[axis] for axis in ("seq", "batch", "tensor"))
    per_device = per_device_links if links == (4, 2, 4) else per_device_any
    return jax.shard_map(
        per_device, mesh=mesh, in_specs=in_specs, out_specs=out_specs, check_vma=False
    )
```

```python
import jax
import jax.numpy as jnp
from jax import lax
from jax.experimental import pallas as pl
from jax.experimental.pallas import tpu as pltpu
from jax.sharding import PartitionSpec as P

D = 2048
HEAD_DIM = 256
ROT = 64
EPS = 1e-05
FLOOR = -1e30
BF = jnp.bfloat16
F32 = jnp.float32


def dot(a, b, dims):
    return lax.dot_general(a, b, (dims, ((), ())), preferred_element_type=F32)


def rotation(places):
    half_rot = ROT // 2
    frequency = 10000.0 ** (jnp.arange(half_rot, dtype=F32) * (-2.0 / ROT))
    angles = places.astype(F32)[:, None] * frequency[None, :]
    return jnp.cos(angles)[:, None, :], jnp.sin(angles)[:, None, :]


def rotate(field, cosine, sine):
    half_rot = ROT // 2
    front = field[..., :half_rot]
    back = field[..., half_rot:ROT]
    return jnp.concatenate(
        [front * cosine - back * sine, back * cosine + front * sine, field[..., ROT:]], -1
    )


def gelu_pair(z):
    phi_cdf = 0.5 * (1.0 + lax.erf(z * 0.7071067811865476))
    density = 0.3989422804014327 * jnp.exp(-0.5 * z * z)
    return z * phi_cdf, phi_cdf + z * density


def per_device_any(
    tokens,
    cotangent,
    lengths,
    block_slot,
    gain_attn,
    shift_attn,
    gain_mlp,
    shift_mlp,
    w_qkv,
    b_qkv,
    w_out,
    b_out,
    w_up,
    b_up,
    w_down,
    b_down,
):
    seqs, block_rows, _ = tokens.shape
    rows = seqs * block_rows
    shard = w_qkv.shape[0]
    heads = w_qkv.shape[1]
    width_qkv = heads * 3 * HEAD_DIM
    width_att = heads * HEAD_DIM
    units = w_up.shape[1]
    fsdp = ("seq", "batch")
    scale = HEAD_DIM ** (-0.5)
    seq_count = lax.axis_size("seq")
    device_ids = jnp.arange(seq_count, dtype=jnp.int32)
    own_slot = jnp.sum(jnp.where(device_ids == lax.axis_index("seq"), block_slot, 0))
    offsets = jnp.arange(block_rows, dtype=jnp.int32)
    query_places = own_slot * block_rows + offsets
    key_places = (block_slot[:, None] * block_rows + offsets[None, :]).reshape(-1)

    attn_shard = jnp.concatenate([w_qkv.reshape(shard, width_qkv), w_out.T], 1)
    mlp_shard = jnp.concatenate([w_up, w_down.T], 1)
    attn_full = lax.all_gather(attn_shard, fsdp, axis=0, tiled=True)
    mlp_full = lax.all_gather(mlp_shard, fsdp, axis=0, tiled=True)
    full_qkv = attn_full[:, :width_qkv]
    full_out_t = attn_full[:, width_qkv:]
    full_up = mlp_full[:, :units]
    full_down_t = mlp_full[:, units:]

    token_rows = tokens.astype(F32).reshape(rows, D)
    centered = token_rows - jnp.mean(token_rows, -1, keepdims=True)
    inverse = lax.rsqrt(jnp.mean(jnp.square(centered), -1, keepdims=True) + EPS)
    xhat = centered * inverse
    input_attn = (xhat * gain_attn + shift_attn).astype(BF)
    input_mlp = (xhat * gain_mlp + shift_mlp).astype(BF)

    valid = (query_places[None, :] < lengths[:, None]).astype(F32)
    grad_rows = (cotangent.astype(F32) * valid[..., None]).reshape(rows, D)
    grad_low = grad_rows.astype(BF)

    project = dot(input_attn, full_qkv, ((1,), (0,))).reshape(
        seqs, block_rows, heads, 3 * HEAD_DIM
    ) + b_qkv
    cosine, sine = rotation(query_places)
    queries = rotate(project[..., :HEAD_DIM], cosine, sine).astype(BF)
    keys = rotate(project[..., HEAD_DIM : 2 * HEAD_DIM], cosine, sine).astype(BF)
    values = project[..., 2 * HEAD_DIM :].astype(BF)
    pair = jnp.concatenate([keys, values], -1)
    gathered = lax.all_gather(pair, "seq", axis=0, tiled=False)
    gathered = jnp.transpose(gathered, (1, 3, 0, 2, 4)).reshape(
        seqs, heads, seq_count * block_rows, 2 * HEAD_DIM
    )
    all_keys = gathered[..., :HEAD_DIM]
    all_values = gathered[..., HEAD_DIM:]

    hidden_pre = dot(input_mlp, full_up, ((1,), (0,))) + b_up
    gelu, slope = gelu_pair(hidden_pre)
    activated = gelu.astype(BF)
    grad_hidden = dot(grad_low, full_down_t, ((1,), (0,))) * slope
    hidden_low = grad_hidden.astype(BF)
    bias_up_sum = jnp.sum(grad_hidden, 0)

    grad_att = dot(grad_low, full_out_t, ((1,), (0,))).reshape(
        seqs, block_rows, heads, HEAD_DIM
    ).astype(BF)

    causal = key_places[None, None, :] <= query_places[None, :, None]
    inside = key_places[None, None, :] < lengths[:, None, None]
    mask = (causal & inside)[:, None]
    scores = jnp.einsum("schd,shtd->shct", queries, all_keys, preferred_element_type=F32) * scale
    scores = jnp.where(mask, scores, FLOOR)
    top = jnp.max(scores, -1, keepdims=True)
    weights = jnp.where(mask, jnp.exp(scores - top), 0.0)
    probs = weights / jnp.sum(weights, -1, keepdims=True)
    prob_low = probs.astype(BF)
    attended = jnp.einsum("shct,shtd->schd", prob_low, all_values, preferred_element_type=F32)
    attended = attended.astype(BF).reshape(rows, width_att)

    partial = dot(attended, full_out_t, ((1,), (1,))) + dot(activated, full_down_t, ((1,), (1,)))
    branch = lax.psum(partial.astype(BF), "tensor").astype(F32)

    grad_mlp_weights = jnp.concatenate(
        [dot(input_mlp, hidden_low, ((0,), (0,))), dot(grad_low, activated, ((0,), (0,)))], 1
    ).astype(BF)
    mlp_reduced = lax.psum_scatter(
        grad_mlp_weights, fsdp, scatter_dimension=0, tiled=True
    ).astype(F32)

    grad_probs = jnp.einsum("schd,shtd->shct", grad_att, all_values, preferred_element_type=F32)
    delta = jnp.sum(probs * grad_probs, -1, keepdims=True)
    grad_scores = (probs * (grad_probs - delta)).astype(BF)
    grad_query = jnp.einsum("shct,shtd->schd", grad_scores, all_keys, preferred_element_type=F32) * scale
    key_term = jnp.einsum("shct,schd->tshd", grad_scores, queries, preferred_element_type=F32) * scale
    value_term = jnp.einsum("shct,schd->tshd", prob_low, grad_att, preferred_element_type=F32)
    terms = jnp.concatenate([key_term, value_term], -1).astype(BF)
    own_terms = lax.psum_scatter(terms, "seq", scatter_dimension=0, tiled=True).astype(F32)
    own_terms = jnp.swapaxes(own_terms, 0, 1)
    grad_key = own_terms[..., :HEAD_DIM]
    grad_value = own_terms[..., HEAD_DIM:]
    grad_project = jnp.concatenate(
        [rotate(grad_query, cosine, -sine), rotate(grad_key, cosine, -sine), grad_value], -1
    ).reshape(rows, width_qkv)
    bias_qkv_sum = jnp.sum(grad_project, 0)
    project_low = grad_project.astype(BF)

    grad_norm_attn = dot(project_low, full_qkv, ((1,), (1,)))
    grad_norm_mlp = dot(hidden_low, full_up, ((1,), (1,)))
    norm_sums = jnp.stack(
        [
            jnp.sum(grad_norm_attn * xhat, 0),
            jnp.sum(grad_norm_attn, 0),
            jnp.sum(grad_norm_mlp * xhat, 0),
            jnp.sum(grad_norm_mlp, 0),
        ]
    )
    grad_xhat = grad_norm_attn * gain_attn + grad_norm_mlp * gain_mlp
    input_part = inverse * (
        grad_xhat
        - jnp.mean(grad_xhat, -1, keepdims=True)
        - xhat * jnp.mean(grad_xhat * xhat, -1, keepdims=True)
    )
    input_part, branch = lax.optimization_barrier((input_part.astype(BF), branch))
    input_sum = lax.psum(input_part, "tensor").astype(F32)
    mixed = (token_rows + branch + b_out + b_down).astype(BF).reshape(tokens.shape)
    tokens_grad = (grad_rows + input_sum).reshape(tokens.shape)

    grad_attn_weights = jnp.concatenate(
        [dot(input_attn, project_low, ((0,), (0,))), dot(grad_low, attended, ((0,), (0,)))], 1
    ).astype(BF)
    attn_reduced = lax.psum_scatter(
        grad_attn_weights, fsdp, scatter_dimension=0, tiled=True
    ).astype(F32)

    norm_sums = lax.psum(norm_sums, "tensor").reshape(-1)
    small = lax.psum(
        jnp.concatenate([norm_sums, bias_qkv_sum, jnp.sum(grad_rows, 0), bias_up_sum]), fsdp
    )
    norm_sums = small[: 4 * D].reshape(4, D)
    small = small[4 * D :]
    bias_qkv_sum = small[:width_qkv].reshape(b_qkv.shape)
    bias_out_sum = small[width_qkv : width_qkv + D]
    bias_up_sum = small[width_qkv + D :]
    return (
        mixed,
        tokens_grad,
        norm_sums[0],
        norm_sums[1],
        norm_sums[2],
        norm_sums[3],
        attn_reduced[:, :width_qkv].reshape(w_qkv.shape),
        bias_qkv_sum,
        attn_reduced[:, width_qkv:].T,
        bias_out_sum,
        mlp_reduced[:, :units],
        bias_up_sum,
        mlp_reduced[:, units:].T,
        bias_out_sum,
    )


def exchange(array, axis, flip):
    size = lax.axis_size(axis)
    return lax.ppermute(array, axis, [(i, i ^ flip) for i in range(size)])


def after(array, *others):
    return lax.optimization_barrier((array, *others))[0]


def along_x(array):
    return exchange(array, "seq", 2)


def along_y(array):
    return exchange(array, "batch", 1)


def to_core(array):
    return exchange(array, "seq", 1)


ORDER = (0, 2, 4, 6, 1, 3, 5, 7)


def block_ins(blocks, width, column):
    return [(pl.BlockSpec((b.shape[0], width), lambda j: (0, column(j))), b) for b in flat(blocks)]


def flat(blocks):
    return [half for b in blocks for half in (b if isinstance(b, tuple) else (b,))]


def both_cores(own, by_x, by_y, far, *others):
    own_c, by_x_c, by_y_c, far_c = others
    return (own, by_y, own_c, by_y_c, by_x, far, by_x_c, far_c)


def call(body, grid, ins, outs, scratch=(), flops=0, moved=0, vmem=60, aliases={}):
    return pl.pallas_call(
        body,
        grid=grid,
        in_specs=[spec for spec, _ in ins],
        out_specs=[spec for spec, _ in outs],
        out_shape=[shape for _, shape in outs],
        scratch_shapes=list(scratch),
        input_output_aliases=aliases,
        compiler_params=pltpu.CompilerParams(vmem_limit_bytes=vmem * 1024 * 1024),
        cost_estimate=pl.CostEstimate(flops=0, bytes_accessed=0, transcendentals=0),
    )(*[array for _, array in ins])


def call_placed(body, grid, info, ins, outs, scratch=(), flops=0, moved=0, vmem=60):
    return pl.pallas_call(
        body,
        grid_spec=pltpu.PrefetchScalarGridSpec(
            num_scalar_prefetch=1,
            grid=grid,
            in_specs=[spec for spec, _ in ins],
            out_specs=[spec for spec, _ in outs],
            scratch_shapes=list(scratch),
        ),
        out_shape=[shape for _, shape in outs],
        compiler_params=pltpu.CompilerParams(vmem_limit_bytes=vmem * 1024 * 1024),
        cost_estimate=pl.CostEstimate(flops=0, bytes_accessed=0, transcendentals=0),
    )(info, *[array for _, array in ins])


def smem():
    return pl.BlockSpec(memory_space=pltpu.SMEM)


def any_place():
    return pl.BlockSpec(memory_space=pl.ANY)


def whole(array):
    dims = len(array.shape)
    return pl.BlockSpec(array.shape, lambda *_: (0,) * dims, pipeline_mode=pl.Buffered(1))


def block(shape, index):
    return pl.BlockSpec(shape, index)


def struct(shape, dtype):
    return jax.ShapeDtypeStruct(shape, dtype)


def columns(ref, info, place):
    start = pl.multiple_of((info[0] ^ place) * 256, 256)
    return ref[:, pl.ds(start, 256)]


def norm_body(info, tok, cot, gain_a, shift_a, gain_m, shift_m, in_a, in_m, grad, grad_sum):
    step = pl.program_id(0)
    t = tok[...].astype(F32)
    centered = t - jnp.mean(t, -1, keepdims=True)
    xhat = centered * lax.rsqrt(jnp.mean(centered * centered, -1, keepdims=True) + EPS)
    in_a[...] = (xhat * gain_a[...] + shift_a[...]).astype(BF)
    in_m[...] = (xhat * gain_m[...] + shift_m[...]).astype(BF)
    place = info[1] * 256 + lax.broadcasted_iota(jnp.int32, t.shape, 0)
    g = jnp.where(place < info[5 + step], cot[...].astype(F32), 0.0)
    grad[...] = g.astype(BF)

    @pl.when(step == 0)
    def _():
        grad_sum[...] = jnp.zeros_like(grad_sum)

    grad_sum[...] += jnp.sum(g, 0, keepdims=True)


def matched(x, blocks, info):
    left = jnp.concatenate([columns(x, info, r) for r in range(8)], 1)
    right = jnp.concatenate([b[...] for b in blocks], 0)
    return jnp.dot(left, right, preferred_element_type=F32)


def turn(z, cos, front, back):
    first = z[:, :128]
    first = (
        first * cos
        + pltpu.roll(first, 96, 1) * front
        + pltpu.roll(first, 32, 1) * back
    )
    return jnp.concatenate([first, z[:, 128:]], 1)


def qkv_body(info, x, bias, cos, front, back, *refs):
    blocks, (q, kv_a, kv_b) = (refs[:8], refs[8:16]), refs[16:]
    step = pl.program_id(0)
    heads = [matched(x, blocks[h], info) + bias[h : h + 1] for h in range(2)]

    def turned():
        c, f, b = (jnp.concatenate([t[...]] * 4, 0) for t in (cos, front, back))
        return jnp.concatenate([turn(z, c, f, b) for z in heads], 1).astype(BF)

    @pl.when(step == 0)
    def _():
        q[...] = turned()

    @pl.when(step == 1)
    def _():
        k = turned()
        kv_a[...] = k[:512]
        kv_b[...] = k[512:]

    @pl.when(step == 2)
    def _():
        v = jnp.concatenate(heads, 1).astype(BF)
        kv_a[...] = v[:512]
        kv_b[...] = v[512:]


def split_body(from_x, from_y, top, bottom):
    top[...] = from_x[...]
    bottom[...] = from_y[...]


def grad_att_body(info, g, *refs):
    refs[16][...] = jnp.concatenate(
        [matched(g, refs[:8], info), matched(g, refs[8:16], info)], 1
    ).astype(BF)


def up_body(info, x, bias, *refs):
    blocks, (act, slope) = refs[:8], refs[8:]
    z = matched(x, blocks, info) + bias[...]
    gelu, steep = gelu_pair(z)
    act[...] = gelu.astype(BF)
    slope[...] = steep.astype(BF)


def hidden_body(info, g, slope, *refs):
    low, total = refs[-2:]
    grad = matched(g, refs[:-2], info) * slope[...].astype(F32)
    low[...] = grad.astype(BF)
    total[...] = jnp.sum(grad, 0, keepdims=True)


def nt(a, b):
    return lax.dot_general(a, b, (((1,), (1,)), ((), ())), preferred_element_type=F32)


def tn(a, b):
    return lax.dot_general(a, b, (((0,), (0,)), ((), ())), preferred_element_type=F32)


def attention_body(first_seq, info, q_ref, ga_ref, cos, front, back, *refs):
    keys, values = refs[:4], refs[4:8]
    att, dq, dq_sum, keep, send = refs[8:]
    terms = (keep.at[0], send.at[0], keep.at[1], send.at[1])
    seq = pl.program_id(0)
    head = pl.program_id(1)
    scale = HEAD_DIM ** (-0.5)
    length = info[5 + first_seq + seq]
    q = q_ref[...] * jnp.asarray(scale, BF)
    ga = ga_ref[...]
    last_seen = jnp.minimum(
        info[1] * 256 + lax.broadcasted_iota(jnp.int32, (256, 256), 0), length - 1
    )
    column = lax.broadcasted_iota(jnp.int32, (256, 256), 1)
    scores = [
        jnp.where(info[1 + r] * 256 + column <= last_seen, nt(q, keys[r][...]), FLOOR) for r in range(4)
    ]
    top = jnp.max(jnp.maximum(jnp.maximum(scores[0], scores[1]), jnp.maximum(scores[2], scores[3])), -1, keepdims=True)
    weights = [jnp.exp(s - top) for s in scores]
    total = jnp.sum(weights[0] + weights[1] + weights[2] + weights[3], -1, keepdims=True)
    inverse = 1.0 / total
    probs = [w * inverse for w in weights]
    low = [p.astype(BF) for p in probs]
    out = jnp.zeros((256, 256), F32)
    for r in range(4):
        out += jnp.dot(low[r], values[r][...], preferred_element_type=F32)
    att[...] = out.astype(BF)
    grad_probs = [nt(ga, values[r][...]) for r in range(4)]
    products = [p * g for p, g in zip(probs, grad_probs)]
    delta = jnp.sum(products[0] + products[1] + products[2] + products[3], -1, keepdims=True)
    grad_q = jnp.zeros((256, 256), F32)
    key_columns = pl.ds(pl.multiple_of(head * 256, 256), 256)
    value_columns = pl.ds(pl.multiple_of(head * 256 + 512, 256), 256)
    for r in range(4):
        grad_scores = (probs[r] * (grad_probs[r] - delta)).astype(BF)
        grad_q += jnp.dot(grad_scores, keys[r][...], preferred_element_type=F32)
        terms[r][:, key_columns] = tn(grad_scores, q).astype(BF)
        terms[r][:, value_columns] = tn(low[r], ga).astype(BF)
    grad_q = turn(grad_q * scale, cos[...], -front[...], -back[...])
    dq[...] = grad_q.astype(BF)
    dq_sum[...] = jnp.sum(grad_q, 0, keepdims=True)[None, None]


def streamed(blocks, width, column):
    ordered = flat([blocks[r] for r in ORDER])
    return [(pl.BlockSpec((b.shape[0], width), lambda i: (0, column(i))), b) for b in ordered]


def branch_body(info, att, act, *refs):
    w_att, w_act, outs, total = refs[:8], refs[8:18], refs[18:20], refs[20]
    step = pl.program_id(0)

    def part(i):
        if i < 6:
            w = w_act[i][...]
        else:
            w = jnp.concatenate([w_act[2 * i - 6][...], w_act[2 * i - 5][...]], 0)
        return nt(att[...], w_att[i][...]) + nt(act[...], w)

    @pl.when(step == 0)
    def _():
        for i in range(8):
            total[:, i * 256 : (i + 1) * 256] = part(i)

    @pl.when(step == 1)
    def _():
        for i, r in enumerate(ORDER):
            there = pl.ds(pl.multiple_of((info[0] ^ r) * 256, 256), 256)
            done = (total[:, i * 256 : (i + 1) * 256] + part(i)).astype(BF)
            outs[0][:, there] = done[:256]
            outs[1][:, there] = done[256:]


def weight_part(refs):
    products = [tn(refs[i][...], refs[i + 1][...]) for i in range(0, len(refs), 2)]
    return products[0] if len(products) == 1 else jnp.concatenate(products, 1)


def weight_send_body(info, *refs):
    refs[-1][...] = weight_part(refs[:-1]).astype(BF)


def weight_add_body(info, *refs):
    received, over_x, over_y, next_y, next_x, own = refs[-6:]
    step = pl.program_id(0)
    part = (weight_part(refs[:-6]) + received[...].astype(F32)).astype(BF)
    left, right = part[:, :1024], part[:, 1024:]

    @pl.when(step == 0)
    def _():
        over_x[...] = left
        next_x[...] = right

    @pl.when(step == 1)
    def _():
        over_x[...] = left
        over_y[...] = right

    @pl.when(step == 2)
    def _():
        next_y[...] = left
        over_y[...] = right

    @pl.when(step == 3)
    def _():
        own[...] = part


class Scatter:
    def __init__(self, pairs):
        self.pairs = pairs

    def operands(self, flip):
        def index(i, info):
            place = jnp.where(i == 0, 4, jnp.where(i == 1, 5, jnp.where(i == 2, 1, 0)))
            return 0, info[0] ^ place ^ flip

        fixed = lambda array: pl.BlockSpec(array.shape, lambda i, info: (0, 0), pipeline_mode=pl.Buffered(1))
        return [
            operand
            for x, h in self.pairs
            for operand in ((block((1024, 256), index), x), (fixed(h), h))
        ]

    def send(self, info):
        self.sent = call_placed(
            weight_send_body,
            (4,),
            info,
            self.operands(2),
            [(block((256, 2048), lambda i, info: (i, 0)), struct((1024, 2048), BF))],
        )[0]
        return self.sent

    def add(self, info, received):
        clip = lambda first: lambda i, info: (jnp.clip(i - first, 0, 1), 0)
        fixed = lambda width: (block((256, width), lambda i, info: (0, 0)), struct((256, width), BF))
        tall = lambda first: (block((256, 1024), clip(first)), struct((512, 1024), BF))
        made = call_placed(
            weight_add_body,
            (4,),
            info,
            self.operands(0) + [(block((256, 2048), lambda i, info: (i, 0)), received)],
            [tall(0), tall(1), fixed(1024), fixed(1024), fixed(2048)],
        )
        self.over_x, self.over_y, self.next_y, self.next_x, self.own = made
        return self.own

    def first(self, done):
        self.from_x = along_x(after(self.over_x, done))
        self.from_y = along_y(after(self.over_y, done))
        return self.from_x, self.from_y

    def second(self, done):
        self.last_y = along_y(plus(after(self.next_y, done), self.from_x[256:]))
        self.last_x = along_x(plus(after(self.next_x, done), self.from_y[:256]))
        return self.last_y, self.last_x

    def total(self, info, turned=False):
        tall = lambda array, row: (block((256, 1024), lambda i: (row, 0)), array)
        shape = (2048, 256) if turned else (256, 2048)
        return call(
            total_turned_body if turned else total_body,
            (1,),
            [
                (smem(), info),
                (whole(self.own), self.own),
                tall(self.from_x, 0),
                tall(self.last_y, 0),
                tall(self.from_y, 1),
                tall(self.last_x, 0),
            ],
            [(block(shape, lambda i: (0, 0)), struct(shape, F32))],
        )[0]


def total_of(own, from_x, last_y, from_y, last_x):
    left = from_x[...].astype(F32) + last_y[...].astype(F32)
    right = from_y[...].astype(F32) + last_x[...].astype(F32)
    return own[...].astype(F32) + jnp.concatenate([left, right], 1)


def total_body(info, *refs):
    refs[-1][...] = total_of(*refs[:-1])


def total_turned_body(info, *refs):
    refs[-1][...] = total_of(*refs[:-1]).T


def project_body(info, q, own, core, far, cos, front, back, low, kv_sum):
    c, f, b = (jnp.concatenate([t[...]] * 2, 0) for t in (cos, front, back))
    for head in range(2):
        mine = slice(head * 256, head * 256 + 256)
        low[:, head * 768 : head * 768 + 256] = q[:, mine]
        for kind in range(2):
            cut = slice(kind * 512 + head * 256, kind * 512 + head * 256 + 256)
            grad = own[:, cut].astype(F32) + core[:, cut].astype(F32) + far[:, cut].astype(F32)
            if kind == 0:
                grad = turn(grad, c, -f, -b)
            kv_sum[:, head * 512 + kind * 256 : head * 512 + kind * 256 + 256] = jnp.sum(grad, 0, keepdims=True)
            start = head * 768 + 256 + kind * 256
            low[:, start : start + 256] = grad.astype(BF)


def input_body(info, low, hid, tok, gain_a, gain_m, *refs):
    w_qkv, w_up, parts, sums, (gx, xh, inv) = refs[:8], refs[8:16], refs[16:18], refs[18], refs[19:]
    step = pl.program_id(0)

    def products(first):
        for i, r in enumerate(ORDER):
            there = pl.ds(pl.multiple_of((info[0] ^ r) * 256, 256), 256)
            from_attn = nt(low[...], w_qkv[i][:, :768])
            from_mlp = nt(hid[...], w_up[i][...])
            xhat = xh[:, there]
            columns_sums = [from_attn * xhat, from_attn, from_mlp * xhat, from_mlp]
            grad = from_attn * gain_a[:, there] + from_mlp * gain_m[:, there]
            for row, values in enumerate(columns_sums):
                added = jnp.sum(values, 0, keepdims=True)
                sums[row : row + 1, there] = added if first else sums[row : row + 1, there] + added
            gx[:, there] = grad if first else gx[:, there] + grad

    @pl.when(step == 0)
    def _():
        t = tok[...].astype(F32)
        centered = t - jnp.mean(t, -1, keepdims=True)
        inverse = lax.rsqrt(jnp.mean(centered * centered, -1, keepdims=True) + EPS)
        xh[...] = centered * inverse
        inv[...] = jnp.broadcast_to(inverse, inv.shape)
        products(True)

    @pl.when(step == 1)
    def _():
        products(False)
        grad = gx[...]
        xhat = xh[...]
        mean = jnp.mean(grad, -1, keepdims=True)
        along = jnp.mean(grad * xhat, -1, keepdims=True)
        out = (inv[:, :1] * (grad - mean - xhat * along)).astype(BF)
        parts[0][...] = out[:256]
        parts[1][...] = out[256:]


def plus(a, b):
    return (a.astype(F32) + b.astype(F32)).astype(BF)


def bar(*arrays):
    return lax.optimization_barrier(arrays)


def finish_body(info, own, from_x, last_y, from_y, last_x, qkv, out):
    total = total_of(own, from_x, last_y, from_y, last_x)
    for head in range(2):
        qkv[:, head, :] = total[:, head * 768 : head * 768 + 768]
    out[...] = total[:, 1536:].T


class Hops:
    def __init__(self, info, tok, grad, bias):
        self.info = info
        self.given = (tok, grad, bias)
        self.mine = {}
        self.ready = {}
        self.pair = None
        self.out = [None, None]

    def start(self, block):
        self.leaving = self.mine[0] = block
        return [exchange(block, "tensor", 1)]

    def land(self, j, arrived, next_block=None):
        half = lambda array: (block((128, D), lambda i: (i, 0)), array)
        fresh = (block((128, D), lambda i: (i, 0)), struct((256, D), BF))
        parts, ins, outs = [], [(smem(), self.info)], []
        if j >= 2:
            self.ready[j - 2] = (self.leaving, arrived[0])
        if j < 8:
            parts.append("pair")
            ins += [half(self.mine[j]), half(arrived[0])]
            outs.append(fresh)
        if 1 <= j <= 8:
            parts.append("sum" if next_block is None else "either")
            ins += [half(self.pair), half(arrived[1])]
            if next_block is not None:
                ins.append(half(next_block))
            outs.append(fresh)
        made = list(call(lambda *refs: land_body(parts, *refs), (2,), ins, outs))
        done = made[0]
        if next_block is not None:
            self.mine[j + 1] = next_block
        pair = made.pop(0) if j < 8 else None
        self.leaving = made.pop(0) if j else after(next_block, pair)
        flying = [exchange(self.leaving, "tensor", 1)]
        if pair is not None:
            self.pair = pair
            flying.append(lax.ppermute(pair, "tensor", [(1, 2), (2, 1)]))
        return flying, done

    def write(self, k, before):
        tok, grad, bias = self.given
        which, place = divmod(k, 4)
        half = lambda array: (block((128, D), lambda i: (i, 0)), array)
        kept = (block((128, D), lambda i: (2 * place + i, 0)), (tok, grad)[which])
        ins = [(smem(), after(self.info, before))] + [half(array) for array in self.ready[k]] + [kept]
        if not which:
            ins.append((whole(bias), bias))
        aliases = {}
        if self.out[which] is not None:
            aliases[len(ins)] = 0
            ins.append((any_place(), self.out[which]))
        made = call(
            (mixed_body, tokens_grad_body)[which],
            (2,),
            ins,
            [(kept[0], struct((1024, D), (BF, F32)[which]))],
            aliases=aliases,
        )[0]
        self.out[which] = made
        return made


def land_body(parts, info, *refs):
    refs = list(refs)
    outs = refs[-len(parts) :]
    for part, out in zip(parts, outs):
        a, b = refs.pop(0), refs.pop(0)
        summed = (a[...].astype(F32) + b[...].astype(F32)).astype(BF)
        out[...] = jnp.where(info[9] > 0, summed, refs.pop(0)[...]) if part == "either" else summed


def tokens_grad_body(info, total, came, grad, *refs):
    refs[-1][...] = jnp.where(info[9] > 0, total[...], came[...]).astype(F32) + grad[...].astype(F32)


def mixed_body(info, total, came, tok, bias, *refs):
    summed = jnp.where(info[9] > 0, total[...], came[...]).astype(F32) + tok[...].astype(F32)
    refs[-1][...] = (summed + bias[...]).astype(BF)


def per_device_links(
    tokens,
    cotangent,
    lengths,
    block_slot,
    gain_attn,
    shift_attn,
    gain_mlp,
    shift_mlp,
    w_qkv,
    b_qkv,
    w_out,
    b_out,
    w_up,
    b_up,
    w_down,
    b_down,
):
    rows = 1024
    seq_id = lax.axis_index("seq")
    slots = [jnp.sum(jnp.where(jnp.arange(4) == (seq_id ^ r), block_slot, 0)) for r in range(4)]
    tensor_id = lax.axis_index("tensor")
    inner = ((tensor_id == 1) | (tensor_id == 2)).astype(jnp.int32)
    me = seq_id * 2 + lax.axis_index("batch")
    info = jnp.concatenate([jnp.stack([me, *slots]), lengths, inner.reshape(1)]).astype(jnp.int32)
    tok = tokens.reshape(rows, D)
    cot = cotangent.reshape(rows, D)
    cosine, sine = rotation(slots[0] * 256 + jnp.arange(256, dtype=jnp.int32))
    cosine, sine = cosine[:, 0], sine[:, 0]
    zero = jnp.zeros_like(sine)
    cos_t = jnp.concatenate([cosine, cosine, zero + 1.0, zero + 1.0], 1)
    front_t = jnp.concatenate([-sine, zero, zero, zero], 1)
    back_t = jnp.concatenate([zero, sine, zero, zero], 1)
    tables = [cos_t, front_t, back_t]
    gains = [v.reshape(1, D) for v in (gain_attn, shift_attn, gain_mlp, shift_mlp)]

    def info_in(*tokens_before):
        return (smem(), after(info, *tokens_before) if tokens_before else info)

    row_block = lambda n: block((256, n), lambda i: (i, 0))
    row_struct = lambda n, kind=BF: struct((rows, n), kind)
    tall = lambda n, index: block((256, n), index)

    head_own = jnp.concatenate(
        [w for h in range(2) for w in (w_qkv[:, h], w_out[h * 256 : (h + 1) * 256].T)], 1
    )
    head_x, head_y = along_x(head_own), along_y(head_own)
    head_c = to_core(head_own)
    in_a, in_m, grad_low, grad_sum = call(
        norm_body,
        (4,),
        [info_in(), (row_block(D), tok), (row_block(D), cot)] + [(whole(v), v) for v in gains],
        [(row_block(D), row_struct(D))] * 3 + [(block((1, D), lambda i: (0, 0)), struct((1, D), F32))],
        moved=5 * rows * D * 2,
    )
    down_own = w_down.T
    bias = jnp.swapaxes(b_qkv.reshape(2, 3, 256), 0, 1)
    head_x, head_y, head_c, in_a, in_m, grad_low, down_own, bias, *tables = bar(
        head_x, head_y, head_c, in_a, in_m, grad_low, down_own, bias, *tables
    )
    tables = [(whole(t), t) for t in tables]

    far_y, far_x = along_y(head_x[:128]), along_x(head_y[128:])
    others = [head_c, to_core(head_x), to_core(head_y)]
    far_y, far_x, up_own, *others = bar(far_y, far_x, w_up, *others)

    up_x, up_y = along_x(up_own), along_y(up_own)
    far = jnp.concatenate([far_y, far_x], 0)
    heads = both_cores(head_own, head_x, head_y, far, *others, to_core(far))
    q, kv_a, kv_b = call(
        lambda info, x, bias, *refs: qkv_body(info, x, bias.at[0], *refs),
        (3,),
        [info_in(), (whole(in_a), in_a), (block((1, 2, 256), lambda j: (j, 0, 0)), bias)]
        + tables
        + block_ins(heads, 256, lambda j: j)
        + block_ins(heads, 256, lambda j: j + 4),
        [
            (block((rows, 512), lambda j: (0, 0)), row_struct(512)),
            (block((512, 512), lambda j: (0, jnp.maximum(j - 1, 0))), struct((512, 1024), BF)),
            (block((512, 512), lambda j: (0, jnp.maximum(j - 1, 0))), struct((512, 1024), BF)),
        ],
        flops=2 * rows * D * 1536,
        moved=2 * (rows * D + D * 1536 + rows * 1536),
    )
    kv_x = along_x(kv_a)
    grad_att = call(
        grad_att_body,
        (1,),
        [info_in(q), (whole(grad_low), grad_low)]
        + block_ins(heads, 256, lambda j: 3)
        + block_ins(heads, 256, lambda j: 7),
        [(block((rows, 512), lambda j: (0, 0)), row_struct(512))],
        flops=2 * rows * D * 512,
        moved=2 * (rows * D + D * 512 + rows * 512),
    )[0]
    up_c = to_core(after(up_own, q))
    up_x, up_y, up_c, grad_att = bar(up_x, up_y, up_c, grad_att)

    up_far = along_y(up_x)
    others = [up_c, to_core(up_x), to_core(up_y)]
    down_own = after(down_own, *others)
    down_x, down_y = along_x(down_own), along_y(down_own)
    up_far, kv_x, kv_a, *others = bar(up_far, kv_x, kv_a, *others)
    ups = both_cores(up_own, up_x, up_y, up_far, *others, to_core(up_far))

    def kv_refs(own, by_x):
        both = to_core(jnp.concatenate([own, by_x], 0))
        return [(own, 0), (both, 0), (by_x, 0), (both, 2)]

    kv = [kv_refs(kv_a, kv_x)]
    act, slope = call(
        up_body,
        (4,),
        [info_in(grad_att), (whole(in_m), in_m), (block((1, 512), lambda j: (0, j)), b_up.reshape(1, -1))]
        + block_ins(ups, 512, lambda j: j),
        [(block((rows, 512), lambda j: (0, j)), row_struct(2048))] * 2,
        flops=2 * rows * D * 2048,
        moved=2 * (rows * D + D * 2048 + 2 * rows * 2048),
    )
    down_c = to_core(after(down_own, ups[7]))
    down_x, down_y, down_c, act, slope = bar(down_x, down_y, down_c, act, slope)

    def attention(part, *before):
        base = part * 2
        spot = lambda offset: block((256, 256), lambda s, h: (s + base, h + offset))
        local = lambda offset, row=0: block((256, 256), lambda s, h: (s + row, h + offset))
        return call(
            lambda *refs: attention_body(base, *refs),
            (2, 2),
            [info_in(*before), (spot(0), q), (spot(0), grad_att)]
            + tables
            + [(local(0, row), b) for b, row in kv[part]]
            + [(local(2, row), b) for b, row in kv[part]],
            [
                (local(0), struct((512, 512), BF)),
                (local(0), struct((512, 512), BF)),
                (block((1, 1, 1, 256), lambda s, h: (s, h, 0, 0)), struct((2, 2, 1, 256), F32)),
            ]
            + [(block((2, 256, 1024), lambda s, h: (0, s, 0)), struct((2, 512, 1024), BF))] * 2,
            flops=4 * 6 * 2 * 256 * 1024 * 256,
            moved=4 * 2 * 256 * 256 * 24,
        )

    def branch(part, att, *before):
        return call(
            branch_body,
            (2,),
            [
                info_in(*before),
                (block((512, 256), lambda i: (0, i)), att),
                (block((512, 1024), lambda i: (part, i)), act),
            ]
            + streamed(heads, 256, lambda i: 3 + 4 * i)
            + streamed(downs, 1024, lambda i: i),
            [(block((256, D), lambda i: (0, 0)), struct((256, D), BF))] * 2,
            scratch=[pltpu.VMEM((512, D), F32)],
            flops=2 * 512 * D * 2560,
            moved=2 * (512 * 2560 + D * 2560 + 512 * D),
        )

    top, bottom = call(
        split_body,
        (1,),
        [
            (block((128, 2048), lambda i: (0, 0)), down_x),
            (block((128, 2048), lambda i: (1, 0)), down_y),
        ],
        [(block((128, 2048), lambda i: (0, 0)), struct((128, 2048), BF))] * 2,
    )
    far_y, far_x = along_y(top), along_x(bottom)
    others = [down_c, to_core(down_x), to_core(down_y)]
    att_a, dq_a, dq_sum_a, keep_a, send_a = attention(0, top)
    far_y, far_x, att_a, kv_b, send_a, *others = bar(far_y, far_x, att_a, kv_b, send_a, *others)

    halves = (far_y, far_x)
    downs = both_cores(down_own, down_x, down_y, halves, *others, tuple(to_core(half) for half in halves))
    kv_x = along_x(kv_b)
    received_a = to_core(send_a)
    branch_a = branch(0, att_a)
    received_a, *branch_a = bar(received_a, *branch_a)

    hops = Hops(info, tok, grad_low, (b_out + b_down).reshape(1, D))

    def hidden_call(before):
        return call(
            hidden_body,
            (4,),
            [info_in(before), (whole(grad_low), grad_low), (block((rows, 512), lambda j: (0, j)), slope)]
            + block_ins(downs, 512, lambda j: j),
            [
                (block((rows, 512), lambda j: (0, j)), row_struct(2048)),
                (block((1, 512), lambda j: (0, j)), struct((1, 2048), F32)),
            ],
            flops=2 * rows * D * 2048,
            moved=2 * (rows * D + D * 2048 + 2 * rows * 2048),
        )

    def project(dq, keep, came, far, before):
        return call(
            project_body,
            (1,),
            [info_in(before), (whole(dq), dq)]
            + [(pl.BlockSpec((None, 512, 1024), lambda i: (0, 0, 0)), t) for t in (keep, came)]
            + [(whole(far), far)]
            + tables,
            [
                (block((512, 1536), lambda i: (0, 0)), struct((512, 1536), BF)),
                (block((1, 1024), lambda i: (0, 0)), struct((1, 1024), F32)),
            ],
            moved=2 * 512 * 5000,
        )

    def input_part(half, low, before):
        return call(
            input_body,
            (2,),
            [
                info_in(before),
                (block((512, 768), lambda i: (0, i)), low),
                (block((512, 1024), lambda i: (half, i)), hidden_low),
                (pl.BlockSpec((512, D), lambda i: (half, 0), pipeline_mode=pl.Buffered(1)), tok),
            ]
            + [(whole(t), t) for t in (gains[0], gains[2])]
            + streamed(heads, 1024, lambda i: i)
            + streamed(ups, 1024, lambda i: i),
            [(block((256, D), lambda i: (0, 0)), struct((256, D), BF))] * 2
            + [(block((8, D), lambda i: (0, 0)), struct((8, D), F32))],
            scratch=[pltpu.VMEM((512, D), F32), pltpu.VMEM((512, D), F32), pltpu.VMEM((512, 128), F32)],
            flops=2 * 512 * D * 3584,
            moved=2 * (512 * 6000 + D * 3584),
        )

    flown = hops.start(branch_a[0])
    far_a = along_x(plus(keep_a[1], received_a[1]))
    hidden_low, b_up_sum = hidden_call(branch_a[0])
    down = Scatter([(grad_low, act)])
    down_sent = down.send(after(info, hidden_low))
    flown, kv_x, down_sent = bar(flown, kv_x, down_sent)

    flown, done = hops.land(0, flown, branch_a[1])
    kv.append(kv_refs(kv_b, after(kv_x, done)))
    down_received = to_core(after(down_sent, done))
    att_b, dq_b, dq_sum_b, keep_b, send_b = attention(1, done)
    branch_b = branch(1, att_b, att_b)
    flown, far_a, down_received, send_b, *branch_b = bar(flown, far_a, down_received, send_b, *branch_b)

    flown, done = hops.land(1, flown, branch_b[0])
    received_b = to_core(after(send_b, done))
    low_a, kv_sum_a = project(dq_a, keep_a, received_a, far_a, done)
    first, second, norm_sum_a = input_part(0, low_a, low_a)
    flown, received_b, first, second = bar(flown, received_b, first, second)

    flown, done = hops.land(2, flown, branch_b[1])
    far_b = along_x(plus(after(keep_b[1], done), received_b[1]))
    token = down.add(after(info, done), down_received)
    up = Scatter([(in_m, hidden_low)])
    up_sent = up.send(after(info, token))
    flown, far_b, up_sent = bar(flown, far_b, up_sent)

    flown, done = hops.land(3, flown, first)
    down_first = down.first(done)
    up_received = to_core(after(up_sent, done))
    low_b, kv_sum_b = project(dq_b, keep_b, received_b, far_b, done)
    third, fourth, norm_sum_b = input_part(1, low_b, low_b)
    q_sums = (dq_sum_a + dq_sum_b).sum(0).reshape(2, 1, 256)
    kv_total = (kv_sum_a + kv_sum_b).reshape(2, 2, 256)
    bias_qkv = jnp.concatenate([q_sums, kv_total], 1).reshape(-1)
    norm_sums = (norm_sum_a + norm_sum_b)[:4].reshape(-1)
    small = jnp.concatenate([norm_sums, bias_qkv, grad_sum[0], b_up_sum[0]]).reshape(-1, 128)
    flown, (down.from_x, down.from_y), up_received, third, fourth, small = bar(
        flown, down_first, up_received, third, fourth, small
    )

    flown, done = hops.land(4, flown, second)
    small_c = to_core(after(small, done))
    down_second = down.second(done)
    token = up.add(after(info, done), up_received)
    hops.write(0, token)
    project_low = jnp.concatenate([after(low_a, token), low_b], 0)
    attended = jnp.concatenate([after(att_a, token), att_b], 0)
    flown, (down.last_y, down.last_x), small_c, project_low, attended = bar(
        flown, down_second, small_c, project_low, attended
    )

    flown, done = hops.land(5, flown, third)
    up_first = up.first(done)
    attn = Scatter([(in_a, project_low), (grad_low, attended)])
    attn_sent = attn.send(after(info, done))
    small = after(small, attn_sent) + small_c
    norms = small[:64]
    norms_z = exchange(norms, "tensor", 1)
    written = hops.write(1, attn_sent)
    flown, (up.from_x, up.from_y), attn_sent, norms_z, hops.out[0] = bar(
        flown, up_first, attn_sent, norms_z, written
    )

    flown, done = hops.land(6, flown, fourth)
    attn_received = to_core(after(attn_sent, done))
    up_second = up.second(done)
    token = attn.add(after(info, done), attn_received)
    norms = after(norms, token) + norms_z
    norms_z = exchange(norms, "tensor", 2)
    flown, (up.last_y, up.last_x), norms_z, token = bar(flown, up_second, norms_z, token)

    flown, done = hops.land(7, flown)
    attn_first = attn.first(done)
    down_grad = down.total(after(info, done), True)
    written = hops.write(2, down_grad)
    written = hops.write(3, written)
    written = hops.write(4, written)
    up_grad = up.total(after(info, written))
    flown, (attn.from_x, attn.from_y), up_grad, down_grad, hops.out[1] = bar(
        flown, attn_first, up_grad, down_grad, hops.out[1]
    )

    flown, done = hops.land(8, flown)
    attn_second = attn.second(done)
    written = hops.write(5, done)
    written = hops.write(6, written)
    small = jnp.concatenate([after(norms, written) + norms_z, small[64:]], 0)
    small = small + along_y(small)
    small = small + along_x(small)
    attn.last_y, attn.last_x = attn_second
    tall = lambda array, row: (block((256, 1024), lambda i: (row, 0)), array)
    qkv_grad, out_grad = call(
        finish_body,
        (1,),
        [
            info_in(written),
            (whole(attn.own), attn.own),
            tall(attn.from_x, 0),
            tall(attn.last_y, 0),
            tall(attn.from_y, 1),
            tall(attn.last_x, 0),
        ],
        [
            (block((256, 2, 768), lambda i: (0, 0, 0)), struct((256, 2, 768), F32)),
            (block((512, 256), lambda i: (0, 0)), struct((512, 256), F32)),
        ],
    )
    hops.ready[7] = (hops.leaving, flown[0])
    (leaving, came), qkv_grad, out_grad, small, hops.out[1] = bar(
        hops.ready[7], qkv_grad, out_grad, small, hops.out[1]
    )
    hops.ready[7] = (leaving, came)
    hops.write(7, came)
    mixed, tokens_grad = hops.out

    norms = small[:64].reshape(4, D)
    small = small[64:].reshape(-1)
    bias_out = small[1536 : 1536 + D]

    return (
        mixed.reshape(tokens.shape),
        tokens_grad.reshape(tokens.shape),
        norms[0],
        norms[1],
        norms[2],
        norms[3],
        qkv_grad,
        small[:1536].reshape(b_qkv.shape),
        out_grad,
        bias_out,
        up_grad,
        small[1536 + D :],
        down_grad,
        bias_out,
    )


def solution(mesh):
    in_specs = (
        P("batch", "seq", None),
        P("batch", "seq", None),
        P("batch"),
        P(),
        P(),
        P(),
        P(),
        P(),
        P(("seq", "batch"), "tensor", None),
        P("tensor", None),
        P("tensor", ("seq", "batch")),
        P(),
        P(("seq", "batch"), "tensor"),
        P("tensor"),
        P("tensor", ("seq", "batch")),
        P(),
    )
    out_specs = (
        P("batch", "seq", None),
        P("batch", "seq", None),
        P(),
        P(),
        P(),
        P(),
        P(("seq", "batch"), "tensor", None),
        P("tensor", None),
        P("tensor", ("seq", "batch")),
        P(),
        P(("seq", "batch"), "tensor"),
        P("tensor"),
        P("tensor", ("seq", "batch")),
        P(),
    )
    links = tuple(mesh.shape[axis] for axis in ("seq", "batch", "tensor"))
    per_device = per_device_links if links == (4, 2, 4) else per_device_any
    return jax.shard_map(
        per_device, mesh=mesh, in_specs=in_specs, out_specs=out_specs, check_vma=False
    )
```
